32 devices in a mesh: seq: 8 (over z, x), tensor: 4 (over y, core).
Axes of the slice: x: 2, y: 2, z: 4, core: 2. Of those that a mesh axis runs over, the one named last changes fastest.
Arguments:
- tokens: bfloat16 [8192, 1024], P('seq'), may hold values from -6 to 6
- item_ids: int32 [8192], replicated, may hold values from 0 to 8, as said below
- text_states: bfloat16 [9, 128, 1024], replicated, may hold values from -6 to 6
- text_lengths: int32 [9], replicated, may hold values from 8 to 128
- norm_gain: bfloat16 [3, 1024], replicated, may hold values from 0.25 to 1.75
- norm_shift: bfloat16 [3, 1024], replicated, may hold values from -3 to 3
- w_self: bfloat16 [3, 1024, 1024], P(None, None, 'tensor'), may hold values from -0.1875 to 0.1875
- b_self: bfloat16 [2, 1024], P(None, 'tensor'), may hold values from -3 to 3
- w_self_out: bfloat16 [1024, 1024], P('tensor'), may hold values from -1 to 1
- w_cross_q: bfloat16 [1024, 1024], P(None, 'tensor'), may hold values from -0.1875 to 0.1875
- w_cross_kv: bfloat16 [2, 1024, 1024], P(None, None, 'tensor'), may hold values from -0.1875 to 0.1875
- b_cross: bfloat16 [2, 1024], P(None, 'tensor'), may hold values from -3 to 3
- w_cross_out: bfloat16 [1024, 1024], P('tensor'), may hold values from -0.75 to 0.75
- w_up: bfloat16 [1024, 4096], P(None, 'tensor'), may hold values from -0.1875 to 0.1875
- b_up: bfloat16 [4096], P('tensor'), may hold values from -3 to 3
- w_down: bfloat16 [4096, 1024], P('tensor'), may hold values from -0.09375 to 0.09375
- out_bias: bfloat16 [3, 1024], replicated, may hold values from -3 to 3
- d_out: bfloat16 [8192, 1024], P('seq'), may hold values from -6 to 6
Outputs:
- out: bfloat16 [8192, 1024], P('seq')
- grad_tokens: float32 [8192, 1024], P('seq')
- grad_text_states: float32 [9, 128, 1024], replicated
- grad_norm_gain: float32 [3, 1024], P(None, 'tensor')
- grad_norm_shift: float32 [3, 1024], P(None, 'tensor')
- grad_w_self: float32 [3, 1024, 1024], P(None, None, 'tensor')
- grad_b_self: float32 [2, 1024], P(None, 'tensor')
- grad_w_self_out: float32 [1024, 1024], P('tensor')
- grad_w_cross_q: float32 [1024, 1024], P(None, 'tensor')
- grad_w_cross_kv: float32 [2, 1024, 1024], P(None, None, 'tensor')
- grad_b_cross: float32 [2, 1024], P(None, 'tensor')
- grad_w_cross_out: float32 [1024, 1024], P('tensor')
- grad_w_up: float32 [1024, 4096], P(None, 'tensor')
- grad_b_up: float32 [4096], P('tensor')
- grad_w_down: float32 [4096, 1024], P('tensor')
- grad_out_bias: float32 [3, 1024], P(None, 'tensor')
The draws below stay inside these ranges and needn't reach their ends.
Inputs may be any that keep to these rules, and one draw needn't show every extreme that they name: `item_ids`: item ids never fall along the tokens and each of 0 to 8 occurs; every item but the first and the last holds exactly 1024 tokens, and the first and the last together hold 1024.
All inputs are finite; a program needn't handle non-finite values.
Results may differ from the reference program's by a relative error of at most 0.035.
Values may be sent and summed in bfloat16 or wider, within the bound.
No kernel may reach another device: no remote copies, remote signals or barrier semaphores. Data moves between devices by JAX's collectives and lax.ppermute only.
A program may use at most 256 MiB of HBM per device.

```python
from functools import partial
import jax
import jax.numpy as jnp
from jax import lax

D = 1024
HEADS = 16
HEAD_SIZE = 64
FF = 4096
TEXT = 128
ITEM_LEN = 1024
TOKENS = 8192
ITEMS = 9


def draw_item_ids(key, part):
    key = jax.random.fold_in(key, 17)
    offset = jax.random.randint(key, (), 1, ITEM_LEN)
    positions = jnp.arange(TOKENS, dtype=jnp.int32)
    return ((positions + offset) // ITEM_LEN).astype(jnp.int32)


def draw_text_lengths(key, part):
    key = jax.random.fold_in(key, 29)
    key_len, key_full = jax.random.split(key)
    lengths = jax.random.randint(key_len, (ITEMS,), 8, TEXT + 1)
    full_item = jax.random.randint(key_full, (), 0, ITEMS)
    return jnp.where(jnp.arange(ITEMS) == full_item, TEXT, lengths).astype(jnp.int32)


def levels(key, extent, cuts, smallest, high):
    level, own = 1.0, jax.random.fold_in(key, 6)
    for position, blocks in cuts:
        steps = jnp.exp(jax.random.uniform(jax.random.fold_in(own, position), (blocks,), jnp.float32, smallest / len(cuts), high / len(cuts)))
        level = level * jnp.repeat(steps, extent[position] // blocks).reshape([-1 if axis == position else 1 for axis in range(len(extent))])
    return level


def gaussian(own_key, dims, deviation, most, cuts=(), held_as=jnp.bfloat16):
    result = jax.random.normal(own_key, dims, jnp.float32) * deviation
    if len(cuts) > 0:
        result = levels(own_key, dims, cuts, -0.22, 0.18) * result
    return jnp.clip(result, min=-most, max=most).astype(held_as)


def setup_inputs(seed: int = 0) -> dict:
    splits = jax.random.split(jax.random.key(seed), 19)
    tokens = gaussian(splits[0], (TOKENS, D), 1.0, 6.0, ((0, 8),))
    item_ids = draw_item_ids(jax.random.fold_in(splits[18], 71), 0)
    text_states = gaussian(splits[2], (ITEMS, TEXT, D), 1.0, 6.0)
    text_lengths = draw_text_lengths(jax.random.fold_in(splits[18], 71), 0)
    norm_gain = jnp.clip(1.0 + 0.15 * jax.random.normal(splits[4], (3, D), jnp.float32), 0.25, 1.75).astype(jnp.bfloat16)
    norm_shift = gaussian(splits[5], (3, D), 0.5, 3.0)
    w_self = gaussian(splits[6], (3, D, D), D ** -0.5, 0.1875, ((2, 4),))
    b_self = gaussian(splits[7], (2, D), 0.5, 3.0, ((1, 4),))
    w_self_out = gaussian(splits[8], (D, D), (D // 32) ** -0.5, 1.0, ((0, 4),))
    w_cross_q = gaussian(splits[9], (D, D), D ** -0.5, 0.1875, ((1, 4),))
    w_cross_kv = gaussian(splits[10], (2, D, D), D ** -0.5, 0.1875, ((2, 4),))
    b_cross = gaussian(splits[11], (2, D), 0.5, 3.0, ((1, 4),))
    w_cross_out = gaussian(splits[12], (D, D), (D // 16) ** -0.5, 0.75, ((0, 4),))
    w_up = gaussian(splits[13], (D, FF), D ** -0.5, 0.1875, ((1, 4),))
    b_up = gaussian(splits[14], (FF,), 0.5, 3.0, ((0, 4),))
    w_down = gaussian(splits[15], (FF, D), FF ** -0.5, 0.09375, ((0, 4),))
    out_bias = gaussian(splits[16], (3, D), 0.5, 3.0)
    d_out = gaussian(splits[17], (TOKENS, D), 1.0, 6.0, ((0, 8),))
    return {"tokens": tokens, "item_ids": item_ids, "text_states": text_states, "text_lengths": text_lengths, "norm_gain": norm_gain, "norm_shift": norm_shift, "w_self": w_self, "b_self": b_self, "w_self_out": w_self_out, "w_cross_q": w_cross_q, "w_cross_kv": w_cross_kv, "b_cross": b_cross, "w_cross_out": w_cross_out, "w_up": w_up, "b_up": b_up, "w_down": w_down, "out_bias": out_bias, "d_out": d_out}


@jax.custom_vjp
def low(v):
    return lax.optimization_barrier(v.astype(jnp.bfloat16)).astype(jnp.float32)

@jax.custom_vjp
def low_back(v):
    return v

def low_keep(v):
    return (low(v), None)

def low_pass(kept, grad):
    return (grad,)

def back_keep(v):
    return (v, None)

def back_low(kept, grad):
    return (low(grad),)
low.defvjp(low_keep, low_pass)
low_back.defvjp(back_keep, back_low)
epsilon = 1e-05
masked_fill = -1e+30

def matmul_exact(left, right):
    return jnp.dot(left, right, precision=lax.Precision.HIGHEST)

def layer_norm(rows_in, gain, shift):
    row_mean = lax.optimization_barrier(jnp.mean(rows_in, axis=-1, keepdims=True))
    centered = rows_in - row_mean
    variance = lax.optimization_barrier(jnp.mean(centered * centered, axis=-1, keepdims=True))
    return centered * lax.rsqrt(variance + epsilon) * gain + shift

def masked_softmax(scores, allowed):
    filled = jnp.where(allowed, scores, masked_fill)
    return jax.nn.softmax(filled, axis=-1)

def self_block(block_queries, key_window, value_window, query_ids, key_ids, first_row, key_first):
    score_scale = HEAD_SIZE ** (-0.5)
    scores = low_back(score_scale * jnp.einsum('qhd,khd->hqk', block_queries, key_window, precision=lax.Precision.HIGHEST))
    query_pos = first_row + jnp.arange(block_queries.shape[0], dtype=jnp.int32)
    key_pos = key_first + jnp.arange(key_window.shape[0], dtype=jnp.int32)
    allowed = (key_pos[None, :] <= query_pos[:, None]) & (key_ids[None, :] == query_ids[:, None])
    attn_probs = masked_softmax(scores, allowed[None])
    return jnp.einsum('hqk,khd->qhd', low(attn_probs), value_window, precision=lax.Precision.HIGHEST)

def cross_block(block_queries, text_keys, text_values, query_ids, slot_item, slot_live):
    score_scale = HEAD_SIZE ** (-0.5)
    scores = low_back(score_scale * jnp.einsum('qhd,shd->hqs', block_queries, text_keys, precision=lax.Precision.HIGHEST))
    allowed = (slot_item[None, :] == query_ids[:, None]) & slot_live[None, :]
    attn_probs = masked_softmax(scores, allowed[None])
    return jnp.einsum('hqs,shd->qhd', low(attn_probs), text_values, precision=lax.Precision.HIGHEST)

def layer_forward(tokens, text_states, norm_gain, norm_shift, w_self, b_self, w_self_out, w_cross_q, w_cross_kv, b_cross, w_cross_out, w_up, b_up, w_down, out_bias, item_ids, text_lengths):
    token_count = tokens.shape[0]
    head_split = (token_count, HEADS, HEAD_SIZE)
    inputs_one = low(layer_norm(tokens, norm_gain[0], norm_shift[0]))
    queries = low(low_back(matmul_exact(inputs_one, w_self[0]) + b_self[0])).reshape(head_split)
    key_rows = low(low_back(matmul_exact(inputs_one, w_self[1]))).reshape(head_split)
    value_rows = low(low_back(matmul_exact(inputs_one, w_self[2]) + b_self[1])).reshape(head_split)
    block_rows = min(512, token_count)
    block_total = token_count // block_rows
    self_parts = []
    for block_index in range(block_total):
        first_row = block_index * block_rows
        last_row = first_row + block_rows
        key_first = max(0, first_row - ITEM_LEN)
        block_fn = jax.checkpoint(partial(self_block, first_row=first_row, key_first=key_first))
        self_parts.append(block_fn(queries[first_row:last_row], key_rows[key_first:last_row], value_rows[key_first:last_row], item_ids[first_row:last_row], item_ids[key_first:last_row]))
    attended = low(low_back(jnp.concatenate(self_parts, axis=0).reshape(token_count, D)))
    after_self = tokens + low_back(matmul_exact(attended, w_self_out) + out_bias[0])
    inputs_two = low(layer_norm(after_self, norm_gain[1], norm_shift[1]))
    cross_queries = low(low_back(matmul_exact(inputs_two, w_cross_q) + b_cross[0])).reshape(head_split)
    slot_total = ITEMS * TEXT
    text_flat = text_states.reshape(slot_total, D)
    text_keys = low(low_back(matmul_exact(text_flat, w_cross_kv[0]))).reshape(slot_total, HEADS, HEAD_SIZE)
    text_values = low(low_back(matmul_exact(text_flat, w_cross_kv[1]) + b_cross[1])).reshape(slot_total, HEADS, HEAD_SIZE)
    slot_index = jnp.arange(slot_total, dtype=jnp.int32)
    slot_item = slot_index // TEXT
    slot_live = slot_index % TEXT < text_lengths[slot_item]
    cross_parts = []
    cross_fn = jax.checkpoint(cross_block)
    for block_index in range(block_total):
        first_row = block_index * block_rows
        last_row = first_row + block_rows
        cross_parts.append(cross_fn(cross_queries[first_row:last_row], text_keys, text_values, item_ids[first_row:last_row], slot_item, slot_live))
    cross_attended = low(low_back(jnp.concatenate(cross_parts, axis=0).reshape(token_count, D)))
    after_cross = after_self + low_back(matmul_exact(cross_attended, w_cross_out) + out_bias[1])
    inputs_three = low(layer_norm(after_cross, norm_gain[2], norm_shift[2]))
    hidden_pre = low_back(matmul_exact(inputs_three, w_up) + b_up)
    hidden_act = low(jax.nn.gelu(hidden_pre))
    return after_cross + low_back(matmul_exact(hidden_act, w_down) + out_bias[2])

def to_float(array_in):
    return array_in.astype(jnp.float32)

def reference(tokens, item_ids, text_states, text_lengths, norm_gain, norm_shift, w_self, b_self, w_self_out, w_cross_q, w_cross_kv, b_cross, w_cross_out, w_up, b_up, w_down, out_bias, d_out):

    def forward_floats(*float_args):
        return layer_forward(*float_args, item_ids, text_lengths)
    float_args = [to_float(tokens), to_float(text_states), to_float(norm_gain), to_float(norm_shift), to_float(w_self), to_float(b_self), to_float(w_self_out), to_float(w_cross_q), to_float(w_cross_kv), to_float(b_cross), to_float(w_cross_out), to_float(w_up), to_float(b_up), to_float(w_down), to_float(out_bias)]
    output, pullback = jax.vjp(forward_floats, *float_args)
    grads = pullback(to_float(d_out))
    return (output.astype(jnp.bfloat16), grads[0], grads[1], grads[2], grads[3], grads[4], grads[5], grads[6], grads[7], grads[8], grads[9], grads[10], grads[11], grads[12], grads[13], grads[14])
```

```python
import jax
import jax.numpy as jnp
from jax import lax
from jax.sharding import PartitionSpec as P

HEAD_SIZE = 64
ITEM_LEN = 1024


epsilon = 1e-05
masked_fill = -1e30


def shifted(value, axis, steps):
    count = lax.axis_size(axis)
    leading, last = (max(0, -steps), min(count, count - steps))
    return lax.ppermute(value, axis, [(source, source + steps) for source in range(leading, last)])


def matmul_low(left, right):
    return jnp.dot(left, right, preferred_element_type=jnp.float32)


def contract_rows(left, right):
    return jnp.einsum("ra,rb->ab", left, right, preferred_element_type=jnp.float32)


def times_transpose(left, right):
    return jnp.einsum("ra,ba->rb", left, right, preferred_element_type=jnp.float32)


def layer_norm(rows_in, gain, shift):
    row_mean = jnp.mean(rows_in, axis=-1, keepdims=True)
    centered = rows_in - row_mean
    variance = jnp.mean(centered * centered, axis=-1, keepdims=True)
    inv_scale = lax.rsqrt(variance + epsilon)
    normal = centered * inv_scale
    return (normal * gain + shift, normal, inv_scale)


def norm_back(grad_normed, normal, inv_scale, gain):
    grad_normal = grad_normed * gain
    grad_mean = jnp.mean(grad_normal, axis=-1, keepdims=True)
    proj_mean = jnp.mean(grad_normal * normal, axis=-1, keepdims=True)
    return inv_scale * (grad_normal - grad_mean - normal * proj_mean)


def split_heads(matrix, head_size):
    return matrix.reshape(matrix.shape[0], matrix.shape[1] // head_size, head_size)


def swapped(value, axis, distance):
    count = lax.axis_size(axis)
    return lax.ppermute(value, axis, [(source, source ^ distance) for source in range(count)])


def axis_bits(axis):
    return (lax.axis_size(axis) - 1).bit_length()


def gather_relative(block, axis):
    blocks = {0: block}
    for bit in reversed(range(axis_bits(axis))):
        blocks.update(
            {d ^ (1 << bit): swapped(held, axis, 1 << bit) for d, held in list(blocks.items())}
        )
    return [blocks[d] for d in range(len(blocks))]


def rank_bit(axis, bit):
    return (lax.axis_index(axis) >> bit) & 1


def shard_offset(axis, row_count):
    offset = 0
    for bit in range(axis_bits(axis)):
        offset = offset + rank_bit(axis, bit) * (row_count >> (bit + 1))
    return offset


def scatter_rows(partial_rows, axis):
    held = partial_rows
    for bit in range(axis_bits(axis)):
        half = held.shape[0] // 2
        mine = rank_bit(axis, bit)
        sent = lax.dynamic_slice_in_dim(held, (1 - mine) * half, half, 0)
        kept = lax.dynamic_slice_in_dim(held, mine * half, half, 0)
        arrived = swapped(sent, axis, 1 << bit)
        held = kept.astype(jnp.float32) + arrived.astype(jnp.float32)
        if bit + 1 < axis_bits(axis):
            held = held.astype(jnp.bfloat16)
    return held


def gather_rows(shard, axis):
    blocks = gather_relative(shard, axis)
    rows = shard.shape[0]
    total = rows * len(blocks)
    own = shard_offset(axis, total)
    full = jnp.zeros((total,) + shard.shape[1:], shard.dtype)
    for d, block in enumerate(blocks):
        start = own
        for bit in range(axis_bits(axis)):
            if (d >> bit) & 1:
                size = total >> (bit + 1)
                start = start + size * (1 - 2 * rank_bit(axis, bit))
        full = lax.dynamic_update_slice_in_dim(full, block, start, 0)
    return full


def scatter_columns(partial, axis):
    held = partial
    for bit in reversed(range(axis_bits(axis))):
        half = held.shape[1] // 2
        mine = rank_bit(axis, bit)
        sent = lax.dynamic_slice_in_dim(held, (1 - mine) * half, half, 1)
        kept = lax.dynamic_slice_in_dim(held, mine * half, half, 1)
        held = kept + swapped(sent, axis, 1 << bit)
    return held


def group_sum(values, axis, turn):
    count = lax.axis_size(axis)
    members = [(place + turn) % count for place in range(count)]
    return lax.psum(values, axis, axis_index_groups=[members])


def butterfly_sum(value, axis):
    for bit in range(axis_bits(axis)):
        value = value + swapped(value, axis, 1 << bit)
    return value


def per_device(
    tokens,
    item_ids,
    text_states,
    text_lengths,
    norm_gain,
    norm_shift,
    w_self,
    b_self,
    w_self_out,
    w_cross_q,
    w_cross_kv,
    b_cross,
    w_cross_out,
    w_up,
    b_up,
    w_down,
    out_bias,
    d_out,
):
    f32, bf16 = jnp.float32, jnp.bfloat16
    row_count = tokens.shape[0]
    assert row_count == ITEM_LEN
    local_width = w_self.shape[2]
    head_count = local_width // HEAD_SIZE
    score_scale = HEAD_SIZE ** (-0.5)
    seq_rank = lax.axis_index("seq")
    tensor_rank = lax.axis_index("tensor")
    shard_rows = row_count // lax.axis_size("tensor")
    shard_start = shard_offset("tensor", row_count)
    cut = jnp.sum((item_ids == 0).astype(jnp.int32))
    row_index = jnp.arange(row_count, dtype=jnp.int32)
    old_item = row_index < cut

    def own_rows(full_rows):
        return lax.dynamic_slice_in_dim(full_rows, shard_start, shard_rows, 0)

    def local_cols(full_rows):
        return lax.dynamic_slice_in_dim(full_rows, tensor_rank * local_width, local_width, axis=1)

    own_allowed = (row_index[None, :] <= row_index[:, None]) & (
        old_item[None, :] == old_item[:, None]
    )
    far_allowed = old_item[:, None] & ~old_item[None, :] & (seq_rank > 0)

    residual = tokens.astype(f32)
    gain_rows = norm_gain.astype(f32)
    shift_rows = norm_shift.astype(f32)
    bias_rows = out_bias.astype(f32)
    normed_one, normal_one, inv_one = layer_norm(residual, gain_rows[0], shift_rows[0])
    inputs_one = normed_one.astype(bf16)
    keys_local = matmul_low(inputs_one, w_self[1]).astype(bf16)
    values_local = (matmul_low(inputs_one, w_self[2]) + b_self[1].astype(f32)).astype(bf16)
    keys_far, values_far = shifted((keys_local, values_local), "seq", 1)
    queries = (matmul_low(inputs_one, w_self[0]) + b_self[0].astype(f32)).astype(bf16)
    all_self_out = jnp.concatenate(gather_relative(w_self_out, "tensor"), axis=0)
    all_cross_out = jnp.concatenate(gather_relative(w_cross_out, "tensor"), axis=0)
    all_cross_q = jnp.concatenate(gather_relative(w_cross_q, "tensor"), axis=1)
    query_heads = split_heads(queries, HEAD_SIZE)

    def scores_of(key_block, allowed):
        scores = score_scale * jnp.einsum(
            "qhd,khd->hqk",
            query_heads,
            split_heads(key_block, HEAD_SIZE),
            preferred_element_type=f32,
        )
        return jnp.where(allowed[None], scores, masked_fill)

    def attend_block(state_now, key_block, value_block, allowed):
        old_max, old_total, old_acc = state_now
        scores = scores_of(key_block, allowed)
        new_max = jnp.maximum(old_max, jnp.max(scores, axis=-1))
        weights = jnp.where(allowed[None], jnp.exp(scores - new_max[..., None]), 0.0)
        factor = jnp.exp(old_max - new_max)
        new_total = old_total * factor + jnp.sum(weights, axis=-1)
        update = jnp.einsum(
            "hqk,khd->hqd",
            weights.astype(bf16),
            split_heads(value_block, HEAD_SIZE),
            preferred_element_type=f32,
        )
        return (new_max, new_total, old_acc * factor[..., None] + update)

    start_max = jnp.full((head_count, row_count), masked_fill, f32)
    start_total = jnp.zeros((head_count, row_count), f32)
    start_acc = jnp.zeros((head_count, row_count, HEAD_SIZE), f32)
    attn_state = attend_block(
        (start_max, start_total, start_acc), keys_local, values_local, own_allowed
    )
    run_max, run_total, run_acc = attend_block(attn_state, keys_far, values_far, far_allowed)
    attn_heads = run_acc / run_total[..., None]
    log_total = run_max + jnp.log(run_total)
    attended = jnp.transpose(attn_heads, (1, 0, 2)).reshape(row_count, local_width).astype(bf16)
    all_attended = jnp.concatenate(gather_relative(attended, "tensor"), axis=1)
    after_self = residual + (matmul_low(all_attended, all_self_out) + bias_rows[0])

    normed_two, normal_two, inv_two = layer_norm(after_self, gain_rows[1], shift_rows[1])
    inputs_two = normed_two.astype(bf16)
    cross_queries = (matmul_low(inputs_two, w_cross_q) + b_cross[0].astype(f32)).astype(bf16)
    item_total, slot_count = text_states.shape[:2]
    slot_total = item_total * slot_count
    window_slots = 2 * slot_count
    text_flat = text_states.reshape(slot_total, text_states.shape[2])
    text_window = lax.dynamic_slice_in_dim(text_flat, seq_rank * slot_count, window_slots, 0)
    text_keys = matmul_low(text_window, w_cross_kv[0]).astype(bf16)
    text_values = (matmul_low(text_window, w_cross_kv[1]) + b_cross[1].astype(f32)).astype(bf16)
    window_index = jnp.arange(window_slots, dtype=jnp.int32)
    first_part = window_index < slot_count
    item_lengths = lax.dynamic_slice_in_dim(text_lengths, seq_rank, 2)
    slot_live = window_index % slot_count < jnp.where(first_part, item_lengths[0], item_lengths[1])
    cross_allowed = ((first_part[None, :] == old_item[:, None]) & slot_live[None, :])[None]
    cross_heads = split_heads(cross_queries, HEAD_SIZE)
    text_key_heads = split_heads(text_keys, HEAD_SIZE)
    text_value_heads = split_heads(text_values, HEAD_SIZE)
    cross_scores = score_scale * jnp.einsum(
        "qhd,shd->hqs", cross_heads, text_key_heads, preferred_element_type=f32
    )
    cross_filled = jnp.where(cross_allowed, cross_scores, masked_fill)
    cross_exp = jnp.exp(cross_filled - jnp.max(cross_filled, axis=-1, keepdims=True))
    cross_probs = cross_exp / jnp.sum(cross_exp, axis=-1, keepdims=True)
    cross_low = cross_probs.astype(bf16)
    cross_rows = jnp.einsum("hqs,shd->qhd", cross_low, text_value_heads, preferred_element_type=f32)
    cross_attended = cross_rows.reshape(row_count, local_width).astype(bf16)
    all_cross_attended = jnp.concatenate(gather_relative(cross_attended, "tensor"), axis=1)
    after_cross = after_self + (matmul_low(all_cross_attended, all_cross_out) + bias_rows[1])

    normed_three, normal_three, inv_three = layer_norm(after_cross, gain_rows[2], shift_rows[2])
    inputs_three = normed_three.astype(bf16)
    hidden_pre = matmul_low(inputs_three, w_up) + b_up.astype(f32)
    hidden_act, gelu_back = jax.vjp(jax.nn.gelu, hidden_pre)
    hidden_low = hidden_act.astype(bf16)
    grad_hidden = times_transpose(d_out, w_down)
    grad_pre = gelu_back(grad_hidden)[0].astype(bf16)
    grad_three_shard = scatter_rows(times_transpose(grad_pre, w_up).astype(bf16), "tensor")
    grad_w_down = contract_rows(hidden_low, d_out).astype(bf16)
    grad_w_up = contract_rows(inputs_three, grad_pre).astype(bf16)
    sum_w_down, sum_w_up = group_sum((grad_w_down, grad_w_up), "seq", 0)
    grad_b_up = jnp.sum(grad_pre.astype(f32), axis=0)
    output_shard = own_rows(after_cross) + (
        scatter_rows(matmul_low(hidden_low, w_down).astype(bf16), "tensor") + bias_rows[2]
    )
    output_rows = gather_rows(output_shard.astype(bf16), "tensor")

    normal_three_shard = own_rows(normal_three)
    grad_gain_three = jnp.sum(grad_three_shard * normal_three_shard, axis=0)
    grad_shift_three = jnp.sum(grad_three_shard, axis=0)
    grad_cross_shard = own_rows(d_out).astype(f32) + norm_back(
        grad_three_shard, normal_three_shard, own_rows(inv_three), gain_rows[2]
    )
    grad_cross_low = gather_rows(grad_cross_shard.astype(bf16), "tensor")
    grad_w_cross_out = contract_rows(cross_attended, grad_cross_low).astype(bf16)
    grad_cross_att = times_transpose(grad_cross_low, w_cross_out).astype(bf16)
    grad_cross_heads = split_heads(grad_cross_att, HEAD_SIZE)
    grad_cross_probs = jnp.einsum(
        "qhd,shd->hqs", grad_cross_heads, text_value_heads, preferred_element_type=f32
    )
    cross_inner = jnp.sum(cross_probs * grad_cross_probs, axis=-1, keepdims=True)
    grad_cross_scores = (cross_probs * (grad_cross_probs - cross_inner)).astype(bf16)
    grad_cross_q = (
        score_scale
        * jnp.einsum("hqs,shd->qhd", grad_cross_scores, text_key_heads, preferred_element_type=f32)
    )
    grad_cross_q = grad_cross_q.reshape(row_count, local_width).astype(bf16)
    all_grad_cross_q = jnp.concatenate(gather_relative(grad_cross_q, "tensor"), axis=1)
    key_window_part = score_scale * jnp.einsum(
        "hqs,qhd->shd", grad_cross_scores, cross_heads, preferred_element_type=f32
    )
    value_window_part = jnp.einsum(
        "hqs,qhd->shd", cross_low, grad_cross_heads, preferred_element_type=f32
    )
    grad_w_cross_q = contract_rows(inputs_two, grad_cross_q).astype(bf16)
    sum_w_cross_out, sum_w_cross_q = group_sum((grad_w_cross_out, grad_w_cross_q), "seq", 1)
    window_parts = jnp.stack((key_window_part, value_window_part)).astype(bf16)
    all_parts = lax.all_gather(window_parts.reshape(2, 2, slot_count, local_width), "seq")
    all_parts = all_parts.astype(f32)
    empty = jnp.zeros_like(all_parts[:1, :, 0])
    text_sums = jnp.concatenate((all_parts[:, :, 0], empty)) + jnp.concatenate(
        (empty, all_parts[:, :, 1])
    )
    text_sums = text_sums.astype(bf16)
    grad_text_keys = text_sums[:, 0].reshape(slot_total, local_width)
    grad_text_values = text_sums[:, 1].reshape(slot_total, local_width)
    grad_w_cross_kv = jnp.stack(
        (contract_rows(text_flat, grad_text_keys), contract_rows(text_flat, grad_text_values))
    )
    grad_text_part = times_transpose(grad_text_keys, w_cross_kv[0]) + times_transpose(
        grad_text_values, w_cross_kv[1]
    )
    grad_text_shard = scatter_rows(grad_text_part.astype(bf16), "tensor").astype(bf16)
    grad_text = gather_rows(grad_text_shard, "tensor").astype(f32).reshape(text_states.shape)
    grad_value_bias = jnp.sum(grad_text_values.astype(f32), axis=0)

    grad_normed_two = times_transpose(all_grad_cross_q, all_cross_q)
    grad_gain_two = jnp.sum(local_cols(grad_normed_two) * local_cols(normal_two), axis=0)
    grad_shift_two = jnp.sum(local_cols(grad_normed_two), axis=0)
    grad_after_self = grad_cross_low.astype(f32) + norm_back(
        grad_normed_two, normal_two, inv_two, gain_rows[1]
    )
    grad_self_low = grad_after_self.astype(bf16)
    grad_w_self_out = contract_rows(attended, grad_self_low).astype(bf16)
    grad_attn_rows = times_transpose(grad_self_low, w_self_out).astype(bf16)
    grad_attn_heads = split_heads(grad_attn_rows, HEAD_SIZE)
    row_inner = jnp.einsum("qhd,hqd->hq", grad_attn_heads.astype(f32), attn_heads)

    def back_block(key_block, value_block, allowed):
        attn_probs = jnp.exp(scores_of(key_block, allowed) - log_total[..., None])
        grad_probs = jnp.einsum(
            "qhd,khd->hqk",
            grad_attn_heads,
            split_heads(value_block, HEAD_SIZE),
            preferred_element_type=f32,
        )
        grad_scores = (attn_probs * (grad_probs - row_inner[..., None])).astype(bf16)
        grad_q_block = score_scale * jnp.einsum(
            "hqk,khd->qhd",
            grad_scores,
            split_heads(key_block, HEAD_SIZE),
            preferred_element_type=f32,
        )
        grad_key_block = score_scale * jnp.einsum(
            "hqk,qhd->khd", grad_scores, query_heads, preferred_element_type=f32
        )
        grad_value_block = jnp.einsum(
            "hqk,qhd->khd", attn_probs.astype(bf16), grad_attn_heads, preferred_element_type=f32
        )
        return tuple(
            part.reshape(row_count, local_width)
            for part in (grad_q_block, grad_key_block, grad_value_block)
        )

    grad_q_far, grad_keys_far, grad_values_far = back_block(keys_far, values_far, far_allowed)
    carry_keys, carry_values = shifted(
        (grad_keys_far.astype(bf16), grad_values_far.astype(bf16)), "seq", -1
    )
    grad_q_own, grad_keys_own, grad_values_own = back_block(keys_local, values_local, own_allowed)
    grad_queries = (grad_q_far + grad_q_own).astype(bf16)
    grad_keys = (grad_keys_own + carry_keys.astype(f32)).astype(bf16)
    grad_values = (grad_values_own + carry_values.astype(f32)).astype(bf16)
    grad_normed_one = (
        times_transpose(grad_queries, w_self[0])
        + times_transpose(grad_keys, w_self[1])
        + times_transpose(grad_values, w_self[2])
    )
    grad_one_shard = scatter_rows(grad_normed_one.astype(bf16), "tensor")
    grad_w_self = jnp.stack(
        (
            contract_rows(inputs_one, grad_queries),
            contract_rows(inputs_one, grad_keys),
            contract_rows(inputs_one, grad_values),
        )
    ).astype(bf16)
    sum_w_self, sum_w_self_out = group_sum((grad_w_self, grad_w_self_out), "seq", 2)
    normal_one_shard = own_rows(normal_one)
    grad_gain_one = jnp.sum(grad_one_shard * normal_one_shard, axis=0)
    grad_shift_one = jnp.sum(grad_one_shard, axis=0)
    grad_token_shard = own_rows(grad_after_self) + norm_back(
        grad_one_shard, normal_one_shard, own_rows(inv_one), gain_rows[0]
    )
    grad_tokens = gather_rows(grad_token_shard.astype(bf16), "tensor").astype(f32)

    shard_sums = scatter_columns(
        jnp.stack((grad_gain_one, grad_shift_one, grad_gain_three, grad_shift_three)), "tensor"
    )

    def token_sum(rows_in):
        return jnp.sum(rows_in.astype(f32), axis=0)

    vectors = jnp.stack(
        (
            grad_gain_two,
            grad_shift_two,
            token_sum(local_cols(grad_self_low)),
            token_sum(local_cols(grad_cross_low)),
            token_sum(local_cols(d_out)),
            token_sum(grad_cross_q),
            token_sum(grad_queries),
            token_sum(grad_values),
        )
    )
    vectors = jnp.concatenate((shard_sums, vectors, grad_b_up.reshape(-1, local_width)))
    vectors = butterfly_sum(vectors, "seq")
    grad_gain = jnp.stack((vectors[0], vectors[4], vectors[2]))
    grad_shift = jnp.stack((vectors[1], vectors[5], vectors[3]))
    grad_bias_out = vectors[6:9]
    grad_b_cross = jnp.stack((vectors[9], grad_value_bias))
    return (
        output_rows,
        grad_tokens,
        grad_text,
        grad_gain,
        grad_shift,
        sum_w_self.astype(f32),
        vectors[10:12],
        sum_w_self_out.astype(f32),
        sum_w_cross_q.astype(f32),
        grad_w_cross_kv,
        grad_b_cross,
        sum_w_cross_out.astype(f32),
        sum_w_up.astype(f32),
        vectors[12:].reshape(-1),
        sum_w_down.astype(f32),
        grad_bias_out,
    )


def solution(mesh):
    placed = (
        P("seq", None),
        P(),
        P(),
        P(),
        P(),
        P(),
        P(None, None, "tensor"),
        P(None, "tensor"),
        P("tensor", None),
        P(None, "tensor"),
        P(None, None, "tensor"),
        P(None, "tensor"),
        P("tensor", None),
        P(None, "tensor"),
        P("tensor"),
        P("tensor", None),
        P(),
        P("seq", None),
    )
    return jax.shard_map(
        per_device,
        mesh=mesh,
        in_specs=placed,
        out_specs=(
            P("seq", None),
            P("seq", None),
            P(),
            P(None, "tensor"),
            P(None, "tensor"),
            P(None, None, "tensor"),
            P(None, "tensor"),
            P("tensor", None),
            P(None, "tensor"),
            P(None, None, "tensor"),
            P(None, "tensor"),
            P("tensor", None),
            P(None, "tensor"),
            P("tensor"),
            P("tensor", None),
            P(None, "tensor"),
        ),
        check_vma=False,
    )
```

```python
import functools

import jax
import jax.numpy as jnp
from jax import lax
from jax.experimental import pallas as pl
from jax.experimental.pallas import tpu as pltpu
from jax.sharding import PartitionSpec as P

HEAD_SIZE = 64
ITEM_LEN = 1024
TILE = 256
STAT = 8
CHUNKS = 2
PAD = 256


epsilon = 1e-05
masked_fill = -1e30
f32, bf16 = jnp.float32, jnp.bfloat16
CUT, HAS_FAR, LENGTH, QUARTER, CORE, SEQ = 0, 1, 2, 4, 5, 6


def shifted(value, axis, steps):
    count = lax.axis_size(axis)
    leading, last = (max(0, -steps), min(count, count - steps))
    return lax.ppermute(value, axis, [(source, source + steps) for source in range(leading, last)])


def matmul_low(left, right):
    return jnp.dot(left, right, preferred_element_type=jnp.float32)


def contract_rows(left, right):
    return jnp.einsum("ra,rb->ab", left, right, preferred_element_type=jnp.float32)


def times_transpose(left, right):
    return jnp.einsum("ra,ba->rb", left, right, preferred_element_type=jnp.float32)


def norm_back(grad_normed, normal, inv_scale, gain):
    grad_normal = grad_normed * gain
    grad_mean = jnp.mean(grad_normal, axis=-1, keepdims=True)
    proj_mean = jnp.mean(grad_normal * normal, axis=-1, keepdims=True)
    return inv_scale * (grad_normal - grad_mean - normal * proj_mean)


def swapped(value, axis, distance):
    count = lax.axis_size(axis)
    return lax.ppermute(value, axis, [(source, source ^ distance) for source in range(count)])


def tied(value, *others):
    return lax.optimization_barrier((value, others))[0]


class Order:
    def __init__(self):
        self.pending = []

    def finish(self, result, during):
        self.pending = jax.tree.leaves(result)[-1:]
        if not during:
            return result
        return lax.optimization_barrier((result, tuple(during)))

    def __call__(self, step, *operands, during=()):
        operands, pending = lax.optimization_barrier((operands, self.pending))
        result = self.finish(step(*operands), during)
        self.pending = pending + self.pending
        return result

    def kernel(self, step, *operands, during=()):
        current.append(self)
        result = step(*operands)
        current.pop()
        return self.finish(result, during)


current = []


def kernel_call(kernel, prefetch=0, grid=(), in_specs=(), out_specs=None, scratch_shapes=(), **options):
    def run(*operands):
        order = current[-1] if current else None
        waits = order.pending if order else []
        count = len(operands)

        def body(*refs):
            kernel(*refs[:count], *refs[count + len(waits) :])

        result = pl.pallas_call(
            body,
            grid_spec=pltpu.PrefetchScalarGridSpec(
                num_scalar_prefetch=prefetch,
                grid=grid,
                in_specs=list(in_specs) + [pl.BlockSpec(memory_space=pl.ANY)] * len(waits),
                out_specs=out_specs,
                scratch_shapes=list(scratch_shapes),
            ),
            **options,
        )(*operands, *waits)
        return result

    return run


def axis_bits(axis):
    return (lax.axis_size(axis) - 1).bit_length()


def gather_relative(block, axis):
    blocks = {0: block}
    for bit in reversed(range(axis_bits(axis))):
        blocks.update(
            {d ^ (1 << bit): swapped(held, axis, 1 << bit) for d, held in list(blocks.items())}
        )
    return [blocks[d] for d in range(len(blocks))]


def gathered(block, across):
    return [block, swapped(block, "tensor", 1), across, swapped(across, "tensor", 1)]


def rank_bit(axis, bit):
    return (lax.axis_index(axis) >> bit) & 1


def shard_offset(axis, row_count):
    offset = 0
    for bit in range(axis_bits(axis)):
        offset = offset + rank_bit(axis, bit) * (row_count >> (bit + 1))
    return offset


def scatter_rows(partial_rows, axis):
    held = partial_rows
    for bit in range(axis_bits(axis)):
        half = held.shape[0] // 2
        mine = rank_bit(axis, bit)
        sent = lax.dynamic_slice_in_dim(held, (1 - mine) * half, half, 0)
        kept = lax.dynamic_slice_in_dim(held, mine * half, half, 0)
        arrived = swapped(sent, axis, 1 << bit)
        held = kept.astype(jnp.float32) + arrived.astype(jnp.float32)
        if bit + 1 < axis_bits(axis):
            held = held.astype(jnp.bfloat16)
    return held


def scatter_columns(partial, axis):
    held = partial
    for bit in reversed(range(axis_bits(axis))):
        half = held.shape[1] // 2
        mine = rank_bit(axis, bit)
        sent = lax.dynamic_slice_in_dim(held, (1 - mine) * half, half, 1)
        kept = lax.dynamic_slice_in_dim(held, mine * half, half, 1)
        held = kept + swapped(sent, axis, 1 << bit)
    return held


def butterfly_sum(value, axis):
    for bit in range(axis_bits(axis)):
        value = value + swapped(value, axis, 1 << bit)
    return value


def nn(left, right):
    return lax.dot_general(left, right, (((1,), (0,)), ((), ())), preferred_element_type=f32)


def nt(left, right):
    return lax.dot_general(left, right, (((1,), (1,)), ((), ())), preferred_element_type=f32)


def tile_rows(index):
    return pl.ds(pl.multiple_of(index * TILE, TILE), TILE)


def head_rows(head):
    return pl.ds(head * HEAD_SIZE, HEAD_SIZE)


def row_of(ref, row):
    return ref[...].astype(f32)[row : row + 1]


def turn(block):
    return jnp.transpose(block.astype(f32))


def by_head(turned, store):
    row_head = lax.broadcasted_iota(jnp.int32, turned.shape, 0) // HEAD_SIZE
    for head in range(store.shape[0]):
        store[head] = jnp.where(row_head == head, turned, 0.0).astype(store.dtype)


def tile_places(query_tile, key_tile):
    query_at = query_tile * TILE + lax.broadcasted_iota(jnp.int32, (1, TILE), 1)
    key_at = key_tile * TILE + lax.broadcasted_iota(jnp.int32, (TILE, 1), 0)
    return query_at, key_at


def own_mask(query_tile, cut):
    def allowed(key_tile):
        query_at, key_at = tile_places(query_tile, key_tile)
        first_key = jnp.where(query_at >= cut, cut, 0)
        return (key_at <= query_at) & (key_at >= first_key)

    return allowed


def far_mask(query_tile, cut):
    def allowed(key_tile):
        query_at, key_at = tile_places(query_tile, key_tile)
        first_key = jnp.where(query_at < cut, cut, TILE * 1024)
        return key_at >= first_key

    return allowed


def text_mask(query_tile, cut, lengths, slots):
    def allowed(key_tile):
        query_at, key_at = tile_places(query_tile, key_tile)
        first_key = jnp.where(query_at < cut, 0, slots)
        last_key = jnp.where(query_at < cut, lengths[0], slots + lengths[1])
        return (key_at >= first_key) & (key_at < last_key)

    return allowed


def own_tiles(query_tile, cut):
    return jnp.where(query_tile * TILE >= cut, cut // TILE, 0), query_tile + 1


def far_tiles(query_tile, cut, has_far, tiles):
    live = (query_tile * TILE < cut) & (has_far > 0)
    return cut // TILE, jnp.where(live, tiles, 0)


def attend_tiles(first, last, mask, key_ref, value_turned, query_heads, top, total, acc):
    heads = query_heads.shape[0]

    def step(key_tile, carry):
        allowed = mask(key_tile)
        keys = key_ref[tile_rows(key_tile), :]
        scores = [
            jnp.where(allowed, nn(keys, query_heads[head]), masked_fill) for head in range(heads)
        ]
        old_top = [top[pl.ds(head, 1), :] for head in range(heads)]
        new_top = [
            jnp.maximum(old, jnp.max(part, axis=0, keepdims=True))
            for old, part in zip(old_top, scores)
        ]
        weights = [jnp.exp(part - new) for part, new in zip(scores, new_top)]
        factors = [jnp.exp(old - new) for old, new in zip(old_top, new_top)]
        sums = [jnp.sum(part, axis=0, keepdims=True) for part in weights]
        values = [
            nn(value_turned[head_rows(head), tile_rows(key_tile)], weights[head].astype(bf16))
            for head in range(heads)
        ]
        for head in range(heads):
            row = pl.ds(head, 1)
            top[row, :] = new_top[head]
            total[row, :] = total[row, :] * factors[head] + sums[head]
            acc[head_rows(head), :] = acc[head_rows(head), :] * factors[head] + values[head]
        return carry

    lax.fori_loop(first, last, step, 0)


def turn_all(source, target):
    for tile in range(source.shape[0] // TILE):
        rows = pl.ds(tile * TILE, TILE)
        target[:, rows] = turn(source[rows, :]).astype(target.dtype)


def own_attend_kernel(flags, inputs, weight, bias, keys, values, queries, top, total, acc, value_turned, query_heads):
    tile = pl.program_id(0)
    cut = flags[0]

    @pl.when(tile == 0)
    def _():
        turn_all(values, value_turned)

    made = (nn(inputs[...], weight[...]) + row_of(bias, 0)).astype(bf16)
    made = made.astype(f32) * HEAD_SIZE**-0.5
    queries[...] = made.astype(bf16)
    by_head(jnp.transpose(made), query_heads)
    top[...] = jnp.full(top.shape, masked_fill, f32)
    total[...] = jnp.zeros(total.shape, f32)
    acc[...] = jnp.zeros(acc.shape, f32)
    first, last = own_tiles(tile, cut)
    attend_tiles(first, last, own_mask(tile, cut), keys, value_turned, query_heads, top, total, acc)


def far_attend_kernel(base, flags, queries, keys, values, top_in, total_in, acc_in, attended, log_total, value_turned, query_heads, top, total, acc):
    tile = base + pl.program_id(0)
    cut = flags[0]

    @pl.when(pl.program_id(0) == 0)
    def _():
        turn_all(values, value_turned)

    by_head(turn(queries[...]), query_heads)
    top[...] = top_in[...]
    total[...] = total_in[...]
    acc[...] = acc_in[...]
    first, last = far_tiles(tile, cut, flags[1], keys.shape[0] // TILE)
    attend_tiles(first, last, far_mask(tile, cut), keys, value_turned, query_heads, top, total, acc)
    log_total[...] = top[...] + jnp.log(total[...])
    for head in range(query_heads.shape[0]):
        acc[head_rows(head), :] = acc[head_rows(head), :] / total[pl.ds(head, 1), :]
    attended[...] = jnp.transpose(acc[...]).astype(bf16)


def spec_rows(width, base=0):
    return pl.BlockSpec((TILE, width), lambda tile: (base + tile, 0))


def spec_columns(height, base=0):
    return pl.BlockSpec((height, TILE), lambda tile: (0, base + tile))


def spec_layer(layer, rows, width):
    return pl.BlockSpec((None, rows, width), lambda tile: (layer, 0, 0))


def spec_side(side, rows, width):
    return pl.BlockSpec((rows, width), lambda tile: (0, side))


def spec_whole(*shape):
    return pl.BlockSpec(shape, lambda tile: (0,) * len(shape))


SMEM = pl.BlockSpec(memory_space=pltpu.SMEM)
params = pltpu.CompilerParams(vmem_limit_bytes=60 * 2**20)
small = pltpu.CompilerParams(vmem_limit_bytes=16 * 2**20)


LIGHT = 0.01


def cost(us):
    return pl.CostEstimate(
        flops=int(us * 1.15e9), bytes_accessed=int(us * 3.6e6), transcendentals=0
    )


def own_attend(flags, inputs, weight, bias, both):
    rows, width = both.shape[0], both.shape[1] // 2
    depth = inputs.shape[1]
    heads = width // HEAD_SIZE
    return kernel_call(
        own_attend_kernel,
        grid=(rows // TILE,),
        in_specs=[SMEM, spec_rows(depth), spec_layer(0, depth, width), spec_whole(*bias.shape), spec_side(0, rows, width), spec_side(1, rows, width)],
        out_specs=[spec_rows(width), spec_columns(STAT), spec_columns(STAT), spec_columns(width)],
        out_shape=[
            jax.ShapeDtypeStruct((rows, width), bf16),
            jax.ShapeDtypeStruct((STAT, rows), f32),
            jax.ShapeDtypeStruct((STAT, rows), f32),
            jax.ShapeDtypeStruct((width, rows), f32),
        ],
        scratch_shapes=[pltpu.VMEM((width, rows), bf16), pltpu.VMEM((heads, width, TILE), bf16)],
        compiler_params=params,
        cost_estimate=cost(LIGHT * 16),
        name="own_attend",
    )(flags, inputs, weight, bias, both, both)


def far_attend(chunk, flags, queries, both, top, total, acc):
    rows, width = both.shape[0], both.shape[1] // 2
    heads = width // HEAD_SIZE
    tiles = rows // CHUNKS // TILE
    base = chunk * tiles
    return kernel_call(
        functools.partial(far_attend_kernel, base),
        grid=(tiles,),
        in_specs=[
            SMEM,
            spec_rows(width, base),
            spec_side(0, rows, width),
            spec_side(1, rows, width),
            spec_columns(STAT, base),
            spec_columns(STAT, base),
            spec_columns(width, base),
        ],
        out_specs=[spec_rows(width), spec_columns(STAT)],
        out_shape=[
            jax.ShapeDtypeStruct((tiles * TILE, width), bf16),
            jax.ShapeDtypeStruct((STAT, tiles * TILE), f32),
        ],
        scratch_shapes=[
            pltpu.VMEM((width, rows), bf16),
            pltpu.VMEM((heads, width, TILE), bf16),
            pltpu.VMEM((STAT, TILE), f32),
            pltpu.VMEM((STAT, TILE), f32),
            pltpu.VMEM((width, TILE), f32),
        ],
        compiler_params=params,
        cost_estimate=cost(LIGHT * 4),
        name="far_attend",
    )(flags, queries, both, both, top, total, acc)


def back_tiles(first, last, mask, refs, stats):
    keys, values, key_turned, query_heads, grad_heads, grad_turned, query_turned, gq, gk, gv = refs
    log_total, inner = stats
    heads = query_heads.shape[0]

    def step(key_tile, carry):
        allowed = mask(key_tile)
        place = tile_rows(key_tile)
        key_block = keys[place, :]
        value_block = values[place, :]
        scores = [nn(key_block, query_heads[head]) for head in range(heads)]
        grad_probs = [nn(value_block, grad_heads[head]) for head in range(heads)]
        probs = [
            jnp.exp(jnp.where(allowed, scores[head], masked_fill) - log_total[pl.ds(head, 1), :])
            for head in range(heads)
        ]
        grad_scores = [
            (probs[head] * (grad_probs[head] - inner[pl.ds(head, 1), :])).astype(bf16)
            for head in range(heads)
        ]
        for head in range(heads):
            rows = head_rows(head)
            gv[rows, place] += nt(grad_turned[rows, :], probs[head].astype(bf16))
            gk[rows, place] += nt(query_turned[rows, :], grad_scores[head])
            gq[rows, :] += nn(key_turned[rows, place], grad_scores[head])
        return carry

    lax.fori_loop(first, last, step, 0)


def far_back_kernel(flags, grad_rows, weight, queries, attended, log_total, keys, values, grad_att, inner, grad_q, grad_both, key_turned, query_heads, grad_heads, query_turned, grad_turned, gk, gv):
    tile = pl.program_id(0)
    cut = flags[0]

    @pl.when(tile == 0)
    def _():
        turn_all(keys, key_turned)
        gk[...] = jnp.zeros(gk.shape, f32)
        gv[...] = jnp.zeros(gv.shape, f32)

    made = nt(grad_rows[...], weight[...]).astype(bf16)
    grad_att[...] = made
    turned = turn(made)
    by_head(turned, grad_heads)
    grad_turned[...] = turned.astype(bf16)
    product = turned * turn(attended[...])
    inner[...] = jnp.zeros(inner.shape, f32)
    for head in range(query_heads.shape[0]):
        inner[pl.ds(head, 1), :] = jnp.sum(product[head * HEAD_SIZE : (head + 1) * HEAD_SIZE], axis=0, keepdims=True)
    turned = turn(queries[...])
    by_head(turned, query_heads)
    query_turned[...] = turned.astype(bf16)
    grad_q[...] = jnp.zeros(grad_q.shape, f32)
    first, last = far_tiles(tile, cut, flags[1], keys.shape[0] // TILE)
    refs = (keys, values, key_turned, query_heads, grad_heads, grad_turned, query_turned, grad_q, gk, gv)
    back_tiles(first, last, far_mask(tile, cut), refs, (log_total, inner))

    @pl.when(tile == pl.num_programs(0) - 1)
    def _():
        for part in range(keys.shape[0] // TILE):
            rows = pl.ds(part * TILE, TILE)
            width = gk.shape[0]
            grad_both[rows, :width] = jnp.transpose(gk[:, rows]).astype(bf16)
            grad_both[rows, width:] = jnp.transpose(gv[:, rows]).astype(bf16)


def far_back(flags, grad_rows, weight, queries, attended, log_total, both):
    rows, width = both.shape[0], both.shape[1] // 2
    depth = grad_rows.shape[1]
    heads = width // HEAD_SIZE
    return kernel_call(
        far_back_kernel,
        grid=(rows // TILE,),
        in_specs=[SMEM, spec_rows(depth), spec_whole(width, depth), spec_rows(width), spec_rows(width), spec_columns(STAT), spec_side(0, rows, width), spec_side(1, rows, width)],
        out_specs=[spec_rows(width), spec_columns(STAT), spec_columns(width), spec_whole(rows, 2 * width)],
        out_shape=[
            jax.ShapeDtypeStruct((rows, width), bf16),
            jax.ShapeDtypeStruct((STAT, rows), f32),
            jax.ShapeDtypeStruct((width, rows), f32),
            jax.ShapeDtypeStruct((rows, 2 * width), bf16),
        ],
        scratch_shapes=[
            pltpu.VMEM((width, rows), bf16),
            pltpu.VMEM((heads, width, TILE), bf16),
            pltpu.VMEM((heads, width, TILE), bf16),
            pltpu.VMEM((width, TILE), bf16),
            pltpu.VMEM((width, TILE), bf16),
            pltpu.VMEM((width, rows), f32),
            pltpu.VMEM((width, rows), f32),
        ],
        compiler_params=params,
        cost_estimate=cost(LIGHT * 9),
        name="far_back",
    )(flags, grad_rows, weight, queries, attended, log_total, both, both)


def own_back_kernel(flags, grad_att, inner, queries, log_total, keys, values, grad_q_in, grad_q, grad_k, grad_v, key_turned, query_heads, grad_heads, query_turned, grad_turned, gq, gk, gv):
    tile = pl.program_id(0)
    cut = flags[0]

    @pl.when(tile == 0)
    def _():
        turn_all(keys, key_turned)
        gk[...] = jnp.zeros(gk.shape, f32)
        gv[...] = jnp.zeros(gv.shape, f32)

    turned = turn(grad_att[...])
    by_head(turned, grad_heads)
    grad_turned[...] = turned.astype(bf16)
    turned = turn(queries[...])
    by_head(turned, query_heads)
    query_turned[...] = turned.astype(bf16)
    gq[...] = grad_q_in[...]
    first, last = own_tiles(tile, cut)
    refs = (keys, values, key_turned, query_heads, grad_heads, grad_turned, query_turned, gq, gk, gv)
    back_tiles(first, last, own_mask(tile, cut), refs, (log_total, inner))
    grad_q[...] = (jnp.transpose(gq[...]) * HEAD_SIZE**-0.5).astype(grad_q.dtype)

    @pl.when(tile == pl.num_programs(0) - 1)
    def _():
        for part in range(keys.shape[0] // TILE):
            rows = pl.ds(part * TILE, TILE)
            grad_k[rows, :] = jnp.transpose(gk[:, rows])
            grad_v[rows, :] = jnp.transpose(gv[:, rows])


def own_back(flags, grad_att, inner, queries, log_total, both, grad_q):
    rows, width = both.shape[0], both.shape[1] // 2
    heads = width // HEAD_SIZE
    return kernel_call(
        own_back_kernel,
        grid=(rows // TILE,),
        in_specs=[SMEM, spec_rows(width), spec_columns(STAT), spec_rows(width), spec_columns(STAT), spec_side(0, rows, width), spec_side(1, rows, width), spec_columns(width)],
        out_specs=[spec_rows(width), spec_whole(rows, width), spec_whole(rows, width)],
        out_shape=[
            jax.ShapeDtypeStruct((rows, width), bf16),
            jax.ShapeDtypeStruct((rows, width), f32),
            jax.ShapeDtypeStruct((rows, width), f32),
        ],
        scratch_shapes=[
            pltpu.VMEM((width, rows), bf16),
            pltpu.VMEM((heads, width, TILE), bf16),
            pltpu.VMEM((heads, width, TILE), bf16),
            pltpu.VMEM((width, TILE), bf16),
            pltpu.VMEM((width, TILE), bf16),
            pltpu.VMEM((width, TILE), f32),
            pltpu.VMEM((width, rows), f32),
            pltpu.VMEM((width, rows), f32),
        ],
        compiler_params=params,
        cost_estimate=cost(LIGHT * 16),
        name="own_back",
    )(flags, grad_att, inner, queries, log_total, both, both, grad_q)


def norm_parts(rows_in):
    row_mean = jnp.mean(rows_in, axis=-1, keepdims=True)
    centered = rows_in - row_mean
    inv_scale = lax.rsqrt(jnp.mean(centered * centered, axis=-1, keepdims=True) + epsilon)
    return centered * inv_scale, inv_scale


def enter_kernel(tokens, wk, wv, bias, gains, shifts, inputs, both):
    normal, _ = norm_parts(tokens[...].astype(f32))
    low = (normal * row_of(gains, 0) + row_of(shifts, 0)).astype(bf16)
    inputs[...] = low
    width = wk.shape[1]
    both[:, :width] = nn(low, wk[...]).astype(bf16)
    both[:, width:] = (nn(low, wv[...]) + row_of(bias, 1)).astype(bf16)


def enter(tokens, w_self, bias, gains, shifts):
    rows, depth = tokens.shape
    width = w_self.shape[2]
    return kernel_call(
        enter_kernel,
        grid=(rows // TILE,),
        in_specs=[
            spec_rows(depth),
            spec_layer(1, depth, width),
            spec_layer(2, depth, width),
            spec_whole(*bias.shape),
            spec_whole(*gains.shape),
            spec_whole(*shifts.shape),
        ],
        out_specs=[spec_rows(depth), spec_rows(2 * width)],
        out_shape=[
            jax.ShapeDtypeStruct((rows, depth), bf16),
            jax.ShapeDtypeStruct((rows, 2 * width), bf16),
        ],
        compiler_params=params,
        cost_estimate=cost(LIGHT * 4),
        name="enter",
    )(tokens, w_self, w_self, bias, gains, shifts)


def after_self_kernel(base, slots, flags, tokens, *refs):
    parts, weights, refs = refs[:4], refs[4:8], refs[8:]
    bias, gains, shifts, wq, bq, text_keys, text_values = refs[:7]
    after, inputs, queries, attended, log_total = refs[7:12]
    value_turned, query_heads, top, total, acc = refs[12:]
    tile = base + pl.program_id(0)

    @pl.when(pl.program_id(0) == 0)
    def _():
        turn_all(text_values, value_turned)

    product = nn(parts[0][...], weights[0][...])
    for part, weight in zip(parts[1:], weights[1:]):
        product = product + nn(part[...], weight[...])
    rows_in = tokens[...].astype(f32) + (product + row_of(bias, 0))
    after[...] = rows_in
    normal, _ = norm_parts(rows_in)
    low = (normal * row_of(gains, 1) + row_of(shifts, 1)).astype(bf16)
    inputs[...] = low
    made = (nn(low, wq[...]) + row_of(bq, 0)).astype(bf16).astype(f32) * HEAD_SIZE**-0.5
    queries[...] = made.astype(bf16)
    by_head(jnp.transpose(made), query_heads)
    top[...] = jnp.full(top.shape, masked_fill, f32)
    total[...] = jnp.zeros(total.shape, f32)
    acc[...] = jnp.zeros(acc.shape, f32)
    mask = text_mask(tile, flags[CUT], (flags[LENGTH], flags[LENGTH + 1]), slots)
    attend_tiles(0, 1, mask, text_keys, value_turned, query_heads, top, total, acc)
    log_total[...] = top[...] + jnp.log(total[...])
    for head in range(query_heads.shape[0]):
        acc[head_rows(head), :] = acc[head_rows(head), :] / total[pl.ds(head, 1), :]
    attended[...] = jnp.transpose(acc[...]).astype(bf16)


def after_self(chunk, flags, tokens, parts, weights, bias, gains, shifts, wq, bq, text_keys, text_values):
    rows, depth = tokens.shape
    width = wq.shape[1]
    heads = width // HEAD_SIZE
    window = text_keys.shape[0]
    assert window == TILE
    tiles = rows // CHUNKS // TILE
    base = chunk * tiles
    part_rows = tiles * TILE
    return kernel_call(
        functools.partial(after_self_kernel, base, window // 2),
        grid=(tiles,),
        in_specs=[SMEM, spec_rows(depth, base)]
        + [spec_rows(width)] * 4
        + [spec_whole(width, depth)] * 4
        + [spec_whole(*bias.shape)] * 3
        + [spec_whole(depth, width), spec_whole(*bq.shape)]
        + [spec_whole(window, width)] * 2,
        out_specs=[
            spec_rows(depth),
            spec_rows(depth),
            spec_rows(width),
            spec_rows(width),
            spec_columns(STAT),
        ],
        out_shape=[
            jax.ShapeDtypeStruct((part_rows, depth), f32),
            jax.ShapeDtypeStruct((part_rows, depth), bf16),
            jax.ShapeDtypeStruct((part_rows, width), bf16),
            jax.ShapeDtypeStruct((part_rows, width), bf16),
            jax.ShapeDtypeStruct((STAT, part_rows), f32),
        ],
        scratch_shapes=[
            pltpu.VMEM((width, window), bf16),
            pltpu.VMEM((heads, width, TILE), bf16),
            pltpu.VMEM((STAT, TILE), f32),
            pltpu.VMEM((STAT, TILE), f32),
            pltpu.VMEM((width, TILE), f32),
        ],
        compiler_params=params,
        cost_estimate=cost(LIGHT * 7),
        name="after_self",
    )(flags, tokens, *parts, *weights, bias, gains, shifts, wq, bq, text_keys, text_values)


def split_store(flags, tile, half_tiles, block, sent, kept):
    place = pl.ds(pl.multiple_of((tile % half_tiles) * TILE, TILE), TILE)
    own = tile // half_tiles == flags[CORE]

    @pl.when(own)
    def _():
        kept[place, :] = block

    @pl.when(jnp.logical_not(own))
    def _():
        sent[place, :] = block


def after_cross_kernel(half_tiles, flags, rows_ref, *refs):
    parts, weights, refs = refs[:4], refs[4:8], refs[8:]
    grad_hidden, w_up, b_up, bias, gains, shifts = refs[:6]
    after, inputs, hidden, grad_pre, sent, kept = refs[-6:]
    product = nn(parts[0][...], weights[0][...])
    for part, weight in zip(parts[1:], weights[1:]):
        product = product + nn(part[...], weight[...])
    rows_in = rows_ref[...] + (product + row_of(bias, 1))
    after[...] = rows_in
    normal, _ = norm_parts(rows_in)
    low = (normal * row_of(gains, 2) + row_of(shifts, 2)).astype(bf16)
    inputs[...] = low
    pre = nn(low, w_up[...]) + row_of(b_up, 0)
    square = pre * pre
    root = (2 / jnp.pi) ** 0.5
    bent = jnp.tanh(root * (pre + 0.044715 * (square * pre)))
    hidden[...] = (0.5 * pre * (1 + bent)).astype(bf16)
    slope = 0.5 * (1 + bent) + (0.5 * root) * pre * (1 - bent * bent) * (1 + 0.134145 * square)
    low_grad = (slope * grad_hidden[...].astype(f32)).astype(bf16)
    grad_pre[...] = low_grad
    block = nt(low_grad, w_up[...]).astype(bf16)
    split_store(flags, pl.program_id(0), half_tiles, block, sent, kept)


ANY = pl.BlockSpec(memory_space=pl.ANY)


def after_cross(chunk, flags, rows_in, parts, weights, grad_hidden, w_up, b_up, bias, gains, shifts, wholes):
    part_rows, depth = rows_in.shape
    width = parts[0].shape[1]
    units = w_up.shape[1]
    tiles = part_rows // TILE
    base = chunk * tiles
    rows = part_rows * CHUNKS
    operands = (flags, rows_in, *parts, *weights, grad_hidden, w_up, b_up, bias, gains, shifts)
    aliases = {len(operands) + place: 1 + place for place in range(len(wholes))}
    return kernel_call(
        functools.partial(after_cross_kernel, tiles // 2),
        grid=(tiles,),
        in_specs=[SMEM, spec_rows(depth)]
        + [spec_rows(width)] * 4
        + [spec_whole(width, depth)] * 4
        + [spec_rows(units, base), spec_whole(depth, units), spec_whole(1, units)]
        + [spec_whole(*bias.shape)] * 3
        + [ANY] * len(wholes),
        out_specs=[
            spec_rows(depth),
            spec_rows(depth, base),
            spec_rows(units, base),
            spec_rows(units, base),
            spec_whole(part_rows // 2, depth),
            spec_whole(part_rows // 2, depth),
        ],
        out_shape=[
            jax.ShapeDtypeStruct((part_rows, depth), f32),
            jax.ShapeDtypeStruct((rows, depth), bf16),
            jax.ShapeDtypeStruct((rows, units), bf16),
            jax.ShapeDtypeStruct((rows, units), bf16),
            jax.ShapeDtypeStruct((part_rows // 2, depth), bf16),
            jax.ShapeDtypeStruct((part_rows // 2, depth), bf16),
        ],
        input_output_aliases=aliases,
        compiler_params=params,
        cost_estimate=cost(LIGHT * 10),
        name="after_cross",
    )(*operands, *wholes)


def split_product_kernel(half_tiles, turned, flags, *refs):
    count = (len(refs) - 2) // 2
    product = nt if turned else nn
    block = product(refs[0][...], refs[count][...])
    for place in range(1, count):
        block = block + product(refs[place][...], refs[count + place][...])
    split_store(flags, pl.program_id(0), half_tiles, block.astype(bf16), *refs[-2:])


def split_product(chunk, flags, lefts, rights, turned):
    part_rows = lefts[0].shape[0] // CHUNKS
    depth = rights[0].shape[-2 if turned else -1]
    tiles = part_rows // TILE
    width = lefts[0].shape[1]
    half = jax.ShapeDtypeStruct((part_rows // 2, depth), bf16)
    return kernel_call(
        functools.partial(split_product_kernel, tiles // 2, turned),
        grid=(tiles,),
        in_specs=[SMEM]
        + [spec_rows(width, chunk * tiles)] * len(lefts)
        + [
            spec_whole(*right.shape) if right.ndim == 2 else spec_layer(layer, *right.shape[1:])
            for layer, right in enumerate(rights)
        ],
        out_specs=[spec_whole(part_rows // 2, depth)] * 2,
        out_shape=[half, half],
        compiler_params=params,
        cost_estimate=cost(LIGHT * 2.3),
        name="split_product",
    )(flags, *lefts, *rights)


def scatter_halves(sent, kept, quarter):
    both = kept.astype(f32) + swapped(sent, "tensor", 1).astype(f32)
    rows = sent.shape[0] // 2
    place = (quarter & 1) * rows
    other = lax.dynamic_slice_in_dim(both, rows - place, rows, 0).astype(bf16)
    return lax.dynamic_slice_in_dim(both, place, rows, 0), swapped(other, "tensor", 2)


def first_add_kernel(flags, arrived, kept, own, other):
    both = kept[...].astype(f32) + arrived[...].astype(f32)
    rows = own.shape[0]
    for second in range(2):

        @pl.when((flags[QUARTER] & 1) == second)
        def _(second=second):
            own[...] = both[second * rows : (second + 1) * rows]
            other[...] = both[(1 - second) * rows : (2 - second) * rows].astype(bf16)


def first_add(flags, arrived, kept):
    rows, depth = kept.shape[0] // 2, kept.shape[1]
    return kernel_call(
        first_add_kernel,
        in_specs=[SMEM] + [pl.BlockSpec(memory_space=pltpu.VMEM)] * 2,
        out_specs=[pl.BlockSpec(memory_space=pltpu.VMEM)] * 2,
        out_shape=[
            jax.ShapeDtypeStruct((rows, depth), f32),
            jax.ShapeDtypeStruct((rows, depth), bf16),
        ],
        compiler_params=small,
        cost_estimate=cost(LIGHT * 1.3),
        name="first_add",
    )(flags, arrived, kept)


def quarter_of(rel):
    return (rel & 1) * 2 + (rel >> 1)


def norm_back_rows_kernel(gain_row, flags, kept, arrived, source, residual, gains, result, sums):
    grad = kept[...] + arrived[...].astype(f32)
    normal, inv_scale = norm_parts(source[...].astype(f32))
    sums[...] = jnp.zeros(sums.shape, f32)
    sums[0:1, :] = jnp.sum(grad * normal, axis=0, keepdims=True)
    sums[1:2, :] = jnp.sum(grad, axis=0, keepdims=True)
    back = norm_back(grad, normal, inv_scale, row_of(gains, gain_row))
    result[...] = (residual[...].astype(f32) + back).astype(bf16)


def norm_back_rows(chunk, gain_row, flags, kept, arrived, source, residual, gains):
    rows, depth = kept.shape
    source_base = 4 * chunk if source.shape[0] > 4 * rows else 0

    def at(base):
        return pl.BlockSpec((rows, depth), lambda step, flags: (base + flags[QUARTER], 0))

    def whole(*shape):
        return pl.BlockSpec(shape, lambda step, flags: (0, 0))

    return kernel_call(
        functools.partial(norm_back_rows_kernel, gain_row),
        prefetch=1,
        grid=(1,),
        in_specs=[
            whole(rows, depth),
            whole(rows, depth),
            at(source_base),
            at(4 * chunk),
            whole(*gains.shape),
        ],
        out_specs=[whole(rows, depth), whole(STAT, depth)],
        out_shape=[
            jax.ShapeDtypeStruct((rows, depth), bf16),
            jax.ShapeDtypeStruct((STAT, depth), f32),
        ],
        compiler_params=small,
        cost_estimate=cost(LIGHT * 1.7),
        name="norm_back_rows",
    )(flags, kept, arrived, source, residual, gains)


def cross_back_kernel(base, slots, flags, *refs):
    pieces, refs = refs[:4], refs[4:]
    weight, queries, attended, log_total, text_keys, text_values = refs[:6]
    grad_rows, grad_q, grad_k, grad_v = refs[6:10]
    key_turned, query_heads, grad_heads, query_turned, grad_turned, inner, gq, gk, gv = refs[10:]
    step = pl.program_id(0)
    tile = base + step

    @pl.when(step == 0)
    def _():
        rows = pieces[0].shape[0]
        for rel, piece in enumerate(pieces):
            start = pl.multiple_of((flags[QUARTER] ^ quarter_of(rel)) * rows, rows)
            grad_rows[pl.ds(start, rows), :] = piece[...]
        turn_all(text_keys, key_turned)
        gk[...] = jnp.zeros(gk.shape, f32)
        gv[...] = jnp.zeros(gv.shape, f32)

    made = nt(grad_rows[tile_rows(step), :], weight[...]).astype(bf16)
    turned = turn(made)
    by_head(turned, grad_heads)
    grad_turned[...] = turned.astype(bf16)
    product = turned * turn(attended[...])
    for head in range(query_heads.shape[0]):
        part = product[head * HEAD_SIZE : (head + 1) * HEAD_SIZE]
        inner[pl.ds(head, 1), :] = jnp.sum(part, axis=0, keepdims=True)
    turned = turn(queries[...])
    by_head(turned, query_heads)
    query_turned[...] = turned.astype(bf16)
    gq[...] = jnp.zeros(gq.shape, f32)
    mask = text_mask(tile, flags[CUT], (flags[LENGTH], flags[LENGTH + 1]), slots)
    refs = (text_keys, text_values, key_turned, query_heads, grad_heads, grad_turned, query_turned, gq, gk, gv)
    back_tiles(0, 1, mask, refs, (log_total, inner))
    grad_q[...] = (jnp.transpose(gq[...]) * HEAD_SIZE**-0.5).astype(bf16)

    @pl.when(step == pl.num_programs(0) - 1)
    def _():
        grad_k[...] = jnp.transpose(gk[...])
        grad_v[...] = jnp.transpose(gv[...])


def cross_back(chunk, flags, pieces, weight, queries, attended, log_total, text_keys, text_values):
    part_rows, width = queries.shape
    depth = weight.shape[1]
    heads = width // HEAD_SIZE
    window = text_keys.shape[0]
    tiles = part_rows // TILE
    return kernel_call(
        functools.partial(cross_back_kernel, chunk * tiles, window // 2),
        grid=(tiles,),
        in_specs=[SMEM]
        + [spec_whole(part_rows // 4, depth)] * 4
        + [spec_whole(width, depth), spec_rows(width), spec_rows(width), spec_columns(STAT)]
        + [spec_whole(window, width)] * 2,
        out_specs=[
            spec_whole(part_rows, depth),
            spec_rows(width),
            spec_whole(window, width),
            spec_whole(window, width),
        ],
        out_shape=[
            jax.ShapeDtypeStruct((part_rows, depth), bf16),
            jax.ShapeDtypeStruct((part_rows, width), bf16),
            jax.ShapeDtypeStruct((window, width), f32),
            jax.ShapeDtypeStruct((window, width), f32),
        ],
        scratch_shapes=[
            pltpu.VMEM((width, window), bf16),
            pltpu.VMEM((heads, width, TILE), bf16),
            pltpu.VMEM((heads, width, TILE), bf16),
            pltpu.VMEM((width, TILE), bf16),
            pltpu.VMEM((width, TILE), bf16),
            pltpu.VMEM((STAT, TILE), f32),
            pltpu.VMEM((width, TILE), f32),
            pltpu.VMEM((width, window), f32),
            pltpu.VMEM((width, window), f32),
        ],
        compiler_params=params,
        cost_estimate=cost(LIGHT * 6),
        name="cross_back",
    )(flags, *pieces, weight, queries, attended, log_total, text_keys, text_values)


def back_to_self_kernel(*refs):
    parts, weights, refs = refs[:4], refs[4:8], refs[8:]
    source, residual, gains = refs[:3]
    result, sums = refs[-2:]
    grad = nt(parts[0][...], weights[0][...])
    for part, weight in zip(parts[1:], weights[1:]):
        grad = grad + nt(part[...], weight[...])
    normal, inv_scale = norm_parts(source[...])
    coming = residual[...].astype(f32)
    low = (coming + norm_back(grad, normal, inv_scale, row_of(gains, 1))).astype(bf16)
    result[...] = low

    @pl.when(pl.program_id(0) == 0)
    def _():
        sums[...] = jnp.zeros(sums.shape, f32)

    for row, term in enumerate((grad * normal, grad, low.astype(f32), coming)):
        sums[row : row + 1, :] += jnp.sum(term, axis=0, keepdims=True)


def back_to_self(chunk, parts, weights, source, residual, gains, wholes):
    part_rows, depth = source.shape
    width = parts[0].shape[1]
    tiles = part_rows // TILE
    operands = (*parts, *weights, source, residual, gains)
    return kernel_call(
        back_to_self_kernel,
        grid=(tiles,),
        in_specs=[spec_rows(width)] * 4
        + [spec_whole(depth, width)] * 4
        + [spec_rows(depth), spec_rows(depth), spec_whole(*gains.shape)]
        + [ANY] * len(wholes),
        out_specs=[spec_rows(depth, chunk * tiles), spec_whole(STAT, depth)],
        out_shape=[
            jax.ShapeDtypeStruct((part_rows * CHUNKS, depth), bf16),
            jax.ShapeDtypeStruct((STAT, depth), f32),
        ],
        input_output_aliases={len(operands) + place: place for place in range(len(wholes))},
        compiler_params=params,
        cost_estimate=cost(LIGHT * 5),
        name="back_to_self",
    )(*operands, *wholes)


def place_quarters_kernel(flags, *refs):
    for place, piece in enumerate(refs[:-1]):

        @pl.when(pl.program_id(0) == place)
        def _(piece=piece):
            refs[-1][...] = piece[...].astype(refs[-1].dtype)


def place_quarters(flags, chunks, dtype):
    rows, depth = chunks[0][0].shape
    pieces = [piece for chunk in chunks for piece in chunk]
    return kernel_call(
        place_quarters_kernel,
        prefetch=1,
        grid=(len(pieces),),
        in_specs=[pl.BlockSpec((rows, depth), lambda step, flags: (0, 0))] * len(pieces),
        out_specs=pl.BlockSpec(
            (rows, depth),
            lambda step, flags: (step // 4 * 4 + (flags[QUARTER] ^ quarter_of(step % 4)), 0),
        ),
        out_shape=jax.ShapeDtypeStruct((rows * len(pieces), depth), dtype),
        compiler_params=small,
        cost_estimate=cost(LIGHT * 5),
        name="place_quarters",
    )(flags, *pieces)


def place_relative_kernel(turned, places, held, arrived, *results):
    step = pl.program_id(0)
    half = pl.num_programs(0) // 2
    each = pl.num_programs(0) // len(results)
    piece = step ^ places[0]

    def store(source):
        for place, result in enumerate(results):

            @pl.when(step // each == place)
            def _(result=result, place=place):
                if place < turned:
                    result[...] = turn(source[0])
                    return
                if result.ndim == 2:
                    result[...] = source[0].astype(f32)
                    return
                width = result.shape[2]
                for part in range(result.shape[0]):
                    result[part] = source[0, :, part * width : (part + 1) * width].astype(f32)

    @pl.when(piece < half)
    def _():
        store(held)

    @pl.when(piece >= half)
    def _():
        store(arrived)


def place_relative(place, held, arrived, parts, stacked, turned):
    count, rows, width = held.shape
    each = 2 * count // stacked
    if turned and rows % 128:
        results = place_relative(place, held, arrived, parts, stacked, 0)
        return [jnp.transpose(part) for part in results[:turned]] + list(results[turned:])
    if parts > 1:
        out_specs = [pl.BlockSpec((parts, rows, width // parts), lambda step, place: (0, step, 0))]
        shape = [jax.ShapeDtypeStruct((parts, 2 * count * rows, width // parts), f32)]
    else:
        out_specs = [
            pl.BlockSpec(
                (rows, width),
                lambda step, place, first=number * each: (jnp.clip(step - first, 0, each - 1), 0),
            )
            for number in range(stacked)
        ]
        shape = [jax.ShapeDtypeStruct((each * rows, width), f32)] * stacked
    for number in range(turned):
        out_specs[number] = pl.BlockSpec(
            (width, rows),
            lambda step, place, first=number * each: (0, jnp.clip(step - first, 0, each - 1)),
        )
        shape[number] = jax.ShapeDtypeStruct((width, each * rows), f32)
    piece = pl.BlockSpec((1, rows, width), lambda step, place: ((step ^ place[0]) % count, 0, 0))
    return kernel_call(
        functools.partial(place_relative_kernel, turned),
        prefetch=1,
        grid=(2 * count,),
        in_specs=[piece, piece],
        out_specs=out_specs,
        out_shape=shape,
        compiler_params=small,
        cost_estimate=cost(LIGHT * 5),
        name="place_relative",
    )(place, held, arrived)


def halving_orders(bits):
    return list(range(bits)), [1, 0] + list(range(2, bits))


class HalvingSum:
    def __init__(self):
        self.orders = halving_orders(axis_bits("seq"))
        self.odd = lax.axis_index("tensor") & 1
        self.mine = []
        for even, odd in zip(*self.orders):
            self.mine.append(jnp.where(self.odd == 0, rank_bit("seq", even), rank_bit("seq", odd)))
        place = 0
        for mine in self.mine:
            place = place * 2 + mine
        self.place = jnp.reshape(place, (1,)).astype(jnp.int32)

    def swap(self, value, level):
        count = lax.axis_size("tensor")
        pairs = []
        for seq in range(lax.axis_size("seq")):
            for tensor in range(count):
                partner = seq ^ (1 << self.orders[tensor & 1][level])
                pairs.append((seq * count + tensor, partner * count + tensor))
        return lax.ppermute(value, ("seq", "tensor"), pairs)

    def scatter(self, held, level):
        rows = held.shape[0] // 2
        mine = self.mine[level]
        sent = lax.dynamic_slice_in_dim(held, (1 - mine) * rows, rows, 0)
        arrived = self.swap(sent, level)
        kept = lax.dynamic_slice_in_dim(held, mine * rows, rows, 0)
        return (kept.astype(f32) + arrived.astype(f32)).astype(bf16)

    def gather(self, held, level):
        return jnp.concatenate((held, self.swap(held, level)))

    def gathers(self, order, value):
        state = {"held": value}
        count = len(self.mine)

        def join(level, held, arrived):
            held = jnp.concatenate((held, arrived))
            state["held"] = held
            if level > 0:
                state["arrived"] = self.swap(held, level - 1)
            return held

        state["arrived"] = self.swap(value, count - 1)
        for level in reversed(range(count)):
            yield functools.partial(join, level), state, order

    def steps(self, order, value, parts=1, stacked=1, turned=0):
        state = {"held": value}
        count = len(self.mine)

        def scatter_send(level):
            rows = state["held"].shape[0] // 2
            mine = self.mine[level]
            sent = lax.dynamic_slice_in_dim(state["held"], (1 - mine) * rows, rows, 0)
            state["arrived"] = self.swap(sent, level)

        def scatter_add(level, held, arrived):
            rows = held.shape[0] // 2
            kept = lax.dynamic_slice_in_dim(held, self.mine[level] * rows, rows, 0)
            held = (kept.astype(f32) + arrived.astype(f32)).astype(bf16)
            state["held"] = held
            if level + 1 < count:
                scatter_send(level + 1)
            else:
                state["held"] = held[None]
                state["arrived"] = self.swap(state["held"], level)
            return held

        def gather_join(level, held, arrived):
            held = jnp.concatenate((held, arrived))
            state["held"] = held
            state["arrived"] = self.swap(held, level - 1)
            return held

        def finish(held, arrived):
            return place_relative(self.place, held, arrived, parts, stacked, turned)

        scatter_send(0)
        for level in range(count):
            yield functools.partial(scatter_add, level), state, order
        for level in reversed(range(1, count)):
            yield functools.partial(gather_join, level), state, order
        yield finish, state, order.kernel


def text_sums_kernel(count, flags, first, second, grad_k, grad_v):
    item = pl.program_id(0)
    has_first = (item < count).astype(f32)
    has_second = (item > 0).astype(f32)
    for place, result in enumerate((grad_k, grad_v)):
        total = first[0, place, 0].astype(f32) * has_first
        total = total + second[0, place, 0].astype(f32) * has_second
        result[...] = total.astype(bf16)


def text_sums(flags, windows):
    count, kinds, _, slots, width = windows.shape
    bits = (count - 1).bit_length()

    def place_of(rank, odd):
        place = 0
        for even_bit, odd_bit in zip(*halving_orders(bits)):
            place = place * 2 + ((rank >> (even_bit + (odd_bit - even_bit) * odd)) & 1)
        return place

    def part(place):
        def index(item, flags):
            owner = jnp.clip(item - place, 0, count - 1)
            odd = flags[CORE]
            return (place_of(owner, odd) ^ place_of(flags[SEQ], odd), 0, place, 0, 0)

        return pl.BlockSpec((1, kinds, 1, slots, width), index)

    result = jax.ShapeDtypeStruct(((count + 1) * slots, width), bf16)
    return kernel_call(
        functools.partial(text_sums_kernel, count),
        prefetch=1,
        grid=(count + 1,),
        in_specs=[part(0), part(1)],
        out_specs=[pl.BlockSpec((slots, width), lambda item, flags: (item, 0))] * 2,
        out_shape=[result, result],
        compiler_params=small,
        cost_estimate=cost(LIGHT * 2),
        name="text_sums",
    )(flags, windows, windows)


def per_device(
    tokens,
    item_ids,
    text_states,
    text_lengths,
    norm_gain,
    norm_shift,
    w_self,
    b_self,
    w_self_out,
    w_cross_q,
    w_cross_kv,
    b_cross,
    w_cross_out,
    w_up,
    b_up,
    w_down,
    out_bias,
    d_out,
):
    row_count = tokens.shape[0]
    assert row_count == ITEM_LEN and lax.axis_size("tensor") == 4
    local_width = w_self.shape[2]
    seq_rank = lax.axis_index("seq")
    tensor_rank = lax.axis_index("tensor")
    quarter = quarter_of(tensor_rank)
    item_total, slot_count = text_states.shape[:2]
    slot_total = item_total * slot_count
    cut = jnp.sum((item_ids == 0).astype(jnp.int32))
    item_lengths = lax.dynamic_slice_in_dim(text_lengths, seq_rank, 2)
    flags = jnp.stack(
        (
            cut,
            (seq_rank > 0).astype(jnp.int32),
            item_lengths[0],
            item_lengths[1],
            quarter,
            tensor_rank & 1,
            seq_rank,
        )
    )
    chunks = range(CHUNKS)
    halving_sum = HalvingSum()

    def local_cols(full_rows):
        return lax.dynamic_slice_in_dim(full_rows, tensor_rank * local_width, local_width, axis=1)

    def token_sum(rows_in):
        return jnp.sum(rows_in.astype(f32), axis=0)

    order = Order()
    gains, shifts, biases = norm_gain, norm_shift, out_bias
    inputs_one, both = order.kernel(enter, tokens, w_self, b_self, gains, shifts)
    both_far = shifted(both, "seq", 1)
    late = tied((w_self_out, w_cross_out), both)
    crossing = [swapped(late[0], "tensor", 2), swapped(late[1], "tensor", 2)]
    queries, top, total, acc = order.kernel(
        own_attend, flags, inputs_one, w_self, b_self, both
    )

    text_flat = text_states.reshape(slot_total, text_states.shape[2])
    text_window = lax.dynamic_slice_in_dim(text_flat, seq_rank * slot_count, 2 * slot_count, 0)

    def project_text(window, key_weight, value_weight, bias):
        text_keys = matmul_low(window, key_weight).astype(bf16)
        return text_keys, (matmul_low(window, value_weight) + bias.astype(f32)).astype(bf16)

    text_keys, text_values = order(
        project_text, text_window, w_cross_kv[0], w_cross_kv[1], b_cross[1]
    )
    grad_hidden = order(
        lambda grad, weight: times_transpose(grad, weight).astype(bf16), d_out, w_down
    )
    attended, log_total, after_one, inputs_two, cross_queries, cross_attended, cross_log = (
        [] for _ in range(7)
    )
    operands = (flags, queries, both_far, top, total, acc)
    first = order.kernel(functools.partial(far_attend, 0), *operands)
    across = [swapped(first[0], "tensor", 2)]
    second, across = order.kernel(functools.partial(far_attend, 1), *operands, during=across)
    attended, log_total = zip(first, second)
    across = [*across, swapped(attended[1], "tensor", 2)]
    crossing = tied(crossing, attended[-1])
    self_out, cross_out = (
        [own, swapped(own, "tensor", 1), across, swapped(across, "tensor", 1)]
        for own, across in zip(late, crossing)
    )
    after_one, inputs_two, cross_queries, cross_attended, cross_log = ([] for _ in range(5))

    def keep(made, *lists):
        for held, part in zip(lists, made):
            held.append(part)

    def run_after_self(chunk, across, during):
        return order.kernel(
            lambda *operands: after_self(
                chunk, *operands[:2], operands[2:6], operands[6:10], *operands[10:]
            ),
            flags,
            tokens,
            *gathered(attended[chunk], across),
            *self_out,
            biases,
            gains,
            shifts,
            w_cross_q,
            b_cross,
            text_keys,
            text_values,
            during=during,
        )

    made, (across_next,) = run_after_self(0, across[0], [across[1]])
    keep(made, after_one, inputs_two, cross_queries, cross_attended, cross_log)
    across = swapped(cross_attended[0], "tensor", 2)
    made, (across,) = run_after_self(1, across_next, [across])
    keep(made, after_one, inputs_two, cross_queries, cross_attended, cross_log)
    across_next = swapped(cross_attended[1], "tensor", 2)

    def low_rows(left, right):
        return contract_rows(left, right).astype(bf16)

    def products(*operands):
        return jnp.concatenate(
            [low_rows(left, right) for left, right in zip(operands[::2], operands[1::2])]
        )

    def scatter_first(chunk_halves):
        arrived = swapped(chunk_halves[0], "tensor", 1)
        kept, other = order.kernel(first_add, flags, arrived, chunk_halves[1])
        return kept, swapped(other, "tensor", 2)

    ready = {}

    def advance(*lanes):
        for lane in lanes:
            step, state, run = next(lane, (None, None, None))
            if step is not None:
                ready[id(lane)] = run(step, state["held"], state["arrived"])

    def begun(lane):
        first = next(lane)

        def rest():
            yield first
            yield from lane

        return rest()

    def run_after_cross(chunk, across, wholes, during):
        return order.kernel(
            lambda *operands: after_cross(
                chunk, *operands[:2], operands[2:6], operands[6:10], *operands[10:16], operands[16:]
            ),
            flags,
            after_one[chunk],
            *gathered(cross_attended[chunk], across),
            *cross_out,
            grad_hidden,
            w_up,
            b_up[None],
            biases,
            gains,
            shifts,
            *wholes,
            during=during,
        )

    made, (across,) = run_after_cross(0, across, (), [across_next])
    after_two = [made[0]]
    late_across = swapped(tied(w_cross_q, across), "tensor", 2)
    kept, other = scatter_first(made[4:])
    made, (other, late_across) = run_after_cross(1, across, made[1:4], [other, late_across])
    after_two.append(made[0])
    inputs_three, hidden, grad_pre = made[1:4]
    all_cross_q = gathered(w_cross_q, late_across)
    kept_next, other_next = scatter_first(made[4:])

    def norm_step(chunk, kept, other):
        return order.kernel(
            functools.partial(norm_back_rows, chunk, 2),
            flags,
            kept,
            other,
            after_two[chunk],
            d_out,
            gains,
        )

    shard, sums = norm_step(0, kept, other)
    shards, shard_sums_three = [shard], [sums]
    across = swapped(shard, "tensor", 2)
    mlp_grads, (other_next,) = order(
        products, hidden, d_out, inputs_three, grad_pre, during=[other_next]
    )
    mlp_shard = lax.psum_scatter(mlp_grads, "seq", scatter_dimension=0, tiled=True)
    shard, sums = norm_step(1, kept_next, other_next)
    shards.append(shard)
    shard_sums_three.append(sums)
    across_next = swapped(shard, "tensor", 2)

    def run_cross_back(chunk, across, during):
        return order.kernel(
            lambda *operands: cross_back(chunk, operands[0], operands[1:5], *operands[5:]),
            flags,
            *gathered(shards[chunk], across),
            w_cross_out,
            cross_queries[chunk],
            cross_attended[chunk],
            cross_log[chunk],
            text_keys,
            text_values,
            during=during,
        )

    grad_cross_low, grad_cross_q, text_key_parts, text_value_parts = ([] for _ in range(4))
    made, (across,) = run_cross_back(0, across, [across_next])
    keep(made, grad_cross_low, grad_cross_q, text_key_parts, text_value_parts)
    across_next = swapped(grad_cross_q[0], "tensor", 2)
    made, (across,) = run_cross_back(1, across, [across_next])
    keep(made, grad_cross_low, grad_cross_q, text_key_parts, text_value_parts)
    across_next = swapped(grad_cross_q[1], "tensor", 2)

    def text_windows(*parts):
        both = jnp.stack((sum(parts[:CHUNKS]), sum(parts[CHUNKS:]))).astype(bf16)
        return both.reshape(1, 2, 2, slot_count, local_width)

    text_lane = order(text_windows, *text_key_parts, *text_value_parts)
    text_lane = begun(halving_sum.gathers(order, text_lane))

    def output_product(chunk, source, weight):
        return split_product(chunk, flags, (source,), (weight,), False)

    first_output, (across_next,) = order.kernel(
        functools.partial(output_product, 0), hidden, w_down, during=[across_next]
    )

    def run_back_to_self(chunk, across, wholes, during=()):
        return order.kernel(
            lambda *operands: back_to_self(
                chunk, operands[:4], operands[4:8], *operands[8:11], operands[11:]
            ),
            *gathered(grad_cross_q[chunk], across),
            *all_cross_q,
            after_one[chunk],
            grad_cross_low[chunk],
            gains,
            *wholes,
            during=during,
        )

    whole, sums = run_back_to_self(0, across, ())
    row_sums = [sums]
    grad_self_low, sums = run_back_to_self(1, across_next, (whole,))
    row_sums.append(sums)
    advance(text_lane)

    def joined(*parts):
        return [jnp.concatenate(parts[k : k + CHUNKS]) for k in range(0, len(parts), CHUNKS)]

    attended, log_rows = order(
        lambda *parts: joined(*parts[:CHUNKS]) + [jnp.concatenate(parts[CHUNKS:], axis=1)],
        *attended,
        *log_total,
    )
    grad_att, inner, grad_q, grad_far = order.kernel(
        far_back, flags, grad_self_low, w_self_out, queries, attended, log_rows, both_far
    )
    carried = shifted(grad_far, "seq", -1)
    advance(text_lane)
    (grad_queries, grad_keys, grad_values), (mlp_shard,) = order.kernel(
        own_back,
        flags,
        grad_att,
        inner,
        queries,
        log_rows,
        both,
        grad_q,
        during=[mlp_shard],
    )
    mlp_sums = lax.all_gather(mlp_shard, "seq", tiled=True)
    joins = order(joined, *grad_cross_q, *inputs_two, *cross_attended, *grad_cross_low)
    cross_grads = order(products, *joins, attended, grad_self_low)
    advance(text_lane)

    def add_carried(grad_keys, grad_values, carried):
        return (
            (grad_keys + carried[:, :local_width].astype(f32)).astype(bf16),
            (grad_values + carried[:, local_width:].astype(f32)).astype(bf16),
        )

    grad_keys, grad_values = order(add_carried, grad_keys, grad_values, carried)

    def self_products(inputs, *grads):
        return jnp.concatenate([low_rows(inputs, grad) for grad in grads], axis=1)

    self_grads = order(self_products, inputs_one, grad_queries, grad_keys, grad_values)
    self_lane = begun(halving_sum.steps(order, self_grads, 3))

    def token_product(chunk, *operands):
        return split_product(chunk, flags, operands[:3], operands[3:], True)

    token_terms = []
    for chunk in chunks:
        made = order.kernel(
            functools.partial(token_product, chunk),
            grad_queries,
            grad_keys,
            grad_values,
            w_self,
            w_self,
            w_self,
        )
        token_terms.append(scatter_first(made))
    for _ in range(axis_bits("seq")):
        advance(text_lane)
    grad_text_keys, grad_text_values = order.kernel(
        functools.partial(text_sums, flags), ready[id(text_lane)]
    )

    def text_grads(grad_text_keys, grad_text_values):
        part = times_transpose(grad_text_keys, w_cross_kv[0]) + times_transpose(
            grad_text_values, w_cross_kv[1]
        )
        return part.astype(bf16)

    grad_text_part, others = order(
        text_grads,
        grad_text_keys,
        grad_text_values,
        during=[other for _, other in token_terms],
    )
    shard_sums_one, token_shards = [], []
    for chunk in chunks:
        shard, sums = order.kernel(
            functools.partial(norm_back_rows, chunk, 0),
            flags,
            token_terms[chunk][0],
            others[chunk],
            tokens,
            grad_self_low,
            gains,
        )
        shard_sums_one.append(sums)
        token_shards.append(shard)
    token_across = [swapped(shard, "tensor", 2) for shard in token_shards]
    grad_text_shard = scatter_rows(grad_text_part, "tensor").astype(bf16)
    advance(self_lane)

    def norm_sums(*parts):
        return jnp.concatenate((sum(parts[:CHUNKS])[:2], sum(parts[CHUNKS:])[:2]))

    shard_sums = order(norm_sums, *shard_sums_one, *shard_sums_three)
    shard_sums = scatter_columns(shard_sums, "tensor")
    second_output, token_across = order.kernel(
        functools.partial(output_product, 1), hidden, w_down, during=token_across
    )
    output_terms = [scatter_first(first_output), scatter_first(second_output)]
    advance(self_lane)

    def vector_rows(cross_grads, shard_sums, d_out, cross_q, queries, values, pre, *row_sums):
        rows = local_cols(sum(row_sums)[:4])
        vectors = jnp.concatenate(
            (
                shard_sums[:1],
                rows[:1],
                shard_sums[2:3],
                shard_sums[1:2],
                rows[1:2],
                shard_sums[3:],
                rows[2:],
                jnp.stack(
                    (
                        token_sum(local_cols(d_out)),
                        token_sum(cross_q),
                        token_sum(queries),
                        token_sum(values),
                    )
                ),
                token_sum(pre).reshape(-1, local_width),
            )
        )
        vectors = vectors.astype(bf16).reshape(-1, cross_grads.shape[1])
        spare = jnp.zeros((PAD - vectors.shape[0], cross_grads.shape[1]), bf16)
        return jnp.concatenate((cross_grads, vectors, spare))

    cross_grads = order(
        vector_rows,
        cross_grads,
        shard_sums,
        d_out,
        joins[0],
        grad_queries,
        grad_values,
        grad_pre,
        *row_sums,
    )
    cross_lane = begun(halving_sum.steps(order, cross_grads, stacked=4, turned=1))
    advance(self_lane)
    grad_text_shard = tied(grad_text_shard, order.pending)
    grad_text_across = swapped(grad_text_shard, "tensor", 2)

    def output_shard(kept, other, rows_in):
        rows = kept.shape[0]
        base = lax.dynamic_slice_in_dim(rows_in, quarter * rows, rows, 0)
        return (base + ((kept + other.astype(f32)) + biases[2].astype(f32))).astype(bf16)

    output_shards = [
        order(output_shard, *output_terms[chunk], after_two[chunk]) for chunk in chunks
    ]
    output_across = [swapped(shard, "tensor", 2) for shard in output_shards]
    pieces = [gathered(token_shards[chunk], token_across[chunk]) for chunk in chunks]
    advance(cross_lane)
    def wide_sums(sums):
        half = sums.shape[0] // 2
        return [sums[:half].astype(f32), sums[half:].astype(f32)]

    sum_w_down, sum_w_up = order(wide_sums, mlp_sums)
    grad_tokens = order.kernel(
        lambda *pieces: place_quarters(flags, (pieces[:4], pieces[4:]), f32), *pieces[0], *pieces[1]
    )
    advance(self_lane, cross_lane)
    grad_w_cross_kv, output_across = order(
        lambda *operands: jnp.stack(
            (contract_rows(operands[0], operands[1]), contract_rows(operands[0], operands[2]))
        ),
        text_flat,
        grad_text_keys,
        grad_text_values,
        during=output_across,
    )
    grad_value_bias = token_sum(grad_text_values)
    advance(self_lane, cross_lane)
    pieces = [gathered(output_shards[chunk], output_across[chunk]) for chunk in chunks]
    output_rows = order.kernel(
        lambda *pieces: place_quarters(flags, (pieces[:4], pieces[4:]), bf16), *pieces[0], *pieces[1]
    )
    advance(self_lane, cross_lane)

    advance(cross_lane)
    grad_text = order.kernel(
        lambda *pieces: place_quarters(flags, (pieces,), f32),
        *gathered(grad_text_shard, grad_text_across),
    )
    grad_text = grad_text.reshape(text_states.shape)
    for _ in range(4 * axis_bits("seq") + 4):
        advance(self_lane, cross_lane)
    (grad_w_self,), cross_grads = ready[id(self_lane)], ready[id(cross_lane)]
    vectors = cross_grads[3][:STAT].reshape(-1, local_width)
    grad_b_cross = jnp.stack((vectors[9], grad_value_bias))
    return (
        output_rows,
        grad_tokens,
        grad_text,
        vectors[:3],
        vectors[3:6],
        grad_w_self,
        vectors[10:12],
        cross_grads[2],
        cross_grads[0],
        grad_w_cross_kv,
        grad_b_cross,
        cross_grads[1],
        sum_w_up,
        vectors[12 : 12 + w_up.shape[1] // local_width].reshape(-1),
        sum_w_down,
        vectors[6:9],
    )


def solution(mesh):
    placed = (
        P("seq", None),
        P(),
        P(),
        P(),
        P(),
        P(),
        P(None, None, "tensor"),
        P(None, "tensor"),
        P("tensor", None),
        P(None, "tensor"),
        P(None, None, "tensor"),
        P(None, "tensor"),
        P("tensor", None),
        P(None, "tensor"),
        P("tensor"),
        P("tensor", None),
        P(),
        P("seq", None),
    )
    return jax.shard_map(
        per_device,
        mesh=mesh,
        in_specs=placed,
        out_specs=(
            P("seq", None),
            P("seq", None),
            P(),
            P(None, "tensor"),
            P(None, "tensor"),
            P(None, None, "tensor"),
            P(None, "tensor"),
            P("tensor", None),
            P(None, "tensor"),
            P(None, None, "tensor"),
            P(None, "tensor"),
            P("tensor", None),
            P(None, "tensor"),
            P("tensor"),
            P("tensor", None),
            P(None, "tensor"),
        ),
        check_vma=False,
    )
```

```python
import functools

import jax
import jax.numpy as jnp
from jax import lax
from jax.experimental import pallas as pl
from jax.experimental.pallas import tpu as pltpu
from jax.sharding import PartitionSpec as P

HEAD_SIZE = 64
ITEM_LEN = 1024
TILE = 256
STAT = 8
CHUNKS = 2
PAD = 256


epsilon = 1e-05
masked_fill = -1e30
f32, bf16 = jnp.float32, jnp.bfloat16
CUT, HAS_FAR, LENGTH, QUARTER, CORE, SEQ = 0, 1, 2, 4, 5, 6


def shifted(value, axis, steps):
    count = lax.axis_size(axis)
    leading, last = (max(0, -steps), min(count, count - steps))
    return lax.ppermute(value, axis, [(source, source + steps) for source in range(leading, last)])


def matmul_low(left, right):
    return jnp.dot(left, right, preferred_element_type=jnp.float32)


def contract_rows(left, right):
    return jnp.einsum("ra,rb->ab", left, right, preferred_element_type=jnp.float32)


def times_transpose(left, right):
    return jnp.einsum("ra,ba->rb", left, right, preferred_element_type=jnp.float32)


def norm_back(grad_normed, normal, inv_scale, gain):
    grad_normal = grad_normed * gain
    grad_mean = jnp.mean(grad_normal, axis=-1, keepdims=True)
    proj_mean = jnp.mean(grad_normal * normal, axis=-1, keepdims=True)
    return inv_scale * (grad_normal - grad_mean - normal * proj_mean)


def swapped(value, axis, distance):
    count = lax.axis_size(axis)
    return lax.ppermute(value, axis, [(source, source ^ distance) for source in range(count)])


def tied(value, *others):
    return lax.optimization_barrier((value, others))[0]


class Order:
    def __init__(self):
        self.pending = []

    def finish(self, result, during):
        self.pending = jax.tree.leaves(result)[-1:]
        if not during:
            return result
        return lax.optimization_barrier((result, tuple(during)))

    def __call__(self, step, *operands, during=()):
        operands, pending = lax.optimization_barrier((operands, self.pending))
        result = self.finish(step(*operands), during)
        self.pending = pending + self.pending
        return result

    def kernel(self, step, *operands, during=()):
        current.append(self)
        result = step(*operands)
        current.pop()
        return self.finish(result, during)


current = []


def kernel_call(kernel, prefetch=0, grid=(), in_specs=(), out_specs=None, scratch_shapes=(), **options):
    def run(*operands):
        order = current[-1] if current else None
        waits = order.pending if order else []
        count = len(operands)

        def body(*refs):
            kernel(*refs[:count], *refs[count + len(waits) :])

        result = pl.pallas_call(
            body,
            grid_spec=pltpu.PrefetchScalarGridSpec(
                num_scalar_prefetch=prefetch,
                grid=grid,
                in_specs=list(in_specs) + [pl.BlockSpec(memory_space=pl.ANY)] * len(waits),
                out_specs=out_specs,
                scratch_shapes=list(scratch_shapes),
            ),
            **options,
        )(*operands, *waits)
        return result

    return run


def axis_bits(axis):
    return (lax.axis_size(axis) - 1).bit_length()


def gather_relative(block, axis):
    blocks = {0: block}
    for bit in reversed(range(axis_bits(axis))):
        blocks.update(
            {d ^ (1 << bit): swapped(held, axis, 1 << bit) for d, held in list(blocks.items())}
        )
    return [blocks[d] for d in range(len(blocks))]


def gathered(block, across):
    return [block, swapped(block, "tensor", 1), across, swapped(across, "tensor", 1)]


def rank_bit(axis, bit):
    return (lax.axis_index(axis) >> bit) & 1


def shard_offset(axis, row_count):
    offset = 0
    for bit in range(axis_bits(axis)):
        offset = offset + rank_bit(axis, bit) * (row_count >> (bit + 1))
    return offset


def scatter_rows(partial_rows, axis):
    held = partial_rows
    for bit in range(axis_bits(axis)):
        half = held.shape[0] // 2
        mine = rank_bit(axis, bit)
        sent = lax.dynamic_slice_in_dim(held, (1 - mine) * half, half, 0)
        kept = lax.dynamic_slice_in_dim(held, mine * half, half, 0)
        arrived = swapped(sent, axis, 1 << bit)
        held = kept.astype(jnp.float32) + arrived.astype(jnp.float32)
        if bit + 1 < axis_bits(axis):
            held = held.astype(jnp.bfloat16)
    return held


def scatter_columns(partial, axis):
    held = partial
    for bit in reversed(range(axis_bits(axis))):
        half = held.shape[1] // 2
        mine = rank_bit(axis, bit)
        sent = lax.dynamic_slice_in_dim(held, (1 - mine) * half, half, 1)
        kept = lax.dynamic_slice_in_dim(held, mine * half, half, 1)
        held = kept + swapped(sent, axis, 1 << bit)
    return held


def butterfly_sum(value, axis):
    for bit in range(axis_bits(axis)):
        value = value + swapped(value, axis, 1 << bit)
    return value


def nn(left, right):
    return lax.dot_general(left, right, (((1,), (0,)), ((), ())), preferred_element_type=f32)


def nt(left, right):
    return lax.dot_general(left, right, (((1,), (1,)), ((), ())), preferred_element_type=f32)


def tile_rows(index):
    return pl.ds(pl.multiple_of(index * TILE, TILE), TILE)


def head_rows(head):
    return pl.ds(head * HEAD_SIZE, HEAD_SIZE)


def row_of(ref, row):
    return ref[...].astype(f32)[row : row + 1]


def turn(block):
    return jnp.transpose(block.astype(f32))


def by_head(turned, store):
    row_head = lax.broadcasted_iota(jnp.int32, turned.shape, 0) // HEAD_SIZE
    for head in range(store.shape[0]):
        store[head] = jnp.where(row_head == head, turned, 0.0).astype(store.dtype)


def tile_places(query_tile, key_tile):
    query_at = query_tile * TILE + lax.broadcasted_iota(jnp.int32, (1, TILE), 1)
    key_at = key_tile * TILE + lax.broadcasted_iota(jnp.int32, (TILE, 1), 0)
    return query_at, key_at


def own_mask(query_tile, cut):
    def allowed(key_tile):
        query_at, key_at = tile_places(query_tile, key_tile)
        first_key = jnp.where(query_at >= cut, cut, 0)
        return (key_at <= query_at) & (key_at >= first_key)

    return allowed


def far_mask(query_tile, cut):
    def allowed(key_tile):
        query_at, key_at = tile_places(query_tile, key_tile)
        first_key = jnp.where(query_at < cut, cut, TILE * 1024)
        return key_at >= first_key

    return allowed


def text_mask(query_tile, cut, lengths, slots):
    def allowed(key_tile):
        query_at, key_at = tile_places(query_tile, key_tile)
        first_key = jnp.where(query_at < cut, 0, slots)
        last_key = jnp.where(query_at < cut, lengths[0], slots + lengths[1])
        return (key_at >= first_key) & (key_at < last_key)

    return allowed


def own_tiles(query_tile, cut):
    return jnp.where(query_tile * TILE >= cut, cut // TILE, 0), query_tile + 1


def far_tiles(query_tile, cut, has_far, tiles):
    live = (query_tile * TILE < cut) & (has_far > 0)
    return cut // TILE, jnp.where(live, tiles, 0)


def attend_tiles(first, last, mask, key_ref, value_turned, query_heads, top, total, acc):
    heads = query_heads.shape[0]

    def step(key_tile, carry):
        allowed = mask(key_tile)
        keys = key_ref[tile_rows(key_tile), :]
        scores = [
            jnp.where(allowed, nn(keys, query_heads[head]), masked_fill) for head in range(heads)
        ]
        old_top = [top[pl.ds(head, 1), :] for head in range(heads)]
        new_top = [
            jnp.maximum(old, jnp.max(part, axis=0, keepdims=True))
            for old, part in zip(old_top, scores)
        ]
        weights = [jnp.exp(part - new) for part, new in zip(scores, new_top)]
        factors = [jnp.exp(old - new) for old, new in zip(old_top, new_top)]
        sums = [jnp.sum(part, axis=0, keepdims=True) for part in weights]
        values = [
            nn(value_turned[head_rows(head), tile_rows(key_tile)], weights[head].astype(bf16))
            for head in range(heads)
        ]
        for head in range(heads):
            row = pl.ds(head, 1)
            top[row, :] = new_top[head]
            total[row, :] = total[row, :] * factors[head] + sums[head]
            acc[head_rows(head), :] = acc[head_rows(head), :] * factors[head] + values[head]
        return carry

    lax.fori_loop(first, last, step, 0)


def turn_all(source, target):
    for tile in range(source.shape[0] // TILE):
        rows = pl.ds(tile * TILE, TILE)
        target[:, rows] = turn(source[rows, :]).astype(target.dtype)


def own_attend_kernel(flags, inputs, weight, bias, keys, values, queries, top, total, acc, value_turned, query_heads):
    tile = pl.program_id(0)
    cut = flags[0]

    @pl.when(tile == 0)
    def _():
        turn_all(values, value_turned)

    made = (nn(inputs[...], weight[...]) + row_of(bias, 0)).astype(bf16)
    made = made.astype(f32) * HEAD_SIZE**-0.5
    queries[...] = made.astype(bf16)
    by_head(jnp.transpose(made), query_heads)
    top[...] = jnp.full(top.shape, masked_fill, f32)
    total[...] = jnp.zeros(total.shape, f32)
    acc[...] = jnp.zeros(acc.shape, f32)
    first, last = own_tiles(tile, cut)
    attend_tiles(first, last, own_mask(tile, cut), keys, value_turned, query_heads, top, total, acc)


def far_attend_kernel(base, flags, queries, keys, values, top_in, total_in, acc_in, attended, log_total, value_turned, query_heads, top, total, acc):
    tile = base + pl.program_id(0)
    cut = flags[0]

    @pl.when(pl.program_id(0) == 0)
    def _():
        turn_all(values, value_turned)

    by_head(turn(queries[...]), query_heads)
    top[...] = top_in[...]
    total[...] = total_in[...]
    acc[...] = acc_in[...]
    first, last = far_tiles(tile, cut, flags[1], keys.shape[0] // TILE)
    attend_tiles(first, last, far_mask(tile, cut), keys, value_turned, query_heads, top, total, acc)
    log_total[...] = top[...] + jnp.log(total[...])
    for head in range(query_heads.shape[0]):
        acc[head_rows(head), :] = acc[head_rows(head), :] / total[pl.ds(head, 1), :]
    attended[...] = jnp.transpose(acc[...]).astype(bf16)


def spec_rows(width, base=0):
    return pl.BlockSpec((TILE, width), lambda tile: (base + tile, 0))


def spec_columns(height, base=0):
    return pl.BlockSpec((height, TILE), lambda tile: (0, base + tile))


def spec_layer(layer, rows, width):
    return pl.BlockSpec((None, rows, width), lambda tile: (layer, 0, 0))


def spec_side(side, rows, width):
    return pl.BlockSpec((rows, width), lambda tile: (0, side))


def spec_whole(*shape):
    return pl.BlockSpec(shape, lambda tile: (0,) * len(shape))


SMEM = pl.BlockSpec(memory_space=pltpu.SMEM)
params = pltpu.CompilerParams(vmem_limit_bytes=48 * 2**20)
small = pltpu.CompilerParams(vmem_limit_bytes=16 * 2**20)


LIGHT = 0.1


def cost(us):
    return pl.CostEstimate(
        flops=int(us * 1.15e9), bytes_accessed=int(us * 3.6e6), transcendentals=0
    )


def own_attend(flags, inputs, weight, bias, both):
    rows, width = both.shape[0], both.shape[1] // 2
    depth = inputs.shape[1]
    heads = width // HEAD_SIZE
    return kernel_call(
        own_attend_kernel,
        grid=(rows // TILE,),
        in_specs=[SMEM, spec_rows(depth), spec_layer(0, depth, width), spec_whole(*bias.shape), spec_side(0, rows, width), spec_side(1, rows, width)],
        out_specs=[spec_rows(width), spec_columns(STAT), spec_columns(STAT), spec_columns(width)],
        out_shape=[
            jax.ShapeDtypeStruct((rows, width), bf16),
            jax.ShapeDtypeStruct((STAT, rows), f32),
            jax.ShapeDtypeStruct((STAT, rows), f32),
            jax.ShapeDtypeStruct((width, rows), f32),
        ],
        scratch_shapes=[pltpu.VMEM((width, rows), bf16), pltpu.VMEM((heads, width, TILE), bf16)],
        compiler_params=params,
        cost_estimate=cost(LIGHT * 16),
        name="own_attend",
    )(flags, inputs, weight, bias, both, both)


def far_attend(chunk, flags, queries, both, top, total, acc):
    rows, width = both.shape[0], both.shape[1] // 2
    heads = width // HEAD_SIZE
    tiles = rows // CHUNKS // TILE
    base = chunk * tiles
    return kernel_call(
        functools.partial(far_attend_kernel, base),
        grid=(tiles,),
        in_specs=[
            SMEM,
            spec_rows(width, base),
            spec_side(0, rows, width),
            spec_side(1, rows, width),
            spec_columns(STAT, base),
            spec_columns(STAT, base),
            spec_columns(width, base),
        ],
        out_specs=[spec_rows(width), spec_columns(STAT)],
        out_shape=[
            jax.ShapeDtypeStruct((tiles * TILE, width), bf16),
            jax.ShapeDtypeStruct((STAT, tiles * TILE), f32),
        ],
        scratch_shapes=[
            pltpu.VMEM((width, rows), bf16),
            pltpu.VMEM((heads, width, TILE), bf16),
            pltpu.VMEM((STAT, TILE), f32),
            pltpu.VMEM((STAT, TILE), f32),
            pltpu.VMEM((width, TILE), f32),
        ],
        compiler_params=params,
        cost_estimate=cost(LIGHT * 4),
        name="far_attend",
    )(flags, queries, both, both, top, total, acc)


def back_tiles(first, last, mask, refs, stats):
    keys, values, key_turned, query_heads, grad_heads, grad_turned, query_turned, gq, gk, gv = refs
    log_total, inner = stats
    heads = query_heads.shape[0]

    def step(key_tile, carry):
        allowed = mask(key_tile)
        place = tile_rows(key_tile)
        key_block = keys[place, :]
        value_block = values[place, :]
        scores = [nn(key_block, query_heads[head]) for head in range(heads)]
        grad_probs = [nn(value_block, grad_heads[head]) for head in range(heads)]
        probs = [
            jnp.exp(jnp.where(allowed, scores[head], masked_fill) - log_total[pl.ds(head, 1), :])
            for head in range(heads)
        ]
        grad_scores = [
            (probs[head] * (grad_probs[head] - inner[pl.ds(head, 1), :])).astype(bf16)
            for head in range(heads)
        ]
        for head in range(heads):
            rows = head_rows(head)
            gv[rows, place] += nt(grad_turned[rows, :], probs[head].astype(bf16))
            gk[rows, place] += nt(query_turned[rows, :], grad_scores[head])
            gq[rows, :] += nn(key_turned[rows, place], grad_scores[head])
        return carry

    lax.fori_loop(first, last, step, 0)


def far_back_kernel(flags, grad_rows, weight, queries, attended, log_total, keys, values, grad_att, inner, grad_q, grad_both, key_turned, query_heads, grad_heads, query_turned, grad_turned, gk, gv):
    tile = pl.program_id(0)
    cut = flags[0]

    @pl.when(tile == 0)
    def _():
        turn_all(keys, key_turned)
        gk[...] = jnp.zeros(gk.shape, f32)
        gv[...] = jnp.zeros(gv.shape, f32)

    made = nt(grad_rows[...], weight[...]).astype(bf16)
    grad_att[...] = made
    turned = turn(made)
    by_head(turned, grad_heads)
    grad_turned[...] = turned.astype(bf16)
    product = turned * turn(attended[...])
    inner[...] = jnp.zeros(inner.shape, f32)
    for head in range(query_heads.shape[0]):
        inner[pl.ds(head, 1), :] = jnp.sum(product[head * HEAD_SIZE : (head + 1) * HEAD_SIZE], axis=0, keepdims=True)
    turned = turn(queries[...])
    by_head(turned, query_heads)
    query_turned[...] = turned.astype(bf16)
    grad_q[...] = jnp.zeros(grad_q.shape, f32)
    first, last = far_tiles(tile, cut, flags[1], keys.shape[0] // TILE)
    refs = (keys, values, key_turned, query_heads, grad_heads, grad_turned, query_turned, grad_q, gk, gv)
    back_tiles(first, last, far_mask(tile, cut), refs, (log_total, inner))

    @pl.when(tile == pl.num_programs(0) - 1)
    def _():
        for part in range(keys.shape[0] // TILE):
            rows = pl.ds(part * TILE, TILE)
            width = gk.shape[0]
            grad_both[rows, :width] = jnp.transpose(gk[:, rows]).astype(bf16)
            grad_both[rows, width:] = jnp.transpose(gv[:, rows]).astype(bf16)


def far_back(flags, grad_rows, weight, queries, attended, log_total, both):
    rows, width = both.shape[0], both.shape[1] // 2
    depth = grad_rows.shape[1]
    heads = width // HEAD_SIZE
    return kernel_call(
        far_back_kernel,
        grid=(rows // TILE,),
        in_specs=[SMEM, spec_rows(depth), spec_whole(width, depth), spec_rows(width), spec_rows(width), spec_columns(STAT), spec_side(0, rows, width), spec_side(1, rows, width)],
        out_specs=[spec_rows(width), spec_columns(STAT), spec_columns(width), spec_whole(rows, 2 * width)],
        out_shape=[
            jax.ShapeDtypeStruct((rows, width), bf16),
            jax.ShapeDtypeStruct((STAT, rows), f32),
            jax.ShapeDtypeStruct((width, rows), f32),
            jax.ShapeDtypeStruct((rows, 2 * width), bf16),
        ],
        scratch_shapes=[
            pltpu.VMEM((width, rows), bf16),
            pltpu.VMEM((heads, width, TILE), bf16),
            pltpu.VMEM((heads, width, TILE), bf16),
            pltpu.VMEM((width, TILE), bf16),
            pltpu.VMEM((width, TILE), bf16),
            pltpu.VMEM((width, rows), f32),
            pltpu.VMEM((width, rows), f32),
        ],
        compiler_params=params,
        cost_estimate=cost(LIGHT * 9),
        name="far_back",
    )(flags, grad_rows, weight, queries, attended, log_total, both, both)


def own_back_kernel(flags, grad_att, inner, queries, log_total, keys, values, grad_q_in, grad_q, grad_k, grad_v, key_turned, query_heads, grad_heads, query_turned, grad_turned, gq, gk, gv):
    tile = pl.program_id(0)
    cut = flags[0]

    @pl.when(tile == 0)
    def _():
        turn_all(keys, key_turned)
        gk[...] = jnp.zeros(gk.shape, f32)
        gv[...] = jnp.zeros(gv.shape, f32)

    turned = turn(grad_att[...])
    by_head(turned, grad_heads)
    grad_turned[...] = turned.astype(bf16)
    turned = turn(queries[...])
    by_head(turned, query_heads)
    query_turned[...] = turned.astype(bf16)
    gq[...] = grad_q_in[...]
    first, last = own_tiles(tile, cut)
    refs = (keys, values, key_turned, query_heads, grad_heads, grad_turned, query_turned, gq, gk, gv)
    back_tiles(first, last, own_mask(tile, cut), refs, (log_total, inner))
    grad_q[...] = (jnp.transpose(gq[...]) * HEAD_SIZE**-0.5).astype(grad_q.dtype)

    @pl.when(tile == pl.num_programs(0) - 1)
    def _():
        for part in range(keys.shape[0] // TILE):
            rows = pl.ds(part * TILE, TILE)
            grad_k[rows, :] = jnp.transpose(gk[:, rows])
            grad_v[rows, :] = jnp.transpose(gv[:, rows])


def own_back(flags, grad_att, inner, queries, log_total, both, grad_q):
    rows, width = both.shape[0], both.shape[1] // 2
    heads = width // HEAD_SIZE
    return kernel_call(
        own_back_kernel,
        grid=(rows // TILE,),
        in_specs=[SMEM, spec_rows(width), spec_columns(STAT), spec_rows(width), spec_columns(STAT), spec_side(0, rows, width), spec_side(1, rows, width), spec_columns(width)],
        out_specs=[spec_rows(width), spec_whole(rows, width), spec_whole(rows, width)],
        out_shape=[
            jax.ShapeDtypeStruct((rows, width), bf16),
            jax.ShapeDtypeStruct((rows, width), f32),
            jax.ShapeDtypeStruct((rows, width), f32),
        ],
        scratch_shapes=[
            pltpu.VMEM((width, rows), bf16),
            pltpu.VMEM((heads, width, TILE), bf16),
            pltpu.VMEM((heads, width, TILE), bf16),
            pltpu.VMEM((width, TILE), bf16),
            pltpu.VMEM((width, TILE), bf16),
            pltpu.VMEM((width, TILE), f32),
            pltpu.VMEM((width, rows), f32),
            pltpu.VMEM((width, rows), f32),
        ],
        compiler_params=params,
        cost_estimate=cost(LIGHT * 16),
        name="own_back",
    )(flags, grad_att, inner, queries, log_total, both, both, grad_q)


def norm_parts(rows_in):
    row_mean = jnp.mean(rows_in, axis=-1, keepdims=True)
    centered = rows_in - row_mean
    inv_scale = lax.rsqrt(jnp.mean(centered * centered, axis=-1, keepdims=True) + epsilon)
    return centered * inv_scale, inv_scale


def enter_kernel(tokens, wk, wv, bias, gains, shifts, inputs, both):
    normal, _ = norm_parts(tokens[...].astype(f32))
    low = (normal * row_of(gains, 0) + row_of(shifts, 0)).astype(bf16)
    inputs[...] = low
    width = wk.shape[1]
    both[:, :width] = nn(low, wk[...]).astype(bf16)
    both[:, width:] = (nn(low, wv[...]) + row_of(bias, 1)).astype(bf16)


def enter(tokens, w_self, bias, gains, shifts):
    rows, depth = tokens.shape
    width = w_self.shape[2]
    return kernel_call(
        enter_kernel,
        grid=(rows // TILE,),
        in_specs=[
            spec_rows(depth),
            spec_layer(1, depth, width),
            spec_layer(2, depth, width),
            spec_whole(*bias.shape),
            spec_whole(*gains.shape),
            spec_whole(*shifts.shape),
        ],
        out_specs=[spec_rows(depth), spec_rows(2 * width)],
        out_shape=[
            jax.ShapeDtypeStruct((rows, depth), bf16),
            jax.ShapeDtypeStruct((rows, 2 * width), bf16),
        ],
        compiler_params=params,
        cost_estimate=cost(LIGHT * 4),
        name="enter",
    )(tokens, w_self, w_self, bias, gains, shifts)


def after_self_kernel(base, slots, flags, tokens, *refs):
    parts, weights, refs = refs[:4], refs[4:8], refs[8:]
    bias, gains, shifts, wq, bq, text_keys, text_values = refs[:7]
    after, inputs, queries, attended, log_total = refs[7:12]
    value_turned, query_heads, top, total, acc = refs[12:]
    tile = base + pl.program_id(0)

    @pl.when(pl.program_id(0) == 0)
    def _():
        turn_all(text_values, value_turned)

    product = nn(parts[0][...], weights[0][...])
    for part, weight in zip(parts[1:], weights[1:]):
        product = product + nn(part[...], weight[...])
    rows_in = tokens[...].astype(f32) + (product + row_of(bias, 0))
    after[...] = rows_in
    normal, _ = norm_parts(rows_in)
    low = (normal * row_of(gains, 1) + row_of(shifts, 1)).astype(bf16)
    inputs[...] = low
    made = (nn(low, wq[...]) + row_of(bq, 0)).astype(bf16).astype(f32) * HEAD_SIZE**-0.5
    queries[...] = made.astype(bf16)
    by_head(jnp.transpose(made), query_heads)
    top[...] = jnp.full(top.shape, masked_fill, f32)
    total[...] = jnp.zeros(total.shape, f32)
    acc[...] = jnp.zeros(acc.shape, f32)
    mask = text_mask(tile, flags[CUT], (flags[LENGTH], flags[LENGTH + 1]), slots)
    attend_tiles(0, 1, mask, text_keys, value_turned, query_heads, top, total, acc)
    log_total[...] = top[...] + jnp.log(total[...])
    for head in range(query_heads.shape[0]):
        acc[head_rows(head), :] = acc[head_rows(head), :] / total[pl.ds(head, 1), :]
    attended[...] = jnp.transpose(acc[...]).astype(bf16)


def after_self(chunk, flags, tokens, parts, weights, bias, gains, shifts, wq, bq, text_keys, text_values):
    rows, depth = tokens.shape
    width = wq.shape[1]
    heads = width // HEAD_SIZE
    window = text_keys.shape[0]
    assert window == TILE
    tiles = rows // CHUNKS // TILE
    base = chunk * tiles
    part_rows = tiles * TILE
    return kernel_call(
        functools.partial(after_self_kernel, base, window // 2),
        grid=(tiles,),
        in_specs=[SMEM, spec_rows(depth, base)]
        + [spec_rows(width)] * 4
        + [spec_whole(width, depth)] * 4
        + [spec_whole(*bias.shape)] * 3
        + [spec_whole(depth, width), spec_whole(*bq.shape)]
        + [spec_whole(window, width)] * 2,
        out_specs=[
            spec_rows(depth),
            spec_rows(depth),
            spec_rows(width),
            spec_rows(width),
            spec_columns(STAT),
        ],
        out_shape=[
            jax.ShapeDtypeStruct((part_rows, depth), f32),
            jax.ShapeDtypeStruct((part_rows, depth), bf16),
            jax.ShapeDtypeStruct((part_rows, width), bf16),
            jax.ShapeDtypeStruct((part_rows, width), bf16),
            jax.ShapeDtypeStruct((STAT, part_rows), f32),
        ],
        scratch_shapes=[
            pltpu.VMEM((width, window), bf16),
            pltpu.VMEM((heads, width, TILE), bf16),
            pltpu.VMEM((STAT, TILE), f32),
            pltpu.VMEM((STAT, TILE), f32),
            pltpu.VMEM((width, TILE), f32),
        ],
        compiler_params=params,
        cost_estimate=cost(LIGHT * 7),
        name="after_self",
    )(flags, tokens, *parts, *weights, bias, gains, shifts, wq, bq, text_keys, text_values)


def split_store(flags, tile, half_tiles, block, sent, kept):
    place = pl.ds(pl.multiple_of((tile % half_tiles) * TILE, TILE), TILE)
    own = tile // half_tiles == flags[CORE]

    @pl.when(own)
    def _():
        kept[place, :] = block

    @pl.when(jnp.logical_not(own))
    def _():
        sent[place, :] = block


def after_cross_kernel(half_tiles, flags, rows_ref, *refs):
    parts, weights, refs = refs[:4], refs[4:8], refs[8:]
    grad_hidden, w_up, b_up, bias, gains, shifts = refs[:6]
    after, inputs, hidden, grad_pre, sent, kept = refs[-6:]
    product = nn(parts[0][...], weights[0][...])
    for part, weight in zip(parts[1:], weights[1:]):
        product = product + nn(part[...], weight[...])
    rows_in = rows_ref[...] + (product + row_of(bias, 1))
    after[...] = rows_in
    normal, _ = norm_parts(rows_in)
    low = (normal * row_of(gains, 2) + row_of(shifts, 2)).astype(bf16)
    inputs[...] = low
    pre = nn(low, w_up[...]) + row_of(b_up, 0)
    square = pre * pre
    root = (2 / jnp.pi) ** 0.5
    bent = jnp.tanh(root * (pre + 0.044715 * (square * pre)))
    hidden[...] = (0.5 * pre * (1 + bent)).astype(bf16)
    slope = 0.5 * (1 + bent) + (0.5 * root) * pre * (1 - bent * bent) * (1 + 0.134145 * square)
    low_grad = (slope * grad_hidden[...].astype(f32)).astype(bf16)
    grad_pre[...] = low_grad
    block = nt(low_grad, w_up[...]).astype(bf16)
    split_store(flags, pl.program_id(0), half_tiles, block, sent, kept)


ANY = pl.BlockSpec(memory_space=pl.ANY)


def after_cross(chunk, flags, rows_in, parts, weights, grad_hidden, w_up, b_up, bias, gains, shifts, wholes):
    part_rows, depth = rows_in.shape
    width = parts[0].shape[1]
    units = w_up.shape[1]
    tiles = part_rows // TILE
    base = chunk * tiles
    rows = part_rows * CHUNKS
    operands = (flags, rows_in, *parts, *weights, grad_hidden, w_up, b_up, bias, gains, shifts)
    aliases = {len(operands) + place: 1 + place for place in range(len(wholes))}
    return kernel_call(
        functools.partial(after_cross_kernel, tiles // 2),
        grid=(tiles,),
        in_specs=[SMEM, spec_rows(depth)]
        + [spec_rows(width)] * 4
        + [spec_whole(width, depth)] * 4
        + [spec_rows(units, base), spec_whole(depth, units), spec_whole(1, units)]
        + [spec_whole(*bias.shape)] * 3
        + [ANY] * len(wholes),
        out_specs=[
            spec_rows(depth),
            spec_rows(depth, base),
            spec_rows(units, base),
            spec_rows(units, base),
            spec_whole(part_rows // 2, depth),
            spec_whole(part_rows // 2, depth),
        ],
        out_shape=[
            jax.ShapeDtypeStruct((part_rows, depth), f32),
            jax.ShapeDtypeStruct((rows, depth), bf16),
            jax.ShapeDtypeStruct((rows, units), bf16),
            jax.ShapeDtypeStruct((rows, units), bf16),
            jax.ShapeDtypeStruct((part_rows // 2, depth), bf16),
            jax.ShapeDtypeStruct((part_rows // 2, depth), bf16),
        ],
        input_output_aliases=aliases,
        compiler_params=params,
        cost_estimate=cost(LIGHT * 10),
        name="after_cross",
    )(*operands, *wholes)


def split_product_kernel(half_tiles, turned, flags, *refs):
    count = (len(refs) - 2) // 2
    product = nt if turned else nn
    block = product(refs[0][...], refs[count][...])
    for place in range(1, count):
        block = block + product(refs[place][...], refs[count + place][...])
    split_store(flags, pl.program_id(0), half_tiles, block.astype(bf16), *refs[-2:])


def split_product(chunk, flags, lefts, rights, turned):
    part_rows = lefts[0].shape[0] // CHUNKS
    depth = rights[0].shape[-2 if turned else -1]
    tiles = part_rows // TILE
    width = lefts[0].shape[1]
    half = jax.ShapeDtypeStruct((part_rows // 2, depth), bf16)
    return kernel_call(
        functools.partial(split_product_kernel, tiles // 2, turned),
        grid=(tiles,),
        in_specs=[SMEM]
        + [spec_rows(width, chunk * tiles)] * len(lefts)
        + [
            spec_whole(*right.shape) if right.ndim == 2 else spec_layer(layer, *right.shape[1:])
            for layer, right in enumerate(rights)
        ],
        out_specs=[spec_whole(part_rows // 2, depth)] * 2,
        out_shape=[half, half],
        compiler_params=params,
        cost_estimate=cost(LIGHT * 2.3),
        name="split_product",
    )(flags, *lefts, *rights)


def scatter_halves(sent, kept, quarter):
    both = kept.astype(f32) + swapped(sent, "tensor", 1).astype(f32)
    rows = sent.shape[0] // 2
    place = (quarter & 1) * rows
    other = lax.dynamic_slice_in_dim(both, rows - place, rows, 0).astype(bf16)
    return lax.dynamic_slice_in_dim(both, place, rows, 0), swapped(other, "tensor", 2)


def first_add_kernel(flags, arrived, kept, own, other):
    both = kept[...].astype(f32) + arrived[...].astype(f32)
    rows = own.shape[0]
    for second in range(2):

        @pl.when((flags[QUARTER] & 1) == second)
        def _(second=second):
            own[...] = both[second * rows : (second + 1) * rows]
            other[...] = both[(1 - second) * rows : (2 - second) * rows].astype(bf16)


def first_add(flags, arrived, kept):
    rows, depth = kept.shape[0] // 2, kept.shape[1]
    return kernel_call(
        first_add_kernel,
        in_specs=[SMEM] + [pl.BlockSpec(memory_space=pltpu.VMEM)] * 2,
        out_specs=[pl.BlockSpec(memory_space=pltpu.VMEM)] * 2,
        out_shape=[
            jax.ShapeDtypeStruct((rows, depth), f32),
            jax.ShapeDtypeStruct((rows, depth), bf16),
        ],
        compiler_params=small,
        cost_estimate=cost(LIGHT * 1.3),
        name="first_add",
    )(flags, arrived, kept)


def quarter_of(rel):
    return (rel & 1) * 2 + (rel >> 1)


def norm_back_rows_kernel(gain_row, flags, kept, arrived, source, residual, gains, result, sums):
    grad = kept[...] + arrived[...].astype(f32)
    normal, inv_scale = norm_parts(source[...].astype(f32))
    sums[...] = jnp.zeros(sums.shape, f32)
    sums[0:1, :] = jnp.sum(grad * normal, axis=0, keepdims=True)
    sums[1:2, :] = jnp.sum(grad, axis=0, keepdims=True)
    back = norm_back(grad, normal, inv_scale, row_of(gains, gain_row))
    result[...] = (residual[...].astype(f32) + back).astype(bf16)


def norm_back_rows(chunk, gain_row, flags, kept, arrived, source, residual, gains):
    rows, depth = kept.shape
    source_base = 4 * chunk if source.shape[0] > 4 * rows else 0

    def at(base):
        return pl.BlockSpec((rows, depth), lambda step, flags: (base + flags[QUARTER], 0))

    def whole(*shape):
        return pl.BlockSpec(shape, lambda step, flags: (0, 0))

    return kernel_call(
        functools.partial(norm_back_rows_kernel, gain_row),
        prefetch=1,
        grid=(1,),
        in_specs=[
            whole(rows, depth),
            whole(rows, depth),
            at(source_base),
            at(4 * chunk),
            whole(*gains.shape),
        ],
        out_specs=[whole(rows, depth), whole(STAT, depth)],
        out_shape=[
            jax.ShapeDtypeStruct((rows, depth), bf16),
            jax.ShapeDtypeStruct((STAT, depth), f32),
        ],
        compiler_params=small,
        cost_estimate=cost(LIGHT * 1.7),
        name="norm_back_rows",
    )(flags, kept, arrived, source, residual, gains)


def cross_back_kernel(base, slots, flags, *refs):
    pieces, refs = refs[:4], refs[4:]
    weight, queries, attended, log_total, text_keys, text_values = refs[:6]
    grad_rows, grad_q, grad_k, grad_v = refs[6:10]
    key_turned, query_heads, grad_heads, query_turned, grad_turned, inner, gq, gk, gv = refs[10:]
    step = pl.program_id(0)
    tile = base + step

    @pl.when(step == 0)
    def _():
        rows = pieces[0].shape[0]
        for rel, piece in enumerate(pieces):
            start = pl.multiple_of((flags[QUARTER] ^ quarter_of(rel)) * rows, rows)
            grad_rows[pl.ds(start, rows), :] = piece[...]
        turn_all(text_keys, key_turned)
        gk[...] = jnp.zeros(gk.shape, f32)
        gv[...] = jnp.zeros(gv.shape, f32)

    made = nt(grad_rows[tile_rows(step), :], weight[...]).astype(bf16)
    turned = turn(made)
    by_head(turned, grad_heads)
    grad_turned[...] = turned.astype(bf16)
    product = turned * turn(attended[...])
    for head in range(query_heads.shape[0]):
        part = product[head * HEAD_SIZE : (head + 1) * HEAD_SIZE]
        inner[pl.ds(head, 1), :] = jnp.sum(part, axis=0, keepdims=True)
    turned = turn(queries[...])
    by_head(turned, query_heads)
    query_turned[...] = turned.astype(bf16)
    gq[...] = jnp.zeros(gq.shape, f32)
    mask = text_mask(tile, flags[CUT], (flags[LENGTH], flags[LENGTH + 1]), slots)
    refs = (text_keys, text_values, key_turned, query_heads, grad_heads, grad_turned, query_turned, gq, gk, gv)
    back_tiles(0, 1, mask, refs, (log_total, inner))
    grad_q[...] = (jnp.transpose(gq[...]) * HEAD_SIZE**-0.5).astype(bf16)

    @pl.when(step == pl.num_programs(0) - 1)
    def _():
        grad_k[...] = jnp.transpose(gk[...])
        grad_v[...] = jnp.transpose(gv[...])


def cross_back(chunk, flags, pieces, weight, queries, attended, log_total, text_keys, text_values):
    part_rows, width = queries.shape
    depth = weight.shape[1]
    heads = width // HEAD_SIZE
    window = text_keys.shape[0]
    tiles = part_rows // TILE
    return kernel_call(
        functools.partial(cross_back_kernel, chunk * tiles, window // 2),
        grid=(tiles,),
        in_specs=[SMEM]
        + [spec_whole(part_rows // 4, depth)] * 4
        + [spec_whole(width, depth), spec_rows(width), spec_rows(width), spec_columns(STAT)]
        + [spec_whole(window, width)] * 2,
        out_specs=[
            spec_whole(part_rows, depth),
            spec_rows(width),
            spec_whole(window, width),
            spec_whole(window, width),
        ],
        out_shape=[
            jax.ShapeDtypeStruct((part_rows, depth), bf16),
            jax.ShapeDtypeStruct((part_rows, width), bf16),
            jax.ShapeDtypeStruct((window, width), f32),
            jax.ShapeDtypeStruct((window, width), f32),
        ],
        scratch_shapes=[
            pltpu.VMEM((width, window), bf16),
            pltpu.VMEM((heads, width, TILE), bf16),
            pltpu.VMEM((heads, width, TILE), bf16),
            pltpu.VMEM((width, TILE), bf16),
            pltpu.VMEM((width, TILE), bf16),
            pltpu.VMEM((STAT, TILE), f32),
            pltpu.VMEM((width, TILE), f32),
            pltpu.VMEM((width, window), f32),
            pltpu.VMEM((width, window), f32),
        ],
        compiler_params=params,
        cost_estimate=cost(LIGHT * 6),
        name="cross_back",
    )(flags, *pieces, weight, queries, attended, log_total, text_keys, text_values)


def back_to_self_kernel(*refs):
    parts, weights, refs = refs[:4], refs[4:8], refs[8:]
    source, residual, gains = refs[:3]
    result, sums = refs[-2:]
    grad = nt(parts[0][...], weights[0][...])
    for part, weight in zip(parts[1:], weights[1:]):
        grad = grad + nt(part[...], weight[...])
    normal, inv_scale = norm_parts(source[...])
    coming = residual[...].astype(f32)
    low = (coming + norm_back(grad, normal, inv_scale, row_of(gains, 1))).astype(bf16)
    result[...] = low

    @pl.when(pl.program_id(0) == 0)
    def _():
        sums[...] = jnp.zeros(sums.shape, f32)

    for row, term in enumerate((grad * normal, grad, low.astype(f32), coming)):
        sums[row : row + 1, :] += jnp.sum(term, axis=0, keepdims=True)


def back_to_self(chunk, parts, weights, source, residual, gains, wholes):
    part_rows, depth = source.shape
    width = parts[0].shape[1]
    tiles = part_rows // TILE
    operands = (*parts, *weights, source, residual, gains)
    return kernel_call(
        back_to_self_kernel,
        grid=(tiles,),
        in_specs=[spec_rows(width)] * 4
        + [spec_whole(depth, width)] * 4
        + [spec_rows(depth), spec_rows(depth), spec_whole(*gains.shape)]
        + [ANY] * len(wholes),
        out_specs=[spec_rows(depth, chunk * tiles), spec_whole(STAT, depth)],
        out_shape=[
            jax.ShapeDtypeStruct((part_rows * CHUNKS, depth), bf16),
            jax.ShapeDtypeStruct((STAT, depth), f32),
        ],
        input_output_aliases={len(operands) + place: place for place in range(len(wholes))},
        compiler_params=params,
        cost_estimate=cost(LIGHT * 5),
        name="back_to_self",
    )(*operands, *wholes)


def place_quarters_kernel(flags, *refs):
    for place, piece in enumerate(refs[:-1]):

        @pl.when(pl.program_id(0) == place)
        def _(piece=piece):
            refs[-1][...] = piece[...].astype(refs[-1].dtype)


def place_quarters(flags, chunks, dtype):
    rows, depth = chunks[0][0].shape
    pieces = [piece for chunk in chunks for piece in chunk]
    return kernel_call(
        place_quarters_kernel,
        prefetch=1,
        grid=(len(pieces),),
        in_specs=[pl.BlockSpec((rows, depth), lambda step, flags: (0, 0))] * len(pieces),
        out_specs=pl.BlockSpec(
            (rows, depth),
            lambda step, flags: (step // 4 * 4 + (flags[QUARTER] ^ quarter_of(step % 4)), 0),
        ),
        out_shape=jax.ShapeDtypeStruct((rows * len(pieces), depth), dtype),
        compiler_params=small,
        cost_estimate=cost(LIGHT * 5),
        name="place_quarters",
    )(flags, *pieces)


def place_relative_kernel(turned, places, held, arrived, *results):
    step = pl.program_id(0)
    half = pl.num_programs(0) // 2
    each = pl.num_programs(0) // len(results)
    piece = step ^ places[0]

    def store(source):
        for place, result in enumerate(results):

            @pl.when(step // each == place)
            def _(result=result, place=place):
                if place < turned:
                    result[...] = turn(source[0])
                    return
                if result.ndim == 2:
                    result[...] = source[0].astype(f32)
                    return
                width = result.shape[2]
                for part in range(result.shape[0]):
                    result[part] = source[0, :, part * width : (part + 1) * width].astype(f32)

    @pl.when(piece < half)
    def _():
        store(held)

    @pl.when(piece >= half)
    def _():
        store(arrived)


def place_relative(place, held, arrived, parts, stacked, turned):
    count, rows, width = held.shape
    each = 2 * count // stacked
    if turned and rows % 128:
        results = place_relative(place, held, arrived, parts, stacked, 0)
        return [jnp.transpose(part) for part in results[:turned]] + list(results[turned:])
    if parts > 1:
        out_specs = [pl.BlockSpec((parts, rows, width // parts), lambda step, place: (0, step, 0))]
        shape = [jax.ShapeDtypeStruct((parts, 2 * count * rows, width // parts), f32)]
    else:
        out_specs = [
            pl.BlockSpec(
                (rows, width),
                lambda step, place, first=number * each: (jnp.clip(step - first, 0, each - 1), 0),
            )
            for number in range(stacked)
        ]
        shape = [jax.ShapeDtypeStruct((each * rows, width), f32)] * stacked
    for number in range(turned):
        out_specs[number] = pl.BlockSpec(
            (width, rows),
            lambda step, place, first=number * each: (0, jnp.clip(step - first, 0, each - 1)),
        )
        shape[number] = jax.ShapeDtypeStruct((width, each * rows), f32)
    piece = pl.BlockSpec((1, rows, width), lambda step, place: ((step ^ place[0]) % count, 0, 0))
    return kernel_call(
        functools.partial(place_relative_kernel, turned),
        prefetch=1,
        grid=(2 * count,),
        in_specs=[piece, piece],
        out_specs=out_specs,
        out_shape=shape,
        compiler_params=small,
        cost_estimate=cost(LIGHT * 5),
        name="place_relative",
    )(place, held, arrived)


def halving_orders(bits):
    return list(range(bits)), [1, 0] + list(range(2, bits))


class HalvingSum:
    def __init__(self):
        self.orders = halving_orders(axis_bits("seq"))
        self.odd = lax.axis_index("tensor") & 1
        self.mine = []
        for even, odd in zip(*self.orders):
            self.mine.append(jnp.where(self.odd == 0, rank_bit("seq", even), rank_bit("seq", odd)))
        place = 0
        for mine in self.mine:
            place = place * 2 + mine
        self.place = jnp.reshape(place, (1,)).astype(jnp.int32)

    def swap(self, value, level):
        count = lax.axis_size("tensor")
        pairs = []
        for seq in range(lax.axis_size("seq")):
            for tensor in range(count):
                partner = seq ^ (1 << self.orders[tensor & 1][level])
                pairs.append((seq * count + tensor, partner * count + tensor))
        return lax.ppermute(value, ("seq", "tensor"), pairs)

    def scatter(self, held, level):
        rows = held.shape[0] // 2
        mine = self.mine[level]
        sent = lax.dynamic_slice_in_dim(held, (1 - mine) * rows, rows, 0)
        arrived = self.swap(sent, level)
        kept = lax.dynamic_slice_in_dim(held, mine * rows, rows, 0)
        return (kept.astype(f32) + arrived.astype(f32)).astype(bf16)

    def gather(self, held, level):
        return jnp.concatenate((held, self.swap(held, level)))

    def gathers(self, order, value):
        state = {"held": value}
        count = len(self.mine)

        def join(level, held, arrived):
            held = jnp.concatenate((held, arrived))
            state["held"] = held
            if level > 0:
                state["arrived"] = self.swap(held, level - 1)
            return held

        state["arrived"] = self.swap(value, count - 1)
        for level in reversed(range(count)):
            yield functools.partial(join, level), state, order

    def steps(self, order, value, parts=1, stacked=1, turned=0):
        state = {"held": value}
        count = len(self.mine)

        def scatter_send(level):
            rows = state["held"].shape[0] // 2
            mine = self.mine[level]
            sent = lax.dynamic_slice_in_dim(state["held"], (1 - mine) * rows, rows, 0)
            state["arrived"] = self.swap(sent, level)

        def scatter_add(level, held, arrived):
            rows = held.shape[0] // 2
            kept = lax.dynamic_slice_in_dim(held, self.mine[level] * rows, rows, 0)
            held = (kept.astype(f32) + arrived.astype(f32)).astype(bf16)
            state["held"] = held
            if level + 1 < count:
                scatter_send(level + 1)
            else:
                state["held"] = held[None]
                state["arrived"] = self.swap(state["held"], level)
            return held

        def gather_join(level, held, arrived):
            held = jnp.concatenate((held, arrived))
            state["held"] = held
            state["arrived"] = self.swap(held, level - 1)
            return held

        def finish(held, arrived):
            return place_relative(self.place, held, arrived, parts, stacked, turned)

        scatter_send(0)
        for level in range(count):
            yield functools.partial(scatter_add, level), state, order
        for level in reversed(range(1, count)):
            yield functools.partial(gather_join, level), state, order
        yield finish, state, order.kernel


def text_sums_kernel(flags, windows, grad_k, grad_v):
    count, _, _, slots, _ = windows.shape
    bits = (count - 1).bit_length()
    odd = flags[CORE]

    def place_of(rank, odd):
        place = 0
        for even_bit, odd_bit in zip(*halving_orders(bits)):
            place = place * 2 + ((rank >> (even_bit + (odd_bit - even_bit) * odd)) & 1)
        return place

    own = place_of(flags[SEQ], odd)
    places = [place_of(owner, odd) ^ own for owner in range(count)]
    for item in range(count + 1):
        for kind, result in enumerate((grad_k, grad_v)):
            total = jnp.zeros((slots, result.shape[1]), f32)
            if item < count:
                total = windows[places[item], kind, 0].astype(f32)
            if item > 0:
                total = total + windows[places[item - 1], kind, 1].astype(f32)
            result[item * slots : (item + 1) * slots] = total.astype(bf16)


def text_sums(flags, windows):
    count, _, _, slots, width = windows.shape
    shape = ((count + 1) * slots, width)
    return kernel_call(
        text_sums_kernel,
        grid=(1,),
        in_specs=[SMEM, spec_whole(*windows.shape)],
        out_specs=[spec_whole(*shape)] * 2,
        out_shape=[jax.ShapeDtypeStruct(shape, bf16)] * 2,
        compiler_params=params,
        cost_estimate=cost(LIGHT * 2),
        name="text_sums",
    )(flags, windows)


def per_device(
    tokens,
    item_ids,
    text_states,
    text_lengths,
    norm_gain,
    norm_shift,
    w_self,
    b_self,
    w_self_out,
    w_cross_q,
    w_cross_kv,
    b_cross,
    w_cross_out,
    w_up,
    b_up,
    w_down,
    out_bias,
    d_out,
):
    row_count = tokens.shape[0]
    assert row_count == ITEM_LEN and lax.axis_size("tensor") == 4
    local_width = w_self.shape[2]
    seq_rank = lax.axis_index("seq")
    tensor_rank = lax.axis_index("tensor")
    quarter = quarter_of(tensor_rank)
    item_total, slot_count = text_states.shape[:2]
    slot_total = item_total * slot_count
    cut = jnp.sum((item_ids == 0).astype(jnp.int32))
    item_lengths = lax.dynamic_slice_in_dim(text_lengths, seq_rank, 2)
    flags = jnp.stack(
        (
            cut,
            (seq_rank > 0).astype(jnp.int32),
            item_lengths[0],
            item_lengths[1],
            quarter,
            tensor_rank & 1,
            seq_rank,
        )
    )
    chunks = range(CHUNKS)
    halving_sum = HalvingSum()

    def local_cols(full_rows):
        return lax.dynamic_slice_in_dim(full_rows, tensor_rank * local_width, local_width, axis=1)

    def token_sum(rows_in):
        return jnp.sum(rows_in.astype(f32), axis=0)

    order = Order()
    gains, shifts, biases = norm_gain, norm_shift, out_bias
    inputs_one, both = order.kernel(enter, tokens, w_self, b_self, gains, shifts)
    both_far = shifted(both, "seq", 1)
    late = tied((w_self_out, w_cross_out), both)
    crossing = [swapped(late[0], "tensor", 2), swapped(late[1], "tensor", 2)]
    queries, top, total, acc = order.kernel(
        own_attend, flags, inputs_one, w_self, b_self, both
    )

    text_flat = text_states.reshape(slot_total, text_states.shape[2])
    text_window = lax.dynamic_slice_in_dim(text_flat, seq_rank * slot_count, 2 * slot_count, 0)

    def project_text(window, key_weight, value_weight, bias):
        text_keys = matmul_low(window, key_weight).astype(bf16)
        return text_keys, (matmul_low(window, value_weight) + bias.astype(f32)).astype(bf16)

    text_keys, text_values = order(
        project_text, text_window, w_cross_kv[0], w_cross_kv[1], b_cross[1]
    )
    grad_hidden = order(
        lambda grad, weight: times_transpose(grad, weight).astype(bf16), d_out, w_down
    )
    attended, log_total, after_one, inputs_two, cross_queries, cross_attended, cross_log = (
        [] for _ in range(7)
    )
    operands = (flags, queries, both_far, top, total, acc)
    first = order.kernel(functools.partial(far_attend, 0), *operands)
    across = [swapped(first[0], "tensor", 2)]
    second, across = order.kernel(functools.partial(far_attend, 1), *operands, during=across)
    attended, log_total = zip(first, second)
    across = [*across, swapped(attended[1], "tensor", 2)]
    crossing = tied(crossing, attended[-1])
    self_out, cross_out = (
        [own, swapped(own, "tensor", 1), across, swapped(across, "tensor", 1)]
        for own, across in zip(late, crossing)
    )
    after_one, inputs_two, cross_queries, cross_attended, cross_log = ([] for _ in range(5))

    def keep(made, *lists):
        for held, part in zip(lists, made):
            held.append(part)

    def run_after_self(chunk, across, during):
        return order.kernel(
            lambda *operands: after_self(
                chunk, *operands[:2], operands[2:6], operands[6:10], *operands[10:]
            ),
            flags,
            tokens,
            *gathered(attended[chunk], across),
            *self_out,
            biases,
            gains,
            shifts,
            w_cross_q,
            b_cross,
            text_keys,
            text_values,
            during=during,
        )

    made, (across_next,) = run_after_self(0, across[0], [across[1]])
    keep(made, after_one, inputs_two, cross_queries, cross_attended, cross_log)
    across = swapped(cross_attended[0], "tensor", 2)
    made, (across,) = run_after_self(1, across_next, [across])
    keep(made, after_one, inputs_two, cross_queries, cross_attended, cross_log)
    across_next = swapped(cross_attended[1], "tensor", 2)

    def low_rows(left, right):
        return contract_rows(left, right).astype(bf16)

    def products(*operands):
        return jnp.concatenate(
            [low_rows(left, right) for left, right in zip(operands[::2], operands[1::2])]
        )

    def scatter_first(chunk_halves):
        arrived = swapped(chunk_halves[0], "tensor", 1)
        kept, other = order.kernel(first_add, flags, arrived, chunk_halves[1])
        return kept, swapped(other, "tensor", 2)

    ready = {}

    def advance(*lanes):
        for lane in lanes:
            step, state, run = next(lane, (None, None, None))
            if step is not None:
                ready[id(lane)] = run(step, state["held"], state["arrived"])

    def begun(lane):
        first = next(lane)

        def rest():
            yield first
            yield from lane

        return rest()

    def run_after_cross(chunk, across, wholes, during):
        return order.kernel(
            lambda *operands: after_cross(
                chunk, *operands[:2], operands[2:6], operands[6:10], *operands[10:16], operands[16:]
            ),
            flags,
            after_one[chunk],
            *gathered(cross_attended[chunk], across),
            *cross_out,
            grad_hidden,
            w_up,
            b_up[None],
            biases,
            gains,
            shifts,
            *wholes,
            during=during,
        )

    made, (across,) = run_after_cross(0, across, (), [across_next])
    after_two = [made[0]]
    late_across = swapped(tied(w_cross_q, across), "tensor", 2)
    kept, other = scatter_first(made[4:])
    made, (other, late_across) = run_after_cross(1, across, made[1:4], [other, late_across])
    after_two.append(made[0])
    inputs_three, hidden, grad_pre = made[1:4]
    all_cross_q = gathered(w_cross_q, late_across)
    kept_next, other_next = scatter_first(made[4:])

    def norm_step(chunk, kept, other):
        return order.kernel(
            functools.partial(norm_back_rows, chunk, 2),
            flags,
            kept,
            other,
            after_two[chunk],
            d_out,
            gains,
        )

    shard, sums = norm_step(0, kept, other)
    shards, shard_sums_three = [shard], [sums]
    across = swapped(shard, "tensor", 2)
    mlp_grads, (other_next,) = order(
        products, hidden, d_out, inputs_three, grad_pre, during=[other_next]
    )
    mlp_shard = lax.psum_scatter(mlp_grads, "seq", scatter_dimension=0, tiled=True)
    early_sums = order(
        lambda left, right: [token_sum(local_cols(left)), token_sum(right)], d_out, grad_pre
    )
    shard, sums = norm_step(1, kept_next, other_next)
    shards.append(shard)
    shard_sums_three.append(sums)
    across_next = swapped(shard, "tensor", 2)

    def run_cross_back(chunk, across, during):
        return order.kernel(
            lambda *operands: cross_back(chunk, operands[0], operands[1:5], *operands[5:]),
            flags,
            *gathered(shards[chunk], across),
            w_cross_out,
            cross_queries[chunk],
            cross_attended[chunk],
            cross_log[chunk],
            text_keys,
            text_values,
            during=during,
        )

    grad_cross_low, grad_cross_q, text_key_parts, text_value_parts = ([] for _ in range(4))
    made, (across,) = run_cross_back(0, across, [across_next])
    keep(made, grad_cross_low, grad_cross_q, text_key_parts, text_value_parts)
    across_next = swapped(grad_cross_q[0], "tensor", 2)
    made, (across,) = run_cross_back(1, across, [across_next])
    keep(made, grad_cross_low, grad_cross_q, text_key_parts, text_value_parts)
    across_next = swapped(grad_cross_q[1], "tensor", 2)

    def text_windows(*parts):
        both = jnp.stack((sum(parts[:CHUNKS]), sum(parts[CHUNKS:]))).astype(bf16)
        return both.reshape(1, 2, 2, slot_count, local_width)

    text_lane = order(text_windows, *text_key_parts, *text_value_parts)
    text_lane = begun(halving_sum.gathers(order, text_lane))

    def output_product(chunk, source, weight):
        return split_product(chunk, flags, (source,), (weight,), False)

    first_output, (across_next,) = order.kernel(
        functools.partial(output_product, 0), hidden, w_down, during=[across_next]
    )

    def run_back_to_self(chunk, across, wholes, during=()):
        return order.kernel(
            lambda *operands: back_to_self(
                chunk, operands[:4], operands[4:8], *operands[8:11], operands[11:]
            ),
            *gathered(grad_cross_q[chunk], across),
            *all_cross_q,
            after_one[chunk],
            grad_cross_low[chunk],
            gains,
            *wholes,
            during=during,
        )

    whole, sums = run_back_to_self(0, across, ())
    row_sums = [sums]
    grad_self_low, sums = run_back_to_self(1, across_next, (whole,))
    row_sums.append(sums)
    advance(text_lane)

    def joined(*parts):
        return [jnp.concatenate(parts[k : k + CHUNKS]) for k in range(0, len(parts), CHUNKS)]

    attended, log_rows = order(
        lambda *parts: joined(*parts[:CHUNKS]) + [jnp.concatenate(parts[CHUNKS:], axis=1)],
        *attended,
        *log_total,
    )
    grad_att, inner, grad_q, grad_far = order.kernel(
        far_back, flags, grad_self_low, w_self_out, queries, attended, log_rows, both_far
    )
    carried = shifted(grad_far, "seq", -1)
    advance(text_lane)
    (grad_queries, grad_keys, grad_values), (mlp_shard,) = order.kernel(
        own_back,
        flags,
        grad_att,
        inner,
        queries,
        log_rows,
        both,
        grad_q,
        during=[mlp_shard],
    )
    mlp_sums = lax.all_gather(mlp_shard, "seq", tiled=True)
    joins = order(joined, *grad_cross_q, *inputs_two, *cross_attended, *grad_cross_low)
    cross_grads = order(products, *joins, attended, grad_self_low)

    def add_carried(grad_keys, grad_values, carried):
        return (
            (grad_keys + carried[:, :local_width].astype(f32)).astype(bf16),
            (grad_values + carried[:, local_width:].astype(f32)).astype(bf16),
        )

    grad_keys, grad_values = order(add_carried, grad_keys, grad_values, carried)

    def self_products(inputs, *grads):
        return jnp.concatenate([low_rows(inputs, grad) for grad in grads], axis=1)

    self_grads = order(self_products, inputs_one, grad_queries, grad_keys, grad_values)
    self_lane = begun(halving_sum.steps(order, self_grads, 3))

    def token_product(chunk, *operands):
        return split_product(chunk, flags, operands[:3], operands[3:], True)

    token_terms = []
    for chunk in chunks:
        made = order.kernel(
            functools.partial(token_product, chunk),
            grad_queries,
            grad_keys,
            grad_values,
            w_self,
            w_self,
            w_self,
        )
        token_terms.append(scatter_first(made))
    for _ in range(axis_bits("seq")):
        advance(text_lane)
    grad_text_keys, grad_text_values = order.kernel(
        functools.partial(text_sums, flags), ready[id(text_lane)]
    )

    def text_grads(grad_text_keys, grad_text_values):
        part = times_transpose(grad_text_keys, w_cross_kv[0]) + times_transpose(
            grad_text_values, w_cross_kv[1]
        )
        return part.astype(bf16)

    grad_text_part, others = order(
        text_grads,
        grad_text_keys,
        grad_text_values,
        during=[other for _, other in token_terms],
    )
    shard_sums_one, token_shards = [], []
    for chunk in chunks:
        shard, sums = order.kernel(
            functools.partial(norm_back_rows, chunk, 0),
            flags,
            token_terms[chunk][0],
            others[chunk],
            tokens,
            grad_self_low,
            gains,
        )
        shard_sums_one.append(sums)
        token_shards.append(shard)
    token_across = [swapped(shard, "tensor", 2) for shard in token_shards]
    grad_text_shard = scatter_rows(grad_text_part, "tensor").astype(bf16)

    def norm_sums(*parts):
        return jnp.concatenate((sum(parts[:CHUNKS])[:2], sum(parts[CHUNKS:])[:2]))

    shard_sums = order(norm_sums, *shard_sums_one, *shard_sums_three)
    shard_sums = scatter_columns(shard_sums, "tensor")
    second_output, token_across = order.kernel(
        functools.partial(output_product, 1), hidden, w_down, during=token_across
    )
    output_terms = [scatter_first(first_output), scatter_first(second_output)]
    advance(self_lane)

    def vector_rows(cross_grads, shard_sums, sum_d_out, sum_pre, cross_q, queries, values, *row_sums):
        rows = local_cols(sum(row_sums)[:4])
        vectors = jnp.concatenate(
            (
                shard_sums[:1],
                rows[:1],
                shard_sums[2:3],
                shard_sums[1:2],
                rows[1:2],
                shard_sums[3:],
                rows[2:],
                sum_d_out[None],
                jnp.stack((token_sum(cross_q), token_sum(queries), token_sum(values))),
                sum_pre.reshape(-1, local_width),
            )
        )
        vectors = vectors.astype(bf16).reshape(-1, cross_grads.shape[1])
        spare = jnp.zeros((PAD - vectors.shape[0], cross_grads.shape[1]), bf16)
        return jnp.concatenate((cross_grads, vectors, spare))

    cross_grads = order(
        vector_rows,
        cross_grads,
        shard_sums,
        *early_sums,
        joins[0],
        grad_queries,
        grad_values,
        *row_sums,
    )
    cross_lane = begun(halving_sum.steps(order, cross_grads, stacked=4, turned=1))
    advance(self_lane)
    grad_text_shard = tied(grad_text_shard, order.pending)
    grad_text_across = swapped(grad_text_shard, "tensor", 2)
    advance(self_lane)

    def output_shard(kept, other, rows_in):
        rows = kept.shape[0]
        base = lax.dynamic_slice_in_dim(rows_in, quarter * rows, rows, 0)
        return (base + ((kept + other.astype(f32)) + biases[2].astype(f32))).astype(bf16)

    output_shards = [
        order(output_shard, *output_terms[chunk], after_two[chunk]) for chunk in chunks
    ]
    output_across = [swapped(shard, "tensor", 2) for shard in output_shards]
    pieces = [gathered(token_shards[chunk], token_across[chunk]) for chunk in chunks]
    advance(cross_lane)
    def wide_sums(sums):
        half = sums.shape[0] // 2
        return [sums[:half].astype(f32), sums[half:].astype(f32)]

    sum_w_down, sum_w_up = order(wide_sums, mlp_sums)
    grad_tokens = order.kernel(
        lambda *pieces: place_quarters(flags, (pieces[:4], pieces[4:]), f32), *pieces[0], *pieces[1]
    )
    advance(self_lane, cross_lane)
    grad_w_cross_kv, output_across = order(
        lambda *operands: jnp.stack(
            (contract_rows(operands[0], operands[1]), contract_rows(operands[0], operands[2]))
        ),
        text_flat,
        grad_text_keys,
        grad_text_values,
        during=output_across,
    )
    grad_value_bias = token_sum(grad_text_values)
    advance(self_lane, cross_lane)
    pieces = [gathered(output_shards[chunk], output_across[chunk]) for chunk in chunks]
    output_rows = order.kernel(
        lambda *pieces: place_quarters(flags, (pieces[:4], pieces[4:]), bf16), *pieces[0], *pieces[1]
    )
    advance(self_lane, cross_lane)

    advance(cross_lane)
    grad_text = order.kernel(
        lambda *pieces: place_quarters(flags, (pieces,), f32),
        *gathered(grad_text_shard, grad_text_across),
    )
    grad_text = grad_text.reshape(text_states.shape)
    for _ in range(4 * axis_bits("seq") + 4):
        advance(self_lane, cross_lane)
    (grad_w_self,), cross_grads = ready[id(self_lane)], ready[id(cross_lane)]
    vectors = cross_grads[3][:STAT].reshape(-1, local_width)
    grad_b_cross = jnp.stack((vectors[9], grad_value_bias))
    return (
        output_rows,
        grad_tokens,
        grad_text,
        vectors[:3],
        vectors[3:6],
        grad_w_self,
        vectors[10:12],
        cross_grads[2],
        cross_grads[0],
        grad_w_cross_kv,
        grad_b_cross,
        cross_grads[1],
        sum_w_up,
        vectors[12 : 12 + w_up.shape[1] // local_width].reshape(-1),
        sum_w_down,
        vectors[6:9],
    )


def solution(mesh):
    placed = (
        P("seq", None),
        P(),
        P(),
        P(),
        P(),
        P(),
        P(None, None, "tensor"),
        P(None, "tensor"),
        P("tensor", None),
        P(None, "tensor"),
        P(None, None, "tensor"),
        P(None, "tensor"),
        P("tensor", None),
        P(None, "tensor"),
        P("tensor"),
        P("tensor", None),
        P(),
        P("seq", None),
    )
    return jax.shard_map(
        per_device,
        mesh=mesh,
        in_specs=placed,
        out_specs=(
            P("seq", None),
            P("seq", None),
            P(),
            P(None, "tensor"),
            P(None, "tensor"),
            P(None, None, "tensor"),
            P(None, "tensor"),
            P("tensor", None),
            P(None, "tensor"),
            P(None, None, "tensor"),
            P(None, "tensor"),
            P("tensor", None),
            P(None, "tensor"),
            P("tensor"),
            P("tensor", None),
            P(None, "tensor"),
        ),
        check_vma=False,
    )
```

```python
import functools

import jax
import jax.numpy as jnp
from jax import lax
from jax.experimental import pallas as pl
from jax.experimental.pallas import tpu as pltpu
from jax.sharding import PartitionSpec as P

HEAD_SIZE = 64
ITEM_LEN = 1024
TILE = 256
STAT = 8
CHUNKS = 2
PAD = 256


epsilon = 1e-05
masked_fill = -1e30
f32, bf16 = jnp.float32, jnp.bfloat16
CUT, HAS_FAR, LENGTH, QUARTER, CORE, SEQ = 0, 1, 2, 4, 5, 6


def shifted(value, axis, steps):
    count = lax.axis_size(axis)
    leading, last = (max(0, -steps), min(count, count - steps))
    return lax.ppermute(value, axis, [(source, source + steps) for source in range(leading, last)])


def matmul_low(left, right):
    return jnp.dot(left, right, preferred_element_type=jnp.float32)


def contract_rows(left, right):
    return jnp.einsum("ra,rb->ab", left, right, preferred_element_type=jnp.float32)


def times_transpose(left, right):
    return jnp.einsum("ra,ba->rb", left, right, preferred_element_type=jnp.float32)


def norm_back(grad_normed, normal, inv_scale, gain):
    grad_normal = grad_normed * gain
    grad_mean = jnp.mean(grad_normal, axis=-1, keepdims=True)
    proj_mean = jnp.mean(grad_normal * normal, axis=-1, keepdims=True)
    return inv_scale * (grad_normal - grad_mean - normal * proj_mean)


def swapped(value, axis, distance):
    count = lax.axis_size(axis)
    return lax.ppermute(value, axis, [(source, source ^ distance) for source in range(count)])


def tied(value, *others):
    return lax.optimization_barrier((value, others))[0]


class Order:
    def __init__(self):
        self.pending = []

    def finish(self, result, during):
        self.pending = jax.tree.leaves(result)[-1:]
        if not during:
            return result
        return lax.optimization_barrier((result, tuple(during)))

    def __call__(self, step, *operands, during=()):
        operands, pending = lax.optimization_barrier((operands, self.pending))
        result = self.finish(step(*operands), during)
        self.pending = pending + self.pending
        return result

    def kernel(self, step, *operands, during=()):
        current.append(self)
        result = step(*operands)
        current.pop()
        return self.finish(result, during)


current = []


def kernel_call(kernel, prefetch=0, grid=(), in_specs=(), out_specs=None, scratch_shapes=(), **options):
    def run(*operands):
        order = current[-1] if current else None
        waits = order.pending if order else []
        count = len(operands)

        def body(*refs):
            kernel(*refs[:count], *refs[count + len(waits) :])

        result = pl.pallas_call(
            body,
            grid_spec=pltpu.PrefetchScalarGridSpec(
                num_scalar_prefetch=prefetch,
                grid=grid,
                in_specs=list(in_specs) + [pl.BlockSpec(memory_space=pl.ANY)] * len(waits),
                out_specs=out_specs,
                scratch_shapes=list(scratch_shapes),
            ),
            **options,
        )(*operands, *waits)
        return result

    return run


def axis_bits(axis):
    return (lax.axis_size(axis) - 1).bit_length()


def gather_relative(block, axis):
    blocks = {0: block}
    for bit in reversed(range(axis_bits(axis))):
        blocks.update(
            {d ^ (1 << bit): swapped(held, axis, 1 << bit) for d, held in list(blocks.items())}
        )
    return [blocks[d] for d in range(len(blocks))]


def gathered(block, across):
    return [block, swapped(block, "tensor", 1), across, swapped(across, "tensor", 1)]


def rank_bit(axis, bit):
    return (lax.axis_index(axis) >> bit) & 1


def shard_offset(axis, row_count):
    offset = 0
    for bit in range(axis_bits(axis)):
        offset = offset + rank_bit(axis, bit) * (row_count >> (bit + 1))
    return offset


def scatter_rows(partial_rows, axis):
    held = partial_rows
    for bit in range(axis_bits(axis)):
        half = held.shape[0] // 2
        mine = rank_bit(axis, bit)
        sent = lax.dynamic_slice_in_dim(held, (1 - mine) * half, half, 0)
        kept = lax.dynamic_slice_in_dim(held, mine * half, half, 0)
        arrived = swapped(sent, axis, 1 << bit)
        held = kept.astype(jnp.float32) + arrived.astype(jnp.float32)
        if bit + 1 < axis_bits(axis):
            held = held.astype(jnp.bfloat16)
    return held


def scatter_columns(partial, axis):
    held = partial
    for bit in reversed(range(axis_bits(axis))):
        half = held.shape[1] // 2
        mine = rank_bit(axis, bit)
        sent = lax.dynamic_slice_in_dim(held, (1 - mine) * half, half, 1)
        kept = lax.dynamic_slice_in_dim(held, mine * half, half, 1)
        held = kept + swapped(sent, axis, 1 << bit)
    return held


def butterfly_sum(value, axis):
    for bit in range(axis_bits(axis)):
        value = value + swapped(value, axis, 1 << bit)
    return value


def nn(left, right):
    return lax.dot_general(left, right, (((1,), (0,)), ((), ())), preferred_element_type=f32)


def nt(left, right):
    return lax.dot_general(left, right, (((1,), (1,)), ((), ())), preferred_element_type=f32)


def tile_rows(index):
    return pl.ds(pl.multiple_of(index * TILE, TILE), TILE)


def head_rows(head):
    return pl.ds(head * HEAD_SIZE, HEAD_SIZE)


def row_of(ref, row):
    return ref[...].astype(f32)[row : row + 1]


def turn(block):
    return jnp.transpose(block.astype(f32))


def by_head(turned, store):
    row_head = lax.broadcasted_iota(jnp.int32, turned.shape, 0) // HEAD_SIZE
    for head in range(store.shape[0]):
        store[head] = jnp.where(row_head == head, turned, 0.0).astype(store.dtype)


def tile_places(query_tile, key_tile):
    query_at = query_tile * TILE + lax.broadcasted_iota(jnp.int32, (1, TILE), 1)
    key_at = key_tile * TILE + lax.broadcasted_iota(jnp.int32, (TILE, 1), 0)
    return query_at, key_at


def own_mask(query_tile, cut):
    def allowed(key_tile):
        query_at, key_at = tile_places(query_tile, key_tile)
        first_key = jnp.where(query_at >= cut, cut, 0)
        return (key_at <= query_at) & (key_at >= first_key)

    return allowed


def far_mask(query_tile, cut):
    def allowed(key_tile):
        query_at, key_at = tile_places(query_tile, key_tile)
        first_key = jnp.where(query_at < cut, cut, TILE * 1024)
        return key_at >= first_key

    return allowed


def text_mask(query_tile, cut, lengths, slots):
    def allowed(key_tile):
        query_at, key_at = tile_places(query_tile, key_tile)
        first_key = jnp.where(query_at < cut, 0, slots)
        last_key = jnp.where(query_at < cut, lengths[0], slots + lengths[1])
        return (key_at >= first_key) & (key_at < last_key)

    return allowed


def own_tiles(query_tile, cut):
    return jnp.where(query_tile * TILE >= cut, cut // TILE, 0), query_tile + 1


def far_tiles(query_tile, cut, has_far, tiles):
    live = (query_tile * TILE < cut) & (has_far > 0)
    return cut // TILE, jnp.where(live, tiles, 0)


def attend_tiles(first, last, mask, key_ref, value_turned, query_heads, top, total, acc):
    heads = query_heads.shape[0]

    def step(key_tile, carry):
        allowed = mask(key_tile)
        keys = key_ref[tile_rows(key_tile), :]
        scores = [
            jnp.where(allowed, nn(keys, query_heads[head]), masked_fill) for head in range(heads)
        ]
        old_top = [top[pl.ds(head, 1), :] for head in range(heads)]
        new_top = [
            jnp.maximum(old, jnp.max(part, axis=0, keepdims=True))
            for old, part in zip(old_top, scores)
        ]
        weights = [jnp.exp(part - new) for part, new in zip(scores, new_top)]
        factors = [jnp.exp(old - new) for old, new in zip(old_top, new_top)]
        sums = [jnp.sum(part, axis=0, keepdims=True) for part in weights]
        values = [
            nn(value_turned[head_rows(head), tile_rows(key_tile)], weights[head].astype(bf16))
            for head in range(heads)
        ]
        for head in range(heads):
            row = pl.ds(head, 1)
            top[row, :] = new_top[head]
            total[row, :] = total[row, :] * factors[head] + sums[head]
            acc[head_rows(head), :] = acc[head_rows(head), :] * factors[head] + values[head]
        return carry

    lax.fori_loop(first, last, step, 0)


def turn_all(source, target):
    for tile in range(source.shape[0] // TILE):
        rows = pl.ds(tile * TILE, TILE)
        target[:, rows] = turn(source[rows, :]).astype(target.dtype)


def own_attend_kernel(flags, inputs, weight, bias, keys, values, queries, top, total, acc, value_turned, query_heads):
    tile = pl.program_id(0)
    cut = flags[0]

    @pl.when(tile == 0)
    def _():
        turn_all(values, value_turned)

    made = (nn(inputs[...], weight[...]) + row_of(bias, 0)).astype(bf16)
    made = made.astype(f32) * HEAD_SIZE**-0.5
    queries[...] = made.astype(bf16)
    by_head(jnp.transpose(made), query_heads)
    top[...] = jnp.full(top.shape, masked_fill, f32)
    total[...] = jnp.zeros(total.shape, f32)
    acc[...] = jnp.zeros(acc.shape, f32)
    first, last = own_tiles(tile, cut)
    attend_tiles(first, last, own_mask(tile, cut), keys, value_turned, query_heads, top, total, acc)


def far_attend_kernel(base, flags, queries, keys, values, top_in, total_in, acc_in, attended, log_total, value_turned, query_heads, top, total, acc):
    tile = base + pl.program_id(0)
    cut = flags[0]

    @pl.when(pl.program_id(0) == 0)
    def _():
        turn_all(values, value_turned)

    by_head(turn(queries[...]), query_heads)
    top[...] = top_in[...]
    total[...] = total_in[...]
    acc[...] = acc_in[...]
    first, last = far_tiles(tile, cut, flags[1], keys.shape[0] // TILE)
    attend_tiles(first, last, far_mask(tile, cut), keys, value_turned, query_heads, top, total, acc)
    log_total[...] = top[...] + jnp.log(total[...])
    for head in range(query_heads.shape[0]):
        acc[head_rows(head), :] = acc[head_rows(head), :] / total[pl.ds(head, 1), :]
    attended[...] = jnp.transpose(acc[...]).astype(bf16)


def spec_rows(width, base=0):
    return pl.BlockSpec((TILE, width), lambda tile: (base + tile, 0))


def spec_columns(height, base=0):
    return pl.BlockSpec((height, TILE), lambda tile: (0, base + tile))


def spec_layer(layer, rows, width):
    return pl.BlockSpec((None, rows, width), lambda tile: (layer, 0, 0))


def spec_side(side, rows, width):
    return pl.BlockSpec((rows, width), lambda tile: (0, side))


def spec_whole(*shape):
    return pl.BlockSpec(shape, lambda tile: (0,) * len(shape))


SMEM = pl.BlockSpec(memory_space=pltpu.SMEM)
params = pltpu.CompilerParams(vmem_limit_bytes=48 * 2**20)
small = pltpu.CompilerParams(vmem_limit_bytes=16 * 2**20)


LIGHT = 0.1


def cost(us):
    return pl.CostEstimate(
        flops=int(us * 1.15e9), bytes_accessed=int(us * 3.6e6), transcendentals=0
    )


def own_attend(flags, inputs, weight, bias, both):
    rows, width = both.shape[0], both.shape[1] // 2
    depth = inputs.shape[1]
    heads = width // HEAD_SIZE
    return kernel_call(
        own_attend_kernel,
        grid=(rows // TILE,),
        in_specs=[SMEM, spec_rows(depth), spec_layer(0, depth, width), spec_whole(*bias.shape), spec_side(0, rows, width), spec_side(1, rows, width)],
        out_specs=[spec_rows(width), spec_columns(STAT), spec_columns(STAT), spec_columns(width)],
        out_shape=[
            jax.ShapeDtypeStruct((rows, width), bf16),
            jax.ShapeDtypeStruct((STAT, rows), f32),
            jax.ShapeDtypeStruct((STAT, rows), f32),
            jax.ShapeDtypeStruct((width, rows), f32),
        ],
        scratch_shapes=[pltpu.VMEM((width, rows), bf16), pltpu.VMEM((heads, width, TILE), bf16)],
        compiler_params=params,
        cost_estimate=cost(LIGHT * 16),
        name="own_attend",
    )(flags, inputs, weight, bias, both, both)


def far_attend(chunk, flags, queries, both, top, total, acc):
    rows, width = both.shape[0], both.shape[1] // 2
    heads = width // HEAD_SIZE
    tiles = rows // CHUNKS // TILE
    base = chunk * tiles
    return kernel_call(
        functools.partial(far_attend_kernel, base),
        grid=(tiles,),
        in_specs=[
            SMEM,
            spec_rows(width, base),
            spec_side(0, rows, width),
            spec_side(1, rows, width),
            spec_columns(STAT, base),
            spec_columns(STAT, base),
            spec_columns(width, base),
        ],
        out_specs=[spec_rows(width), spec_columns(STAT)],
        out_shape=[
            jax.ShapeDtypeStruct((tiles * TILE, width), bf16),
            jax.ShapeDtypeStruct((STAT, tiles * TILE), f32),
        ],
        scratch_shapes=[
            pltpu.VMEM((width, rows), bf16),
            pltpu.VMEM((heads, width, TILE), bf16),
            pltpu.VMEM((STAT, TILE), f32),
            pltpu.VMEM((STAT, TILE), f32),
            pltpu.VMEM((width, TILE), f32),
        ],
        compiler_params=params,
        cost_estimate=cost(LIGHT * 4),
        name="far_attend",
    )(flags, queries, both, both, top, total, acc)


def back_tiles(first, last, mask, refs, stats):
    keys, values, key_turned, query_heads, grad_heads, grad_turned, query_turned, gq, gk, gv = refs
    log_total, inner = stats
    heads = query_heads.shape[0]

    def step(key_tile, carry):
        allowed = mask(key_tile)
        place = tile_rows(key_tile)
        key_block = keys[place, :]
        value_block = values[place, :]
        scores = [nn(key_block, query_heads[head]) for head in range(heads)]
        grad_probs = [nn(value_block, grad_heads[head]) for head in range(heads)]
        probs = [
            jnp.exp(jnp.where(allowed, scores[head], masked_fill) - log_total[pl.ds(head, 1), :])
            for head in range(heads)
        ]
        grad_scores = [
            (probs[head] * (grad_probs[head] - inner[pl.ds(head, 1), :])).astype(bf16)
            for head in range(heads)
        ]
        for head in range(heads):
            rows = head_rows(head)
            gv[rows, place] += nt(grad_turned[rows, :], probs[head].astype(bf16))
            gk[rows, place] += nt(query_turned[rows, :], grad_scores[head])
            gq[rows, :] += nn(key_turned[rows, place], grad_scores[head])
        return carry

    lax.fori_loop(first, last, step, 0)


def far_back_kernel(flags, grad_rows, weight, queries, attended, log_total, keys, values, grad_att, inner, grad_q, grad_both, key_turned, query_heads, grad_heads, query_turned, grad_turned, gk, gv):
    tile = pl.program_id(0)
    cut = flags[0]

    @pl.when(tile == 0)
    def _():
        turn_all(keys, key_turned)
        gk[...] = jnp.zeros(gk.shape, f32)
        gv[...] = jnp.zeros(gv.shape, f32)

    made = nt(grad_rows[...], weight[...]).astype(bf16)
    grad_att[...] = made
    turned = turn(made)
    by_head(turned, grad_heads)
    grad_turned[...] = turned.astype(bf16)
    product = turned * turn(attended[...])
    inner[...] = jnp.zeros(inner.shape, f32)
    for head in range(query_heads.shape[0]):
        inner[pl.ds(head, 1), :] = jnp.sum(product[head * HEAD_SIZE : (head + 1) * HEAD_SIZE], axis=0, keepdims=True)
    turned = turn(queries[...])
    by_head(turned, query_heads)
    query_turned[...] = turned.astype(bf16)
    grad_q[...] = jnp.zeros(grad_q.shape, f32)
    first, last = far_tiles(tile, cut, flags[1], keys.shape[0] // TILE)
    refs = (keys, values, key_turned, query_heads, grad_heads, grad_turned, query_turned, grad_q, gk, gv)
    back_tiles(first, last, far_mask(tile, cut), refs, (log_total, inner))

    @pl.when(tile == pl.num_programs(0) - 1)
    def _():
        for part in range(keys.shape[0] // TILE):
            rows = pl.ds(part * TILE, TILE)
            width = gk.shape[0]
            grad_both[rows, :width] = jnp.transpose(gk[:, rows]).astype(bf16)
            grad_both[rows, width:] = jnp.transpose(gv[:, rows]).astype(bf16)


def far_back(flags, grad_rows, weight, queries, attended, log_total, both):
    rows, width = both.shape[0], both.shape[1] // 2
    depth = grad_rows.shape[1]
    heads = width // HEAD_SIZE
    return kernel_call(
        far_back_kernel,
        grid=(rows // TILE,),
        in_specs=[SMEM, spec_rows(depth), spec_whole(width, depth), spec_rows(width), spec_rows(width), spec_columns(STAT), spec_side(0, rows, width), spec_side(1, rows, width)],
        out_specs=[spec_rows(width), spec_columns(STAT), spec_columns(width), spec_whole(rows, 2 * width)],
        out_shape=[
            jax.ShapeDtypeStruct((rows, width), bf16),
            jax.ShapeDtypeStruct((STAT, rows), f32),
            jax.ShapeDtypeStruct((width, rows), f32),
            jax.ShapeDtypeStruct((rows, 2 * width), bf16),
        ],
        scratch_shapes=[
            pltpu.VMEM((width, rows), bf16),
            pltpu.VMEM((heads, width, TILE), bf16),
            pltpu.VMEM((heads, width, TILE), bf16),
            pltpu.VMEM((width, TILE), bf16),
            pltpu.VMEM((width, TILE), bf16),
            pltpu.VMEM((width, rows), f32),
            pltpu.VMEM((width, rows), f32),
        ],
        compiler_params=params,
        cost_estimate=cost(LIGHT * 9),
        name="far_back",
    )(flags, grad_rows, weight, queries, attended, log_total, both, both)


def own_back_kernel(flags, grad_att, inner, queries, log_total, keys, values, grad_q_in, grad_q, grad_k, grad_v, key_turned, query_heads, grad_heads, query_turned, grad_turned, gq, gk, gv):
    tile = pl.program_id(0)
    cut = flags[0]

    @pl.when(tile == 0)
    def _():
        turn_all(keys, key_turned)
        gk[...] = jnp.zeros(gk.shape, f32)
        gv[...] = jnp.zeros(gv.shape, f32)

    turned = turn(grad_att[...])
    by_head(turned, grad_heads)
    grad_turned[...] = turned.astype(bf16)
    turned = turn(queries[...])
    by_head(turned, query_heads)
    query_turned[...] = turned.astype(bf16)
    gq[...] = grad_q_in[...]
    first, last = own_tiles(tile, cut)
    refs = (keys, values, key_turned, query_heads, grad_heads, grad_turned, query_turned, gq, gk, gv)
    back_tiles(first, last, own_mask(tile, cut), refs, (log_total, inner))
    grad_q[...] = (jnp.transpose(gq[...]) * HEAD_SIZE**-0.5).astype(grad_q.dtype)

    @pl.when(tile == pl.num_programs(0) - 1)
    def _():
        for part in range(keys.shape[0] // TILE):
            rows = pl.ds(part * TILE, TILE)
            grad_k[rows, :] = jnp.transpose(gk[:, rows])
            grad_v[rows, :] = jnp.transpose(gv[:, rows])


def own_back(flags, grad_att, inner, queries, log_total, both, grad_q):
    rows, width = both.shape[0], both.shape[1] // 2
    heads = width // HEAD_SIZE
    return kernel_call(
        own_back_kernel,
        grid=(rows // TILE,),
        in_specs=[SMEM, spec_rows(width), spec_columns(STAT), spec_rows(width), spec_columns(STAT), spec_side(0, rows, width), spec_side(1, rows, width), spec_columns(width)],
        out_specs=[spec_rows(width), spec_whole(rows, width), spec_whole(rows, width)],
        out_shape=[
            jax.ShapeDtypeStruct((rows, width), bf16),
            jax.ShapeDtypeStruct((rows, width), f32),
            jax.ShapeDtypeStruct((rows, width), f32),
        ],
        scratch_shapes=[
            pltpu.VMEM((width, rows), bf16),
            pltpu.VMEM((heads, width, TILE), bf16),
            pltpu.VMEM((heads, width, TILE), bf16),
            pltpu.VMEM((width, TILE), bf16),
            pltpu.VMEM((width, TILE), bf16),
            pltpu.VMEM((width, TILE), f32),
            pltpu.VMEM((width, rows), f32),
            pltpu.VMEM((width, rows), f32),
        ],
        compiler_params=params,
        cost_estimate=cost(LIGHT * 16),
        name="own_back",
    )(flags, grad_att, inner, queries, log_total, both, both, grad_q)


def norm_parts(rows_in):
    row_mean = jnp.mean(rows_in, axis=-1, keepdims=True)
    centered = rows_in - row_mean
    inv_scale = lax.rsqrt(jnp.mean(centered * centered, axis=-1, keepdims=True) + epsilon)
    return centered * inv_scale, inv_scale


def enter_kernel(tokens, wk, wv, bias, gains, shifts, inputs, both):
    normal, _ = norm_parts(tokens[...].astype(f32))
    low = (normal * row_of(gains, 0) + row_of(shifts, 0)).astype(bf16)
    inputs[...] = low
    width = wk.shape[1]
    both[:, :width] = nn(low, wk[...]).astype(bf16)
    both[:, width:] = (nn(low, wv[...]) + row_of(bias, 1)).astype(bf16)


def enter(tokens, w_self, bias, gains, shifts):
    rows, depth = tokens.shape
    width = w_self.shape[2]
    return kernel_call(
        enter_kernel,
        grid=(rows // TILE,),
        in_specs=[
            spec_rows(depth),
            spec_layer(1, depth, width),
            spec_layer(2, depth, width),
            spec_whole(*bias.shape),
            spec_whole(*gains.shape),
            spec_whole(*shifts.shape),
        ],
        out_specs=[spec_rows(depth), spec_rows(2 * width)],
        out_shape=[
            jax.ShapeDtypeStruct((rows, depth), bf16),
            jax.ShapeDtypeStruct((rows, 2 * width), bf16),
        ],
        compiler_params=params,
        cost_estimate=cost(LIGHT * 4),
        name="enter",
    )(tokens, w_self, w_self, bias, gains, shifts)


def after_self_kernel(base, slots, flags, tokens, *refs):
    parts, weights, refs = refs[:4], refs[4:8], refs[8:]
    bias, gains, shifts, wq, bq, text_keys, text_values = refs[:7]
    after, inputs, queries, attended, log_total = refs[7:12]
    value_turned, query_heads, top, total, acc = refs[12:]
    tile = base + pl.program_id(0)

    @pl.when(pl.program_id(0) == 0)
    def _():
        turn_all(text_values, value_turned)

    product = nn(parts[0][...], weights[0][...])
    for part, weight in zip(parts[1:], weights[1:]):
        product = product + nn(part[...], weight[...])
    rows_in = tokens[...].astype(f32) + (product + row_of(bias, 0))
    after[...] = rows_in.astype(bf16)
    normal, _ = norm_parts(rows_in)
    low = (normal * row_of(gains, 1) + row_of(shifts, 1)).astype(bf16)
    inputs[...] = low
    made = (nn(low, wq[...]) + row_of(bq, 0)).astype(bf16).astype(f32) * HEAD_SIZE**-0.5
    queries[...] = made.astype(bf16)
    by_head(jnp.transpose(made), query_heads)
    top[...] = jnp.full(top.shape, masked_fill, f32)
    total[...] = jnp.zeros(total.shape, f32)
    acc[...] = jnp.zeros(acc.shape, f32)
    mask = text_mask(tile, flags[CUT], (flags[LENGTH], flags[LENGTH + 1]), slots)
    attend_tiles(0, 1, mask, text_keys, value_turned, query_heads, top, total, acc)
    log_total[...] = top[...] + jnp.log(total[...])
    for head in range(query_heads.shape[0]):
        acc[head_rows(head), :] = acc[head_rows(head), :] / total[pl.ds(head, 1), :]
    attended[...] = jnp.transpose(acc[...]).astype(bf16)


def after_self(chunk, flags, tokens, parts, weights, bias, gains, shifts, wq, bq, text_keys, text_values):
    rows, depth = tokens.shape
    width = wq.shape[1]
    heads = width // HEAD_SIZE
    window = text_keys.shape[0]
    assert window == TILE
    tiles = rows // CHUNKS // TILE
    base = chunk * tiles
    part_rows = tiles * TILE
    return kernel_call(
        functools.partial(after_self_kernel, base, window // 2),
        grid=(tiles,),
        in_specs=[SMEM, spec_rows(depth, base)]
        + [spec_rows(width)] * 4
        + [spec_whole(width, depth)] * 4
        + [spec_whole(*bias.shape)] * 3
        + [spec_whole(depth, width), spec_whole(*bq.shape)]
        + [spec_whole(window, width)] * 2,
        out_specs=[
            spec_rows(depth),
            spec_rows(depth),
            spec_rows(width),
            spec_rows(width),
            spec_columns(STAT),
        ],
        out_shape=[
            jax.ShapeDtypeStruct((part_rows, depth), bf16),
            jax.ShapeDtypeStruct((part_rows, depth), bf16),
            jax.ShapeDtypeStruct((part_rows, width), bf16),
            jax.ShapeDtypeStruct((part_rows, width), bf16),
            jax.ShapeDtypeStruct((STAT, part_rows), f32),
        ],
        scratch_shapes=[
            pltpu.VMEM((width, window), bf16),
            pltpu.VMEM((heads, width, TILE), bf16),
            pltpu.VMEM((STAT, TILE), f32),
            pltpu.VMEM((STAT, TILE), f32),
            pltpu.VMEM((width, TILE), f32),
        ],
        compiler_params=params,
        cost_estimate=cost(LIGHT * 7),
        name="after_self",
    )(flags, tokens, *parts, *weights, bias, gains, shifts, wq, bq, text_keys, text_values)


def split_store(flags, tile, half_tiles, block, sent, kept):
    place = pl.ds(pl.multiple_of((tile % half_tiles) * TILE, TILE), TILE)
    own = tile // half_tiles == flags[CORE]

    @pl.when(own)
    def _():
        kept[place, :] = block

    @pl.when(jnp.logical_not(own))
    def _():
        sent[place, :] = block


def after_cross_kernel(half_tiles, flags, rows_ref, *refs):
    parts, weights, refs = refs[:4], refs[4:8], refs[8:]
    grad_hidden, w_up, b_up, bias, gains, shifts = refs[:6]
    after, inputs, hidden, grad_pre, sent, kept = refs[-6:]
    product = nn(parts[0][...], weights[0][...])
    for part, weight in zip(parts[1:], weights[1:]):
        product = product + nn(part[...], weight[...])
    rows_in = rows_ref[...].astype(f32) + (product + row_of(bias, 1))
    after[...] = rows_in
    normal, _ = norm_parts(rows_in)
    low = (normal * row_of(gains, 2) + row_of(shifts, 2)).astype(bf16)
    inputs[...] = low
    pre = nn(low, w_up[...]) + row_of(b_up, 0)
    square = pre * pre
    root = (2 / jnp.pi) ** 0.5
    bent = jnp.tanh(root * (pre + 0.044715 * (square * pre)))
    hidden[...] = (0.5 * pre * (1 + bent)).astype(bf16)
    slope = 0.5 * (1 + bent) + (0.5 * root) * pre * (1 - bent * bent) * (1 + 0.134145 * square)
    low_grad = (slope * grad_hidden[...].astype(f32)).astype(bf16)
    grad_pre[...] = low_grad
    block = nt(low_grad, w_up[...]).astype(bf16)
    split_store(flags, pl.program_id(0), half_tiles, block, sent, kept)


ANY = pl.BlockSpec(memory_space=pl.ANY)


def after_cross(chunk, flags, rows_in, parts, weights, grad_hidden, w_up, b_up, bias, gains, shifts, wholes):
    part_rows, depth = rows_in.shape
    width = parts[0].shape[1]
    units = w_up.shape[1]
    tiles = part_rows // TILE
    base = chunk * tiles
    rows = part_rows * CHUNKS
    operands = (flags, rows_in, *parts, *weights, grad_hidden, w_up, b_up, bias, gains, shifts)
    aliases = {len(operands) + place: 1 + place for place in range(len(wholes))}
    return kernel_call(
        functools.partial(after_cross_kernel, tiles // 2),
        grid=(tiles,),
        in_specs=[SMEM, spec_rows(depth)]
        + [spec_rows(width)] * 4
        + [spec_whole(width, depth)] * 4
        + [spec_rows(units, base), spec_whole(depth, units), spec_whole(1, units)]
        + [spec_whole(*bias.shape)] * 3
        + [ANY] * len(wholes),
        out_specs=[
            spec_rows(depth),
            spec_rows(depth, base),
            spec_rows(units, base),
            spec_rows(units, base),
            spec_whole(part_rows // 2, depth),
            spec_whole(part_rows // 2, depth),
        ],
        out_shape=[
            jax.ShapeDtypeStruct((part_rows, depth), f32),
            jax.ShapeDtypeStruct((rows, depth), bf16),
            jax.ShapeDtypeStruct((rows, units), bf16),
            jax.ShapeDtypeStruct((rows, units), bf16),
            jax.ShapeDtypeStruct((part_rows // 2, depth), bf16),
            jax.ShapeDtypeStruct((part_rows // 2, depth), bf16),
        ],
        input_output_aliases=aliases,
        compiler_params=params,
        cost_estimate=cost(LIGHT * 10),
        name="after_cross",
    )(*operands, *wholes)


def split_product_kernel(half_tiles, turned, flags, *refs):
    count = (len(refs) - 2) // 2
    product = nt if turned else nn
    block = product(refs[0][...], refs[count][...])
    for place in range(1, count):
        block = block + product(refs[place][...], refs[count + place][...])
    split_store(flags, pl.program_id(0), half_tiles, block.astype(bf16), *refs[-2:])


def split_product(chunk, flags, lefts, rights, turned):
    part_rows = lefts[0].shape[0] // CHUNKS
    depth = rights[0].shape[-2 if turned else -1]
    tiles = part_rows // TILE
    width = lefts[0].shape[1]
    half = jax.ShapeDtypeStruct((part_rows // 2, depth), bf16)
    return kernel_call(
        functools.partial(split_product_kernel, tiles // 2, turned),
        grid=(tiles,),
        in_specs=[SMEM]
        + [spec_rows(width, chunk * tiles)] * len(lefts)
        + [
            spec_whole(*right.shape) if right.ndim == 2 else spec_layer(layer, *right.shape[1:])
            for layer, right in enumerate(rights)
        ],
        out_specs=[spec_whole(part_rows // 2, depth)] * 2,
        out_shape=[half, half],
        compiler_params=params,
        cost_estimate=cost(LIGHT * 2.3),
        name="split_product",
    )(flags, *lefts, *rights)


def scatter_halves(sent, kept, quarter):
    both = kept.astype(f32) + swapped(sent, "tensor", 1).astype(f32)
    rows = sent.shape[0] // 2
    place = (quarter & 1) * rows
    other = lax.dynamic_slice_in_dim(both, rows - place, rows, 0).astype(bf16)
    return lax.dynamic_slice_in_dim(both, place, rows, 0), swapped(other, "tensor", 2)


def first_add_kernel(flags, arrived, kept, own, other):
    both = kept[...].astype(f32) + arrived[...].astype(f32)
    rows = own.shape[0]
    for second in range(2):

        @pl.when((flags[QUARTER] & 1) == second)
        def _(second=second):
            own[...] = both[second * rows : (second + 1) * rows]
            other[...] = both[(1 - second) * rows : (2 - second) * rows].astype(bf16)


def first_add(flags, arrived, kept):
    rows, depth = kept.shape[0] // 2, kept.shape[1]
    return kernel_call(
        first_add_kernel,
        in_specs=[SMEM] + [pl.BlockSpec(memory_space=pltpu.VMEM)] * 2,
        out_specs=[pl.BlockSpec(memory_space=pltpu.VMEM)] * 2,
        out_shape=[
            jax.ShapeDtypeStruct((rows, depth), f32),
            jax.ShapeDtypeStruct((rows, depth), bf16),
        ],
        compiler_params=small,
        cost_estimate=cost(LIGHT * 1.3),
        name="first_add",
    )(flags, arrived, kept)


def quarter_of(rel):
    return (rel & 1) * 2 + (rel >> 1)


def norm_back_rows_kernel(gain_row, flags, kept, arrived, source, residual, gains, result, sums):
    grad = kept[...] + arrived[...].astype(f32)
    normal, inv_scale = norm_parts(source[...].astype(f32))
    sums[...] = jnp.zeros(sums.shape, f32)
    sums[0:1, :] = jnp.sum(grad * normal, axis=0, keepdims=True)
    sums[1:2, :] = jnp.sum(grad, axis=0, keepdims=True)
    back = norm_back(grad, normal, inv_scale, row_of(gains, gain_row))
    result[...] = (residual[...].astype(f32) + back).astype(bf16)


def norm_back_rows(chunk, gain_row, flags, kept, arrived, source, residual, gains):
    rows, depth = kept.shape
    source_base = 4 * chunk if source.shape[0] > 4 * rows else 0

    def at(base):
        return pl.BlockSpec((rows, depth), lambda step, flags: (base + flags[QUARTER], 0))

    def whole(*shape):
        return pl.BlockSpec(shape, lambda step, flags: (0, 0))

    return kernel_call(
        functools.partial(norm_back_rows_kernel, gain_row),
        prefetch=1,
        grid=(1,),
        in_specs=[
            whole(rows, depth),
            whole(rows, depth),
            at(source_base),
            at(4 * chunk),
            whole(*gains.shape),
        ],
        out_specs=[whole(rows, depth), whole(STAT, depth)],
        out_shape=[
            jax.ShapeDtypeStruct((rows, depth), bf16),
            jax.ShapeDtypeStruct((STAT, depth), f32),
        ],
        compiler_params=small,
        cost_estimate=cost(LIGHT * 1.7),
        name="norm_back_rows",
    )(flags, kept, arrived, source, residual, gains)


def cross_back_kernel(base, slots, flags, *refs):
    pieces, refs = refs[:4], refs[4:]
    weight, queries, attended, log_total, text_keys, text_values = refs[:6]
    grad_rows, grad_q, grad_k, grad_v = refs[6:10]
    key_turned, query_heads, grad_heads, query_turned, grad_turned, inner, gq, gk, gv = refs[10:]
    step = pl.program_id(0)
    tile = base + step

    @pl.when(step == 0)
    def _():
        rows = pieces[0].shape[0]
        for rel, piece in enumerate(pieces):
            start = pl.multiple_of((flags[QUARTER] ^ quarter_of(rel)) * rows, rows)
            grad_rows[pl.ds(start, rows), :] = piece[...]
        turn_all(text_keys, key_turned)
        gk[...] = jnp.zeros(gk.shape, f32)
        gv[...] = jnp.zeros(gv.shape, f32)

    made = nt(grad_rows[tile_rows(step), :], weight[...]).astype(bf16)
    turned = turn(made)
    by_head(turned, grad_heads)
    grad_turned[...] = turned.astype(bf16)
    product = turned * turn(attended[...])
    for head in range(query_heads.shape[0]):
        part = product[head * HEAD_SIZE : (head + 1) * HEAD_SIZE]
        inner[pl.ds(head, 1), :] = jnp.sum(part, axis=0, keepdims=True)
    turned = turn(queries[...])
    by_head(turned, query_heads)
    query_turned[...] = turned.astype(bf16)
    gq[...] = jnp.zeros(gq.shape, f32)
    mask = text_mask(tile, flags[CUT], (flags[LENGTH], flags[LENGTH + 1]), slots)
    refs = (text_keys, text_values, key_turned, query_heads, grad_heads, grad_turned, query_turned, gq, gk, gv)
    back_tiles(0, 1, mask, refs, (log_total, inner))
    grad_q[...] = (jnp.transpose(gq[...]) * HEAD_SIZE**-0.5).astype(bf16)

    @pl.when(step == pl.num_programs(0) - 1)
    def _():
        grad_k[...] = jnp.transpose(gk[...])
        grad_v[...] = jnp.transpose(gv[...])


def cross_back(chunk, flags, pieces, weight, queries, attended, log_total, text_keys, text_values):
    part_rows, width = queries.shape
    depth = weight.shape[1]
    heads = width // HEAD_SIZE
    window = text_keys.shape[0]
    tiles = part_rows // TILE
    return kernel_call(
        functools.partial(cross_back_kernel, chunk * tiles, window // 2),
        grid=(tiles,),
        in_specs=[SMEM]
        + [spec_whole(part_rows // 4, depth)] * 4
        + [spec_whole(width, depth), spec_rows(width), spec_rows(width), spec_columns(STAT)]
        + [spec_whole(window, width)] * 2,
        out_specs=[
            spec_whole(part_rows, depth),
            spec_rows(width),
            spec_whole(window, width),
            spec_whole(window, width),
        ],
        out_shape=[
            jax.ShapeDtypeStruct((part_rows, depth), bf16),
            jax.ShapeDtypeStruct((part_rows, width), bf16),
            jax.ShapeDtypeStruct((window, width), f32),
            jax.ShapeDtypeStruct((window, width), f32),
        ],
        scratch_shapes=[
            pltpu.VMEM((width, window), bf16),
            pltpu.VMEM((heads, width, TILE), bf16),
            pltpu.VMEM((heads, width, TILE), bf16),
            pltpu.VMEM((width, TILE), bf16),
            pltpu.VMEM((width, TILE), bf16),
            pltpu.VMEM((STAT, TILE), f32),
            pltpu.VMEM((width, TILE), f32),
            pltpu.VMEM((width, window), f32),
            pltpu.VMEM((width, window), f32),
        ],
        compiler_params=params,
        cost_estimate=cost(LIGHT * 6),
        name="cross_back",
    )(flags, *pieces, weight, queries, attended, log_total, text_keys, text_values)


def back_to_self_kernel(*refs):
    parts, weights, refs = refs[:4], refs[4:8], refs[8:]
    source, residual, gains = refs[:3]
    result, sums = refs[-2:]
    grad = nt(parts[0][...], weights[0][...])
    for part, weight in zip(parts[1:], weights[1:]):
        grad = grad + nt(part[...], weight[...])
    normal, inv_scale = norm_parts(source[...].astype(f32))
    coming = residual[...].astype(f32)
    low = (coming + norm_back(grad, normal, inv_scale, row_of(gains, 1))).astype(bf16)
    result[...] = low

    @pl.when(pl.program_id(0) == 0)
    def _():
        sums[...] = jnp.zeros(sums.shape, f32)

    for row, term in enumerate((grad * normal, grad, low.astype(f32), coming)):
        sums[row : row + 1, :] += jnp.sum(term, axis=0, keepdims=True)


def back_to_self(chunk, parts, weights, source, residual, gains, wholes):
    part_rows, depth = source.shape
    width = parts[0].shape[1]
    tiles = part_rows // TILE
    operands = (*parts, *weights, source, residual, gains)
    return kernel_call(
        back_to_self_kernel,
        grid=(tiles,),
        in_specs=[spec_rows(width)] * 4
        + [spec_whole(depth, width)] * 4
        + [spec_rows(depth), spec_rows(depth), spec_whole(*gains.shape)]
        + [ANY] * len(wholes),
        out_specs=[spec_rows(depth, chunk * tiles), spec_whole(STAT, depth)],
        out_shape=[
            jax.ShapeDtypeStruct((part_rows * CHUNKS, depth), bf16),
            jax.ShapeDtypeStruct((STAT, depth), f32),
        ],
        input_output_aliases={len(operands) + place: place for place in range(len(wholes))},
        compiler_params=params,
        cost_estimate=cost(LIGHT * 5),
        name="back_to_self",
    )(*operands, *wholes)


def place_quarters_kernel(flags, *refs):
    for place, piece in enumerate(refs[:-1]):

        @pl.when(pl.program_id(0) == place)
        def _(piece=piece):
            refs[-1][...] = piece[...].astype(refs[-1].dtype)


def place_quarters(flags, chunks, dtype):
    rows, depth = chunks[0][0].shape
    pieces = [piece for chunk in chunks for piece in chunk]
    return kernel_call(
        place_quarters_kernel,
        prefetch=1,
        grid=(len(pieces),),
        in_specs=[pl.BlockSpec((rows, depth), lambda step, flags: (0, 0))] * len(pieces),
        out_specs=pl.BlockSpec(
            (rows, depth),
            lambda step, flags: (step // 4 * 4 + (flags[QUARTER] ^ quarter_of(step % 4)), 0),
        ),
        out_shape=jax.ShapeDtypeStruct((rows * len(pieces), depth), dtype),
        compiler_params=small,
        cost_estimate=cost(LIGHT * 5),
        name="place_quarters",
    )(flags, *pieces)


def place_relative_kernel(turned, places, held, arrived, *results):
    step = pl.program_id(0)
    half = pl.num_programs(0) // 2
    each = pl.num_programs(0) // len(results)
    piece = step ^ places[0]

    def store(source):
        for place, result in enumerate(results):

            @pl.when(step // each == place)
            def _(result=result, place=place):
                if place < turned:
                    result[...] = turn(source[0])
                    return
                if result.ndim == 2:
                    result[...] = source[0].astype(f32)
                    return
                width = result.shape[2]
                for part in range(result.shape[0]):
                    result[part] = source[0, :, part * width : (part + 1) * width].astype(f32)

    @pl.when(piece < half)
    def _():
        store(held)

    @pl.when(piece >= half)
    def _():
        store(arrived)


def place_relative(place, held, arrived, parts, stacked, turned):
    count, rows, width = held.shape
    each = 2 * count // stacked
    if turned and rows % 128:
        results = place_relative(place, held, arrived, parts, stacked, 0)
        return [jnp.transpose(part) for part in results[:turned]] + list(results[turned:])
    if parts > 1:
        out_specs = [pl.BlockSpec((parts, rows, width // parts), lambda step, place: (0, step, 0))]
        shape = [jax.ShapeDtypeStruct((parts, 2 * count * rows, width // parts), f32)]
    else:
        out_specs = [
            pl.BlockSpec(
                (rows, width),
                lambda step, place, first=number * each: (jnp.clip(step - first, 0, each - 1), 0),
            )
            for number in range(stacked)
        ]
        shape = [jax.ShapeDtypeStruct((each * rows, width), f32)] * stacked
    for number in range(turned):
        out_specs[number] = pl.BlockSpec(
            (width, rows),
            lambda step, place, first=number * each: (0, jnp.clip(step - first, 0, each - 1)),
        )
        shape[number] = jax.ShapeDtypeStruct((width, each * rows), f32)
    piece = pl.BlockSpec((1, rows, width), lambda step, place: ((step ^ place[0]) % count, 0, 0))
    return kernel_call(
        functools.partial(place_relative_kernel, turned),
        prefetch=1,
        grid=(2 * count,),
        in_specs=[piece, piece],
        out_specs=out_specs,
        out_shape=shape,
        compiler_params=small,
        cost_estimate=cost(LIGHT * 5),
        name="place_relative",
    )(place, held, arrived)


def halving_orders(bits):
    return list(range(bits)), [1, 0] + list(range(2, bits))


class HalvingSum:
    def __init__(self):
        self.orders = halving_orders(axis_bits("seq"))
        self.odd = lax.axis_index("tensor") & 1
        self.mine = []
        for even, odd in zip(*self.orders):
            self.mine.append(jnp.where(self.odd == 0, rank_bit("seq", even), rank_bit("seq", odd)))
        place = 0
        for mine in self.mine:
            place = place * 2 + mine
        self.place = jnp.reshape(place, (1,)).astype(jnp.int32)

    def swap(self, value, level):
        count = lax.axis_size("tensor")
        pairs = []
        for seq in range(lax.axis_size("seq")):
            for tensor in range(count):
                partner = seq ^ (1 << self.orders[tensor & 1][level])
                pairs.append((seq * count + tensor, partner * count + tensor))
        return lax.ppermute(value, ("seq", "tensor"), pairs)

    def scatter(self, held, level):
        rows = held.shape[0] // 2
        mine = self.mine[level]
        sent = lax.dynamic_slice_in_dim(held, (1 - mine) * rows, rows, 0)
        arrived = self.swap(sent, level)
        kept = lax.dynamic_slice_in_dim(held, mine * rows, rows, 0)
        return (kept.astype(f32) + arrived.astype(f32)).astype(bf16)

    def gather(self, held, level):
        return jnp.concatenate((held, self.swap(held, level)))

    def gathers(self, order, value):
        state = {"held": value}
        count = len(self.mine)

        def join(level, held, arrived):
            held = jnp.concatenate((held, arrived))
            state["held"] = held
            if level > 0:
                state["arrived"] = self.swap(held, level - 1)
            return held

        state["arrived"] = self.swap(value, count - 1)
        for level in reversed(range(count)):
            yield functools.partial(join, level), state, order

    def steps(self, order, value, parts=1, stacked=1, turned=0):
        state = {"held": value}
        count = len(self.mine)

        def scatter_send(level):
            rows = state["held"].shape[0] // 2
            mine = self.mine[level]
            sent = lax.dynamic_slice_in_dim(state["held"], (1 - mine) * rows, rows, 0)
            state["arrived"] = self.swap(sent, level)

        def scatter_add(level, held, arrived):
            rows = held.shape[0] // 2
            kept = lax.dynamic_slice_in_dim(held, self.mine[level] * rows, rows, 0)
            held = (kept.astype(f32) + arrived.astype(f32)).astype(bf16)
            state["held"] = held
            if level + 1 < count:
                scatter_send(level + 1)
            else:
                state["held"] = held[None]
                state["arrived"] = self.swap(state["held"], level)
            return held

        def gather_join(level, held, arrived):
            held = jnp.concatenate((held, arrived))
            state["held"] = held
            state["arrived"] = self.swap(held, level - 1)
            return held

        def finish(held, arrived):
            return place_relative(self.place, held, arrived, parts, stacked, turned)

        scatter_send(0)
        for level in range(count):
            yield functools.partial(scatter_add, level), state, order
        for level in reversed(range(1, count)):
            yield functools.partial(gather_join, level), state, order
        yield finish, state, order.kernel


def text_sums_kernel(flags, windows, grad_k, grad_v):
    count, _, _, slots, _ = windows.shape
    bits = (count - 1).bit_length()
    odd = flags[CORE]

    def place_of(rank, odd):
        place = 0
        for even_bit, odd_bit in zip(*halving_orders(bits)):
            place = place * 2 + ((rank >> (even_bit + (odd_bit - even_bit) * odd)) & 1)
        return place

    own = place_of(flags[SEQ], odd)
    places = [place_of(owner, odd) ^ own for owner in range(count)]
    for item in range(count + 1):
        for kind, result in enumerate((grad_k, grad_v)):
            total = jnp.zeros((slots, result.shape[1]), f32)
            if item < count:
                total = windows[places[item], kind, 0].astype(f32)
            if item > 0:
                total = total + windows[places[item - 1], kind, 1].astype(f32)
            result[item * slots : (item + 1) * slots] = total.astype(bf16)


def text_sums(flags, windows):
    count, _, _, slots, width = windows.shape
    shape = ((count + 1) * slots, width)
    return kernel_call(
        text_sums_kernel,
        grid=(1,),
        in_specs=[SMEM, spec_whole(*windows.shape)],
        out_specs=[spec_whole(*shape)] * 2,
        out_shape=[jax.ShapeDtypeStruct(shape, bf16)] * 2,
        compiler_params=params,
        cost_estimate=cost(LIGHT * 2),
        name="text_sums",
    )(flags, windows)


def per_device(
    tokens,
    item_ids,
    text_states,
    text_lengths,
    norm_gain,
    norm_shift,
    w_self,
    b_self,
    w_self_out,
    w_cross_q,
    w_cross_kv,
    b_cross,
    w_cross_out,
    w_up,
    b_up,
    w_down,
    out_bias,
    d_out,
):
    row_count = tokens.shape[0]
    assert row_count == ITEM_LEN and lax.axis_size("tensor") == 4
    local_width = w_self.shape[2]
    seq_rank = lax.axis_index("seq")
    tensor_rank = lax.axis_index("tensor")
    quarter = quarter_of(tensor_rank)
    item_total, slot_count = text_states.shape[:2]
    slot_total = item_total * slot_count
    cut = jnp.sum((item_ids == 0).astype(jnp.int32))
    item_lengths = lax.dynamic_slice_in_dim(text_lengths, seq_rank, 2)
    flags = jnp.stack(
        (
            cut,
            (seq_rank > 0).astype(jnp.int32),
            item_lengths[0],
            item_lengths[1],
            quarter,
            tensor_rank & 1,
            seq_rank,
        )
    )
    chunks = range(CHUNKS)
    halving_sum = HalvingSum()

    def local_cols(full_rows):
        return lax.dynamic_slice_in_dim(full_rows, tensor_rank * local_width, local_width, axis=1)

    def token_sum(rows_in):
        return jnp.sum(rows_in.astype(f32), axis=0)

    order = Order()
    gains, shifts, biases = norm_gain, norm_shift, out_bias
    inputs_one, both = order.kernel(enter, tokens, w_self, b_self, gains, shifts)
    both_far = shifted(both, "seq", 1)
    late = tied((w_self_out, w_cross_out), both)
    crossing = [swapped(late[0], "tensor", 2), swapped(late[1], "tensor", 2)]
    queries, top, total, acc = order.kernel(
        own_attend, flags, inputs_one, w_self, b_self, both
    )

    text_flat = text_states.reshape(slot_total, text_states.shape[2])
    text_window = lax.dynamic_slice_in_dim(text_flat, seq_rank * slot_count, 2 * slot_count, 0)

    def project_text(window, key_weight, value_weight, bias):
        text_keys = matmul_low(window, key_weight).astype(bf16)
        return text_keys, (matmul_low(window, value_weight) + bias.astype(f32)).astype(bf16)

    text_keys, text_values = order(
        project_text, text_window, w_cross_kv[0], w_cross_kv[1], b_cross[1]
    )
    grad_hidden = order(
        lambda grad, weight: times_transpose(grad, weight).astype(bf16), d_out, w_down
    )
    attended, log_total, after_one, inputs_two, cross_queries, cross_attended, cross_log = (
        [] for _ in range(7)
    )
    operands = (flags, queries, both_far, top, total, acc)
    first = order.kernel(functools.partial(far_attend, 0), *operands)
    across = [swapped(first[0], "tensor", 2)]
    second, across = order.kernel(functools.partial(far_attend, 1), *operands, during=across)
    attended, log_total = zip(first, second)
    across = [*across, swapped(attended[1], "tensor", 2)]
    crossing = tied(crossing, attended[-1])
    self_out, cross_out = (
        [own, swapped(own, "tensor", 1), across, swapped(across, "tensor", 1)]
        for own, across in zip(late, crossing)
    )
    after_one, inputs_two, cross_queries, cross_attended, cross_log = ([] for _ in range(5))

    def keep(made, *lists):
        for held, part in zip(lists, made):
            held.append(part)

    def run_after_self(chunk, across, during):
        return order.kernel(
            lambda *operands: after_self(
                chunk, *operands[:2], operands[2:6], operands[6:10], *operands[10:]
            ),
            flags,
            tokens,
            *gathered(attended[chunk], across),
            *self_out,
            biases,
            gains,
            shifts,
            w_cross_q,
            b_cross,
            text_keys,
            text_values,
            during=during,
        )

    made, (across_next,) = run_after_self(0, across[0], [across[1]])
    keep(made, after_one, inputs_two, cross_queries, cross_attended, cross_log)
    across = swapped(cross_attended[0], "tensor", 2)
    made, (across,) = run_after_self(1, across_next, [across])
    keep(made, after_one, inputs_two, cross_queries, cross_attended, cross_log)
    across_next = swapped(cross_attended[1], "tensor", 2)

    def low_rows(left, right):
        return contract_rows(left, right).astype(bf16)

    def products(*operands):
        return jnp.concatenate(
            [low_rows(left, right) for left, right in zip(operands[::2], operands[1::2])]
        )

    def scatter_first(chunk_halves):
        arrived = swapped(chunk_halves[0], "tensor", 1)
        kept, other = order.kernel(first_add, flags, arrived, chunk_halves[1])
        return kept, swapped(other, "tensor", 2)

    ready = {}

    def advance(*lanes):
        for lane in lanes:
            step, state, run = next(lane, (None, None, None))
            if step is not None:
                ready[id(lane)] = run(step, state["held"], state["arrived"])

    def begun(lane):
        first = next(lane)

        def rest():
            yield first
            yield from lane

        return rest()

    def run_after_cross(chunk, across, wholes, during):
        return order.kernel(
            lambda *operands: after_cross(
                chunk, *operands[:2], operands[2:6], operands[6:10], *operands[10:16], operands[16:]
            ),
            flags,
            after_one[chunk],
            *gathered(cross_attended[chunk], across),
            *cross_out,
            grad_hidden,
            w_up,
            b_up[None],
            biases,
            gains,
            shifts,
            *wholes,
            during=during,
        )

    made, (across,) = run_after_cross(0, across, (), [across_next])
    after_two = [made[0]]
    late_across = swapped(tied(w_cross_q, across), "tensor", 2)
    kept, other = scatter_first(made[4:])
    made, (other, late_across) = run_after_cross(1, across, made[1:4], [other, late_across])
    after_two.append(made[0])
    inputs_three, hidden, grad_pre = made[1:4]
    all_cross_q = gathered(w_cross_q, late_across)
    kept_next, other_next = scatter_first(made[4:])

    def norm_step(chunk, kept, other):
        return order.kernel(
            functools.partial(norm_back_rows, chunk, 2),
            flags,
            kept,
            other,
            after_two[chunk],
            d_out,
            gains,
        )

    shard, sums = norm_step(0, kept, other)
    shards, shard_sums_three = [shard], [sums]
    across = swapped(shard, "tensor", 2)
    mlp_grads, (other_next,) = order(
        products, hidden, d_out, inputs_three, grad_pre, during=[other_next]
    )
    mlp_shard = lax.psum_scatter(mlp_grads, "seq", scatter_dimension=0, tiled=True)
    early_sums = order(
        lambda left, right: [token_sum(local_cols(left)), token_sum(right)], d_out, grad_pre
    )
    shard, sums = norm_step(1, kept_next, other_next)
    shards.append(shard)
    shard_sums_three.append(sums)
    across_next = swapped(shard, "tensor", 2)

    def run_cross_back(chunk, across, during):
        return order.kernel(
            lambda *operands: cross_back(chunk, operands[0], operands[1:5], *operands[5:]),
            flags,
            *gathered(shards[chunk], across),
            w_cross_out,
            cross_queries[chunk],
            cross_attended[chunk],
            cross_log[chunk],
            text_keys,
            text_values,
            during=during,
        )

    grad_cross_low, grad_cross_q, text_key_parts, text_value_parts = ([] for _ in range(4))
    made, (across,) = run_cross_back(0, across, [across_next])
    keep(made, grad_cross_low, grad_cross_q, text_key_parts, text_value_parts)
    across_next = swapped(grad_cross_q[0], "tensor", 2)
    made, (across,) = run_cross_back(1, across, [across_next])
    keep(made, grad_cross_low, grad_cross_q, text_key_parts, text_value_parts)
    across_next = swapped(grad_cross_q[1], "tensor", 2)

    def text_windows(*parts):
        both = jnp.stack((sum(parts[:CHUNKS]), sum(parts[CHUNKS:]))).astype(bf16)
        return both.reshape(1, 2, 2, slot_count, local_width)

    text_lane = order(text_windows, *text_key_parts, *text_value_parts)
    text_lane = begun(halving_sum.gathers(order, text_lane))

    def output_product(chunk, source, weight):
        return split_product(chunk, flags, (source,), (weight,), False)

    first_output, (across_next,) = order.kernel(
        functools.partial(output_product, 0), hidden, w_down, during=[across_next]
    )

    def run_back_to_self(chunk, across, wholes, during=()):
        return order.kernel(
            lambda *operands: back_to_self(
                chunk, operands[:4], operands[4:8], *operands[8:11], operands[11:]
            ),
            *gathered(grad_cross_q[chunk], across),
            *all_cross_q,
            after_one[chunk],
            grad_cross_low[chunk],
            gains,
            *wholes,
            during=during,
        )

    whole, sums = run_back_to_self(0, across, ())
    row_sums = [sums]
    grad_self_low, sums = run_back_to_self(1, across_next, (whole,))
    row_sums.append(sums)
    advance(text_lane)

    def joined(*parts):
        return [jnp.concatenate(parts[k : k + CHUNKS]) for k in range(0, len(parts), CHUNKS)]

    attended, log_rows = order(
        lambda *parts: joined(*parts[:CHUNKS]) + [jnp.concatenate(parts[CHUNKS:], axis=1)],
        *attended,
        *log_total,
    )
    grad_att, inner, grad_q, grad_far = order.kernel(
        far_back, flags, grad_self_low, w_self_out, queries, attended, log_rows, both_far
    )
    carried = shifted(grad_far, "seq", -1)
    advance(text_lane)
    (grad_queries, grad_keys, grad_values), (mlp_shard,) = order.kernel(
        own_back,
        flags,
        grad_att,
        inner,
        queries,
        log_rows,
        both,
        grad_q,
        during=[mlp_shard],
    )
    mlp_sums = lax.all_gather(mlp_shard, "seq", tiled=True)
    joins = order(joined, *grad_cross_q, *inputs_two, *cross_attended, *grad_cross_low)
    cross_grads = order(products, *joins, attended, grad_self_low)

    def add_carried(grad_keys, grad_values, carried):
        return (
            (grad_keys + carried[:, :local_width].astype(f32)).astype(bf16),
            (grad_values + carried[:, local_width:].astype(f32)).astype(bf16),
        )

    grad_keys, grad_values = order(add_carried, grad_keys, grad_values, carried)

    def self_products(inputs, *grads):
        return jnp.concatenate([low_rows(inputs, grad) for grad in grads], axis=1)

    self_grads = order(self_products, inputs_one, grad_queries, grad_keys, grad_values)
    self_lane = begun(halving_sum.steps(order, self_grads, 3))

    def token_product(chunk, *operands):
        return split_product(chunk, flags, operands[:3], operands[3:], True)

    token_terms = []
    for chunk in chunks:
        made = order.kernel(
            functools.partial(token_product, chunk),
            grad_queries,
            grad_keys,
            grad_values,
            w_self,
            w_self,
            w_self,
        )
        token_terms.append(scatter_first(made))
    for _ in range(axis_bits("seq")):
        advance(text_lane)
    grad_text_keys, grad_text_values = order.kernel(
        functools.partial(text_sums, flags), ready[id(text_lane)]
    )

    def text_grads(grad_text_keys, grad_text_values):
        part = times_transpose(grad_text_keys, w_cross_kv[0]) + times_transpose(
            grad_text_values, w_cross_kv[1]
        )
        return part.astype(bf16)

    grad_text_part, others = order(
        text_grads,
        grad_text_keys,
        grad_text_values,
        during=[other for _, other in token_terms],
    )
    shard_sums_one, token_shards = [], []
    for chunk in chunks:
        shard, sums = order.kernel(
            functools.partial(norm_back_rows, chunk, 0),
            flags,
            token_terms[chunk][0],
            others[chunk],
            tokens,
            grad_self_low,
            gains,
        )
        shard_sums_one.append(sums)
        token_shards.append(shard)
    token_across = [swapped(shard, "tensor", 2) for shard in token_shards]
    grad_text_shard = scatter_rows(grad_text_part, "tensor").astype(bf16)

    def norm_sums(*parts):
        return jnp.concatenate((sum(parts[:CHUNKS])[:2], sum(parts[CHUNKS:])[:2]))

    shard_sums = order(norm_sums, *shard_sums_one, *shard_sums_three)
    shard_sums = scatter_columns(shard_sums, "tensor")
    second_output, token_across = order.kernel(
        functools.partial(output_product, 1), hidden, w_down, during=token_across
    )
    output_terms = [scatter_first(first_output), scatter_first(second_output)]
    advance(self_lane)

    def vector_rows(cross_grads, shard_sums, sum_d_out, sum_pre, cross_q, queries, values, *row_sums):
        rows = local_cols(sum(row_sums)[:4])
        vectors = jnp.concatenate(
            (
                shard_sums[:1],
                rows[:1],
                shard_sums[2:3],
                shard_sums[1:2],
                rows[1:2],
                shard_sums[3:],
                rows[2:],
                sum_d_out[None],
                jnp.stack((token_sum(cross_q), token_sum(queries), token_sum(values))),
                sum_pre.reshape(-1, local_width),
            )
        )
        vectors = vectors.astype(bf16).reshape(-1, cross_grads.shape[1])
        spare = jnp.zeros((PAD - vectors.shape[0], cross_grads.shape[1]), bf16)
        return jnp.concatenate((cross_grads, vectors, spare))

    cross_grads = order(
        vector_rows,
        cross_grads,
        shard_sums,
        *early_sums,
        joins[0],
        grad_queries,
        grad_values,
        *row_sums,
    )
    cross_lane = begun(halving_sum.steps(order, cross_grads, stacked=4, turned=1))
    advance(self_lane)
    grad_text_shard = tied(grad_text_shard, order.pending)
    grad_text_across = swapped(grad_text_shard, "tensor", 2)
    advance(self_lane)

    def output_shard(kept, other, rows_in):
        rows = kept.shape[0]
        base = lax.dynamic_slice_in_dim(rows_in, quarter * rows, rows, 0)
        return (base + ((kept + other.astype(f32)) + biases[2].astype(f32))).astype(bf16)

    output_shards = [
        order(output_shard, *output_terms[chunk], after_two[chunk]) for chunk in chunks
    ]
    output_across = [swapped(shard, "tensor", 2) for shard in output_shards]
    pieces = [gathered(token_shards[chunk], token_across[chunk]) for chunk in chunks]
    advance(cross_lane)
    def wide_sums(sums):
        half = sums.shape[0] // 2
        return [sums[:half].astype(f32), sums[half:].astype(f32)]

    sum_w_down, sum_w_up = order(wide_sums, mlp_sums)
    grad_tokens = order.kernel(
        lambda *pieces: place_quarters(flags, (pieces[:4], pieces[4:]), f32), *pieces[0], *pieces[1]
    )
    advance(self_lane, cross_lane)
    grad_w_cross_kv, output_across = order(
        lambda *operands: jnp.stack(
            (contract_rows(operands[0], operands[1]), contract_rows(operands[0], operands[2]))
        ),
        text_flat,
        grad_text_keys,
        grad_text_values,
        during=output_across,
    )
    grad_value_bias = token_sum(grad_text_values)
    advance(self_lane, cross_lane)
    pieces = [gathered(output_shards[chunk], output_across[chunk]) for chunk in chunks]
    output_rows = order.kernel(
        lambda *pieces: place_quarters(flags, (pieces[:4], pieces[4:]), bf16), *pieces[0], *pieces[1]
    )
    advance(self_lane, cross_lane)

    advance(cross_lane)
    grad_text = order.kernel(
        lambda *pieces: place_quarters(flags, (pieces,), f32),
        *gathered(grad_text_shard, grad_text_across),
    )
    grad_text = grad_text.reshape(text_states.shape)
    for _ in range(4 * axis_bits("seq") + 4):
        advance(self_lane, cross_lane)
    (grad_w_self,), cross_grads = ready[id(self_lane)], ready[id(cross_lane)]
    vectors = cross_grads[3][:STAT].reshape(-1, local_width)
    grad_b_cross = jnp.stack((vectors[9], grad_value_bias))
    return (
        output_rows,
        grad_tokens,
        grad_text,
        vectors[:3],
        vectors[3:6],
        grad_w_self,
        vectors[10:12],
        cross_grads[2],
        cross_grads[0],
        grad_w_cross_kv,
        grad_b_cross,
        cross_grads[1],
        sum_w_up,
        vectors[12 : 12 + w_up.shape[1] // local_width].reshape(-1),
        sum_w_down,
        vectors[6:9],
    )


def solution(mesh):
    placed = (
        P("seq", None),
        P(),
        P(),
        P(),
        P(),
        P(),
        P(None, None, "tensor"),
        P(None, "tensor"),
        P("tensor", None),
        P(None, "tensor"),
        P(None, None, "tensor"),
        P(None, "tensor"),
        P("tensor", None),
        P(None, "tensor"),
        P("tensor"),
        P("tensor", None),
        P(),
        P("seq", None),
    )
    return jax.shard_map(
        per_device,
        mesh=mesh,
        in_specs=placed,
        out_specs=(
            P("seq", None),
            P("seq", None),
            P(),
            P(None, "tensor"),
            P(None, "tensor"),
            P(None, None, "tensor"),
            P(None, "tensor"),
            P("tensor", None),
            P(None, "tensor"),
            P(None, None, "tensor"),
            P(None, "tensor"),
            P("tensor", None),
            P(None, "tensor"),
            P("tensor"),
            P("tensor", None),
            P(None, "tensor"),
        ),
        check_vma=False,
    )
```
